32 devices in a mesh: dp: 16 (over z, y, core), fsdp: 2 (over x).
Axes of the slice: x: 2, y: 2, z: 4, core: 2. Of those that a mesh axis runs over, the one named last changes fastest.
Arguments:
- tokens: bfloat16 [32768, 1152], P(('dp', 'fsdp')), may hold values from -6 to 6
- image_lengths: int32 [128], P(('dp', 'fsdp')), may hold values from 0 to 1024, as said below
- timesteps: int32 [128], P(('dp', 'fsdp')), may hold values from 0 to 999
- patch_cells: int32 [32768], P(('dp', 'fsdp')), may hold values from 0 to 1023, as said below
- norm1_gain: bfloat16 [1152], P(('dp', 'fsdp')), may hold values from 0.5 to 1.5
- norm1_bias: bfloat16 [1152], P(('dp', 'fsdp')), may hold values from -2.5 to 2.5
- qkv_weight: bfloat16 [1152, 3456], P(None, ('dp', 'fsdp')), may hold values from -0.1875 to 0.1875
- time_weight: bfloat16 [1152, 2304], P(None, ('dp', 'fsdp')), may hold values from -0.1875 to 0.1875
- out_weight: bfloat16 [1152, 1152], P(('dp', 'fsdp')), may hold values from -1 to 1
- out_bias: bfloat16 [1152], P(('dp', 'fsdp')), may hold values from -2.5 to 2.5
- norm2_gain: bfloat16 [1152], P(('dp', 'fsdp')), may hold values from 0.5 to 1.5
- norm2_bias: bfloat16 [1152], P(('dp', 'fsdp')), may hold values from -2.5 to 2.5
- fc1_weight: bfloat16 [1152, 4608], P(None, ('dp', 'fsdp')), may hold values from -0.1875 to 0.1875
- fc1_bias: bfloat16 [4608], P(('dp', 'fsdp')), may hold values from -2.5 to 2.5
- fc2_weight: bfloat16 [4608, 1152], P(('dp', 'fsdp')), may hold values from -0.09375 to 0.09375
- fc2_bias: bfloat16 [1152], P(('dp', 'fsdp')), may hold values from -2.5 to 2.5
- row_table: bfloat16 [16, 63], P('fsdp'), may hold values from -4 to 4
- col_table: bfloat16 [16, 63], P('fsdp'), may hold values from -4 to 4
- cotangent: bfloat16 [32768, 1152], P(('dp', 'fsdp')), may hold values from -6 to 6
Outputs:
- layer_out: bfloat16 [32768, 1152], P(('dp', 'fsdp'))
- input_grad: bfloat16 [32768, 1152], P(('dp', 'fsdp'))
- norm1_gain_grad: float32 [1152], P(('dp', 'fsdp'))
- norm1_bias_grad: float32 [1152], P(('dp', 'fsdp'))
- qkv_weight_grad: float32 [1152, 3456], P(None, ('dp', 'fsdp'))
- time_weight_grad: float32 [1152, 2304], P(None, ('dp', 'fsdp'))
- out_weight_grad: float32 [1152, 1152], P(('dp', 'fsdp'))
- out_bias_grad: float32 [1152], P(('dp', 'fsdp'))
- norm2_gain_grad: float32 [1152], P(('dp', 'fsdp'))
- norm2_bias_grad: float32 [1152], P(('dp', 'fsdp'))
- fc1_weight_grad: float32 [1152, 4608], P(None, ('dp', 'fsdp'))
- fc1_bias_grad: float32 [4608], P(('dp', 'fsdp'))
- fc2_weight_grad: float32 [4608, 1152], P(('dp', 'fsdp'))
- fc2_bias_grad: float32 [1152], P(('dp', 'fsdp'))
- row_table_grad: float32 [16, 63], P('fsdp')
- col_table_grad: float32 [16, 63], P('fsdp')
The draws below stay inside these ranges and needn't reach their ends.
Inputs may be any that keep to these rules, and one draw needn't show every extreme that they name: `image_lengths`: entries come in aligned groups of 4, one group for each frame of 1024 token rows. A frame holds either one large image: its first entry is the image's length, 512 to 1024, and the other entries are 0; or 4 small images in slots of 256 rows, each of length 128 to 256. An image's tokens are the first rows of its slot (of the frame for a large image); the other rows are padding. Every draw has a large image of length 1024 and a small image of length 256. `patch_cells`: A row's patch as patch_row * 32 + patch_column on its image's grid (32 x 32 for a large image, 16 x 16 for a small one); within an image's slot, padding rows included, no patch repeats.
All inputs are finite; a program needn't handle non-finite values.
Results may differ from the reference program's by a relative error of at most 0.013.
Values may be sent and summed in bfloat16 or wider, within the bound.
A program may use at most 384 MiB of HBM per device.

```python
import math
import jax
import jax.numpy as jnp
from jax import lax

D = 1152
HEADS = 16
FF = 4608
GRID = 32
SMALL = 16
HEAD_DIM = 72
TOKENS = 32768
IMAGE_SLOTS = 128


def frame_plan(key):
    frames = TOKENS // (GRID * GRID)
    key_kind, key_first, key_second = jax.random.split(key, 3)
    kinds = jax.random.randint(key_kind, (frames,), 0, 4)
    first_large = jax.random.randint(key_first, (), 0, frames)
    first_small = (first_large + 1 + jax.random.randint(key_second, (), 0, frames - 1)) % frames
    order = jnp.arange(frames)
    large_frame = ((kinds == 0) | (order == first_large)) & (order != first_small)
    return (large_frame, first_large, first_small)


def draw_image_lengths(key, part):
    large_frame, first_large, first_small = frame_plan(key)
    key = jax.random.fold_in(key, 11)
    frames = TOKENS // (GRID * GRID)
    frame_rows = GRID * GRID
    slot_rows = SMALL * SMALL
    per_frame = frame_rows // slot_rows
    key_large, key_small = jax.random.split(key)
    large_length = jax.random.randint(key_large, (frames,), frame_rows // 2, frame_rows + 1)
    small_length = jax.random.randint(key_small, (frames, per_frame), slot_rows // 2, slot_rows + 1)
    order = jnp.arange(frames)
    large_length = jnp.where(order == first_large, frame_rows, large_length)
    small_length = small_length.at[first_small, 0].set(slot_rows)
    column = jnp.arange(per_frame)
    large_rows = jnp.where(column[None, :] == 0, large_length[:, None], 0)
    table = jnp.where(large_frame[:, None], large_rows, small_length)
    return table.reshape(frames * per_frame).astype(jnp.int32)


def shuffled_cells(key, count):
    return jax.random.permutation(key, count)


def draw_patch_cells(key, part):
    large_frame, first_large, first_small = frame_plan(key)
    key = jax.random.fold_in(key, 23)
    frames = TOKENS // (GRID * GRID)
    frame_rows = GRID * GRID
    slot_rows = SMALL * SMALL
    per_frame = frame_rows // slot_rows
    large_keys = jax.random.split(jax.random.fold_in(key, 1), frames)
    small_keys = jax.random.split(jax.random.fold_in(key, 2), frames * per_frame)
    large_cells = jax.vmap(lambda single: shuffled_cells(single, frame_rows))(large_keys)
    small_order = jax.vmap(lambda single: shuffled_cells(single, slot_rows))(small_keys).reshape(frames, frame_rows)
    small_cells = small_order // SMALL * GRID + small_order % SMALL
    cells = jnp.where(large_frame[:, None], large_cells, small_cells)
    return cells.reshape(TOKENS).astype(jnp.int32)


def plant(values, own_key, smallest, largest):
    longest = values.shape.index(max(values.shape))
    spots = []
    for shift in (0, 1):
        where = [jax.random.randint(jax.random.fold_in(own_key, axis), (), 0, length) for axis, length in enumerate(values.shape)]
        where[longest] = (where[longest] + shift) % values.shape[longest]
        spots.append(tuple(where))
    return values.at[spots[0]].set(smallest).at[spots[1]].set(largest)


def levels(stream_key, extent, shards, low, largest):
    factor_of, own = 1.0, jax.random.fold_in(stream_key, 6)
    for position, blocks in shards:
        draws = jnp.exp(jax.random.uniform(jax.random.fold_in(own, position), (blocks,), jnp.float32, low / len(shards), largest / len(shards)))
        factor_of = factor_of * jnp.repeat(draws, extent[position] // blocks).reshape([-1 if axis == position else 1 for axis in range(len(extent))])
    return factor_of


def centred(key, dims, deviation, limit, cuts=(), kind=jnp.bfloat16):
    factor_of = levels(key, dims, cuts, -0.22, 0.18) if cuts else 1.0
    entries = jax.random.normal(key, dims, jnp.float32) * deviation * factor_of
    return jnp.minimum(jnp.maximum(entries, -limit), limit).astype(kind)


def setup_inputs(seed: int = 0) -> dict:
    streams_of = jax.random.split(jax.random.key(seed), 20)
    return {
        "tokens": centred(streams_of[0], (TOKENS, D), 1.0, 6.0, ((0, 32),)),
        "image_lengths": draw_image_lengths(jax.random.fold_in(streams_of[19], 71), 0),
        "timesteps": plant(jax.random.randint(streams_of[2], (IMAGE_SLOTS,), 0, 1000), jax.random.fold_in(streams_of[2], 1), 0, 999).astype(jnp.int32),
        "patch_cells": draw_patch_cells(jax.random.fold_in(streams_of[19], 71), 0),
        "norm1_gain": jnp.clip(1.0 + 0.1 * jax.random.normal(streams_of[4], (D,), jnp.float32), 0.5, 1.5).astype(jnp.bfloat16),
        "norm1_bias": centred(streams_of[5], (D,), 0.3, 2.5, ((0, 32),)),
        "qkv_weight": centred(streams_of[6], (D, 3 * D), D ** -0.5, 0.1875, ((1, 32),)),
        "time_weight": centred(streams_of[7], (D, 2 * D), D ** -0.5, 0.1875, ((1, 32),)),
        "out_weight": centred(streams_of[8], (D, D), (HEAD_DIM // 2) ** -0.5, 1.0, ((0, 32),)),
        "out_bias": centred(streams_of[9], (D,), 0.3, 2.5, ((0, 32),)),
        "norm2_gain": jnp.clip(1.0 + 0.1 * jax.random.normal(streams_of[10], (D,), jnp.float32), 0.5, 1.5).astype(jnp.bfloat16),
        "norm2_bias": centred(streams_of[11], (D,), 0.3, 2.5, ((0, 32),)),
        "fc1_weight": centred(streams_of[12], (D, FF), D ** -0.5, 0.1875, ((1, 32),)),
        "fc1_bias": centred(streams_of[13], (FF,), 0.3, 2.5, ((0, 32),)),
        "fc2_weight": centred(streams_of[14], (FF, D), FF ** -0.5, 0.09375, ((0, 32),)),
        "fc2_bias": centred(streams_of[15], (D,), 0.3, 2.5, ((0, 32),)),
        "row_table": centred(streams_of[16], (HEADS, 2 * GRID - 1), 0.7, 4.0, ((0, 2),)),
        "col_table": centred(streams_of[17], (HEADS, 2 * GRID - 1), 0.7, 4.0, ((0, 2),)),
        "cotangent": centred(streams_of[18], (TOKENS, D), 1.0, 6.0, ((0, 32),)),
    }


@jax.custom_vjp
def low(v):
    return lax.optimization_barrier(v.astype(jnp.bfloat16)).astype(jnp.float32)

@jax.custom_vjp
def low_back(v):
    return v

def low_keep(v):
    return (low(v), None)

def low_pass(kept, grad):
    return (grad,)

def back_keep(v):
    return (v, None)

def back_low(kept, grad):
    return (low(grad),)
low.defvjp(low_keep, low_pass)
low_back.defvjp(back_keep, back_low)

def norm_rows(values, row_gain, offset):
    centre = values - lax.optimization_barrier(jnp.mean(values, axis=-1, keepdims=True))
    spread = lax.optimization_barrier(jnp.mean(centre * centre, axis=-1, keepdims=True))
    return centre * lax.rsqrt(spread + 1e-06) * row_gain + offset

def time_embed(stamps, feat_width):
    half_width = feat_width // 2
    frequency = jnp.exp(-math.log(10000.0) * jnp.arange(half_width, dtype=jnp.float32) / half_width)
    angles = stamps.astype(jnp.float32)[:, None] * frequency[None, :]
    return jnp.concatenate([jnp.cos(angles), jnp.sin(angles)], axis=1)

def frame_layout(lengths_frame):
    frame_rows = GRID * GRID
    slot_rows = SMALL * SMALL
    local_rows = jnp.arange(frame_rows, dtype=jnp.int32)
    large_image = lengths_frame[0] > slot_rows
    slot_index = jnp.where(large_image, 0, local_rows // slot_rows).astype(jnp.int32)
    slot_start = jnp.where(large_image, 0, slot_index * slot_rows)
    valid_rows = local_rows - slot_start < lengths_frame[slot_index]
    return (slot_index, valid_rows)

def attend(query, keys, values, cells, slot_index, valid_rows, row_table, col_table):
    frame_rows, feat_width = query.shape
    head_dim = feat_width // HEADS
    query_heads = query.reshape(frame_rows, HEADS, head_dim)
    key_heads = keys.reshape(frame_rows, HEADS, head_dim)
    value_heads = values.reshape(frame_rows, HEADS, head_dim)
    scores = jnp.einsum('qhd,khd->hqk', query_heads, key_heads, precision=lax.Precision.HIGHEST) * (1.0 / math.sqrt(head_dim))
    patch_row = cells // GRID
    patch_col = cells % GRID
    scores = scores + row_table[:, patch_row[:, None] - patch_row[None, :] + GRID - 1]
    scores = scores + col_table[:, patch_col[:, None] - patch_col[None, :] + GRID - 1]
    scores = low_back(scores)
    allowed = (slot_index[:, None] == slot_index[None, :]) & valid_rows[None, :]
    scores = jnp.where(allowed[None], scores, -1e+30)
    top_score = lax.optimization_barrier(jnp.max(scores, axis=-1, keepdims=True))
    exponent = jnp.exp(scores - top_score)
    softmax_block = exponent / lax.optimization_barrier(jnp.sum(exponent, axis=-1, keepdims=True))
    mixed = jnp.einsum('hqk,khd->qhd', low(softmax_block), value_heads, precision=lax.Precision.HIGHEST)
    return low(low_back(mixed.reshape(frame_rows, feat_width)))

def layer(weights, token_rows, cells, slot_index, valid_rows, embedded):
    gain_one, shift_one, w_qkv, w_time, w_out, b_out, gain_two, shift_two, w_up, b_up, w_down, b_down, row_table, col_table = weights
    highest = lax.Precision.HIGHEST
    feat_width = token_rows.shape[1]
    normed_one = low(norm_rows(token_rows, gain_one, shift_one))
    time_proj = jnp.dot(low(embedded), w_time, precision=highest)
    time_rows = time_proj[slot_index]
    projected = jnp.dot(normed_one, w_qkv, precision=highest)
    query = low(low_back(projected[:, :feat_width] + time_rows[:, :feat_width]))
    keys = low(low_back(projected[:, feat_width:2 * feat_width]))
    values = low(low_back(projected[:, 2 * feat_width:] + time_rows[:, feat_width:]))
    attended = jax.checkpoint(attend)(query, keys, values, cells, slot_index, valid_rows, row_table, col_table)
    branch_one = low_back(jnp.dot(attended, w_out, precision=highest) + b_out)
    hidden_one = token_rows + branch_one
    normed_two = low(norm_rows(hidden_one, gain_two, shift_two))
    pre_act = low_back(jnp.dot(normed_two, w_up, precision=highest) + b_up)
    activated = low(jax.nn.gelu(pre_act, approximate=False))
    branch_two = low_back(jnp.dot(activated, w_down, precision=highest) + b_down)
    return hidden_one + branch_two

def reference(tokens, image_lengths, timesteps, patch_cells, norm1_gain, norm1_bias, qkv_weight, time_weight, out_weight, out_bias, norm2_gain, norm2_bias, fc1_weight, fc1_bias, fc2_weight, fc2_bias, row_table, col_table, cotangent):
    frame_rows = GRID * GRID
    per_frame = frame_rows // (SMALL * SMALL)
    frames = tokens.shape[0] // frame_rows
    params = tuple((member.astype(jnp.float32) for member in (norm1_gain, norm1_bias, qkv_weight, time_weight, out_weight, out_bias, norm2_gain, norm2_bias, fc1_weight, fc1_bias, fc2_weight, fc2_bias, row_table, col_table)))

    def frame_step(totals, inputs):
        token_frame, lengths_frame, stamps_frame, cells_frame, cot_frame = inputs
        slot_index, valid_rows = frame_layout(lengths_frame)
        embedded = time_embed(stamps_frame, D)

        def forward(weights, input_rows):
            return layer(weights, input_rows, cells_frame, slot_index, valid_rows, embedded)
        result, pullback = jax.vjp(forward, params, token_frame.astype(jnp.float32))
        weight_grads, input_grads = pullback(cot_frame.astype(jnp.float32) * valid_rows[:, None].astype(jnp.float32))
        totals = tuple((running + addend for running, addend in zip(totals, weight_grads)))
        return (totals, (result.astype(jnp.bfloat16), input_grads.astype(jnp.bfloat16)))
    initial = tuple((jnp.zeros_like(member) for member in params))
    inputs = (tokens.reshape(frames, frame_rows, -1), image_lengths.reshape(frames, per_frame), timesteps.reshape(frames, per_frame), patch_cells.reshape(frames, frame_rows), cotangent.reshape(frames, frame_rows, -1))
    totals, (layer_out, input_grad) = lax.scan(frame_step, initial, inputs)
    return (layer_out.reshape(tokens.shape), input_grad.reshape(tokens.shape), totals[0], totals[1], totals[2], totals[3], totals[4], totals[5], totals[6], totals[7], totals[8], totals[9], totals[10], totals[11], totals[12], totals[13])
```

```python
import functools
import math

import jax
import jax.numpy as jnp
from jax import lax
from jax.experimental import pallas as pl
from jax.experimental.pallas import tpu as pltpu
from jax.sharding import PartitionSpec as P

HEADS = 16
GRID = 32
SMALL = 16
AXES = ("dp", "fsdp")
LANES = 128
PIECE = 48
BIG = -1e30
F32 = jnp.float32
BF16 = jnp.bfloat16
HIGHEST = lax.Precision.HIGHEST
MESH_ID = pl.DeviceIdType.MESH
VMEM_LIMIT = 60 * 1024 * 1024


def dot_nn(a, b):
    return lax.dot_general(a, b, (((1,), (0,)), ((), ())), preferred_element_type=F32)


def dot_nt(a, b):
    return lax.dot_general(a, b, (((1,), (1,)), ((), ())), preferred_element_type=F32)


def dot_tn(a, b):
    return lax.dot_general(a, b, (((0,), (0,)), ((), ())), preferred_element_type=F32)


def params(**more):
    return pltpu.CompilerParams(vmem_limit_bytes=VMEM_LIMIT, **more)


def resident(shape):
    zeros = (0,) * len(shape)
    return pl.BlockSpec(shape, lambda *_: zeros, pipeline_mode=pl.Buffered(1))


def split_dp(dp):
    g2 = 1 if dp <= 16 else 4
    return dp // 4 // g2, g2


class Place:
    def __init__(self, dims):
        self.G1, self.G2 = dims
        dp, self.q = lax.axis_index("dp"), lax.axis_index("fsdp")
        self.c = dp % 2
        rest = dp // 2
        self.g2 = rest % self.G2
        rest = rest // self.G2
        self.p = rest % 2
        self.g1 = rest // 2
        c, p, q = self.c, self.p, self.q
        self.ap, self.aq = (1 - p) * (1 - c) + p * c, q * (1 - c) + (1 - q) * c
        self.bp, self.bq = p * (1 - c) + (1 - p) * c, (1 - q) * (1 - c) + q * c
        self.whole = (pl.ds(0, self.G1), pl.ds(0, self.G2))

    def device(self, g1, p, g2, c, q):
        return (((g1 * 2 + p) * self.G2 + g2) * 2 + c, q)

    def line(self):
        found = []
        for step in range(1, self.G1 * self.G2):
            found.append(((self.g1 + step // self.G2) % self.G1, (self.g2 + step % self.G2) % self.G2))
        return found

    def on_line(self, spot):
        return self.device(spot[0], self.p, spot[1], self.c, self.q)

    def first(self):
        return self.device(self.g1, self.ap, self.g2, self.c, self.aq)

    def second(self):
        return self.device(self.g1, self.bp, self.g2, self.c, self.bq)

    def sibling(self):
        return self.device(self.g1, self.p, self.g2, 1 - self.c, self.q)

    def barrier(self):
        partners = [self.on_line(spot) for spot in self.line()] + [self.first(), self.second(), self.sibling()]
        semaphore = pltpu.get_barrier_semaphore()
        for partner in partners:
            pl.semaphore_signal(semaphore, inc=1, device_id=partner, device_id_type=MESH_ID)
        pl.semaphore_wait(semaphore, len(partners))


def wait_for(view, semaphore):
    pltpu.make_async_copy(view, view, semaphore).wait()


class Gather:
    STAGES = 5

    def __init__(self, dims, pieces, sources, results, sems, own_sems):
        self.at = Place(dims)
        self.pieces, self.sources, self.results = pieces, sources, results
        self.sems, self.own_sems = sems, own_sems

    @staticmethod
    def scratch(dims, pieces):
        return [
            pltpu.SemaphoreType.DMA((len(pieces), 7 + dims[0] * dims[1], 2)),
            pltpu.SemaphoreType.DMA((len(pieces),)),
        ]

    def send(self, k, kind, source, target, to):
        pltpu.make_async_remote_copy(
            src_ref=source,
            dst_ref=target,
            send_sem=self.sems.at[k, kind, 0],
            recv_sem=self.sems.at[k, kind, 1],
            device_id=to,
            device_id_type=MESH_ID,
        ).start()

    def finish(self, k, kind, view):
        wait_for(view, self.sems.at[k, kind, 1])
        wait_for(view, self.sems.at[k, kind, 0])

    def stage(self, k, number):
        at = self.at
        array, start = self.pieces[k]
        rows = pl.ds(start, PIECE)
        result = self.results[array]
        every, every2 = at.whole
        source = self.sources[array].at[rows]
        own = result.at[at.g1, at.p, at.g2, at.c, at.q, rows]

        def plane(p, q):
            return result.at[every, p, every2, at.c, q, rows]

        if number == 0:
            pltpu.make_async_copy(source, own, self.own_sems.at[k]).start()
            for i, spot in enumerate(at.line()):
                self.send(k, 8 + i, source, own, at.on_line(spot))
        if number == 1:
            pltpu.make_async_copy(source, own, self.own_sems.at[k]).wait()
            for i in range(len(at.line())):
                self.finish(k, 8 + i, own)
            mine = plane(at.p, at.q)
            self.send(k, 1, mine, mine, at.first())
            self.send(k, 3, mine, mine, at.sibling())
        if number == 2:
            mine, came = plane(at.p, at.q), plane(at.ap, at.aq)
            self.finish(k, 1, came)
            self.send(k, 2, mine, mine, at.second())
            self.send(k, 4, came, came, at.second())
            self.send(k, 5, came, came, at.sibling())
        if number == 3:
            for kind, came in ((2, plane(at.bp, at.bq)), (4, plane(1 - at.p, 1 - at.q))):
                self.finish(k, kind, came)
                self.send(k, 6 + kind // 4, came, came, at.sibling())
        if number == 4:
            for kind in (3, 5, 6, 7):
                self.finish(k, kind, plane(at.p, at.q))

    def round(self, number):
        for k in range(len(self.pieces)):
            if 0 <= number - k < self.STAGES:
                self.stage(k, number - k)

    def rounds(self):
        return len(self.pieces) + self.STAGES - 1


class Scatter:
    STAGES = 5

    def __init__(self, dims, pieces, sources, results, held, from_core, from_second, from_first, from_line, sems):
        self.at = Place(dims)
        self.pieces, self.sources, self.results = pieces, sources, results
        self.held, self.from_core, self.from_second = held, from_core, from_second
        self.from_first, self.from_line, self.sems = from_first, from_line, sems

    @staticmethod
    def scratch(dims, pieces, width):
        G1, G2 = dims
        n = len(pieces)
        return [
            pltpu.VMEM((n, G1, 2, G2, 2, PIECE, width), BF16),
            pltpu.VMEM((n, G1, 2, G2, 2, PIECE, width), BF16),
            pltpu.VMEM((n, 2, G1, G2, PIECE, width), BF16),
            pltpu.VMEM((n, G1, G2, PIECE, width), BF16),
            pltpu.VMEM((n, G1 * G2 - 1, PIECE, width), BF16),
            pltpu.SemaphoreType.DMA((n, 5 + G1 * G2, 2)),
        ]

    def send(self, k, kind, source, target, to):
        pltpu.make_async_remote_copy(
            src_ref=source,
            dst_ref=target,
            send_sem=self.sems.at[k, kind, 0],
            recv_sem=self.sems.at[k, kind, 1],
            device_id=to,
            device_id_type=MESH_ID,
        ).start()

    def add(self, target, addend):
        at = self.at

        def body(i, carry):
            g1, g2 = i // at.G2, i % at.G2
            total = target[g1, g2].astype(F32) + addend[g1, g2].astype(F32)
            target[g1, g2] = total.astype(BF16)
            return carry

        lax.fori_loop(0, at.G1 * at.G2, body, 0)

    def stage(self, k, number):
        at = self.at
        array, start = self.pieces[k]
        rows = pl.ds(start, PIECE)
        source = self.sources[array]
        every, every2 = at.whole
        both = pl.ds(0, 2)
        held = self.held.at[k]

        def plane(p, q):
            return held.at[every, p, every2, q]

        local_copy = lambda: pltpu.make_async_copy(
            source.at[every, both, every2, at.c, both, rows], held, self.sems.at[k, 4, 0]
        )
        if number == 0:
            self.send(k, 0, source.at[every, both, every2, 1 - at.c, both, rows], self.from_core.at[k], at.sibling())
            local_copy().start()
        if number == 1:
            local_copy().wait()
            wait_for(self.from_core.at[k], self.sems.at[k, 0, 1])
            core = self.from_core.at[k]
            for p, q in ((at.bp, at.bq), (1 - at.p, 1 - at.q)):
                self.add(plane(p, q), core.at[every, p, every2, q])
            self.send(k, 1, plane(at.bp, at.bq), self.from_second.at[k, 0], at.second())
            self.send(k, 2, plane(1 - at.p, 1 - at.q), self.from_second.at[k, 1], at.second())
            for p, q in ((at.p, at.q), (at.ap, at.aq)):
                self.add(plane(p, q), core.at[every, p, every2, q])
        if number == 2:
            for kind in (1, 2):
                wait_for(self.from_second.at[k, kind - 1], self.sems.at[k, kind, 1])
            self.add(plane(at.ap, at.aq), self.from_second.at[k, 1])
            self.send(k, 3, plane(at.ap, at.aq), self.from_first.at[k], at.first())
            self.add(plane(at.p, at.q), self.from_second.at[k, 0])
        if number == 3:
            wait_for(self.from_first.at[k], self.sems.at[k, 3, 1])
            self.add(plane(at.p, at.q), self.from_first.at[k])
            for i, spot in enumerate(at.line()):
                self.send(
                    k, 5 + i, held.at[spot[0], at.p, spot[1], at.q], self.from_line.at[k, i], at.on_line(spot)
                )
        if number == 4:
            total = held[at.g1, at.p, at.g2, at.q].astype(F32)
            for i in range(at.G1 * at.G2 - 1):
                wait_for(self.from_line.at[k, i], self.sems.at[k, 5 + i, 1])
                total = total + self.from_line[k, i].astype(F32)
            self.results[array][rows] = total
            wait_for(self.from_core.at[k], self.sems.at[k, 0, 0])
            for kind in (1, 2):
                wait_for(self.from_second.at[k, kind - 1], self.sems.at[k, kind, 0])
            wait_for(self.from_first.at[k], self.sems.at[k, 3, 0])
            for i in range(at.G1 * at.G2 - 1):
                wait_for(self.from_line.at[k, i], self.sems.at[k, 5 + i, 0])

    def round(self, number):
        for k in range(len(self.pieces)):
            if 0 <= number - k < self.STAGES:
                self.stage(k, number - k)

    def rounds(self):
        return len(self.pieces) + self.STAGES - 1


def pieces_of(shards):
    per = [(array, start) for array, shard in enumerate(shards) for start in range(0, shard, PIECE)]
    return sorted(per, key=lambda piece: piece[1])


def pad_rows(shard):
    rows = shard.shape[0]
    return jnp.pad(shard, ((0, -rows % PIECE), (0, 0)))


def gather(shards, dims, collective):
    pieces = pieces_of([shard.shape[0] for shard in shards])
    count = len(shards)

    def kernel(*refs):
        work = Gather(dims, pieces, refs[:count], refs[count : 2 * count], *refs[2 * count :])
        work.at.barrier()
        for number in range(work.rounds()):
            work.round(number)

    G1, G2 = dims
    anywhere = pl.BlockSpec(memory_space=pl.ANY)
    return pl.pallas_call(
        kernel,
        out_shape=[jax.ShapeDtypeStruct((G1, 2, G2, 2, 2) + s.shape, s.dtype) for s in shards],
        in_specs=[anywhere] * count,
        out_specs=[anywhere] * count,
        scratch_shapes=Gather.scratch(dims, pieces),
        compiler_params=params(collective_id=collective, has_side_effects=True),
    )(*shards)


def scatter(parts, dims, collective):
    pieces = pieces_of([part.shape[5] for part in parts])
    count = len(parts)
    width = parts[0].shape[6]

    def kernel(*refs):
        work = Scatter(dims, pieces, refs[:count], refs[count : 2 * count], *refs[2 * count :])
        work.at.barrier()
        for number in range(work.rounds()):
            work.round(number)

    return pl.pallas_call(
        kernel,
        out_shape=[jax.ShapeDtypeStruct(part.shape[5:], F32) for part in parts],
        in_specs=[pl.BlockSpec(memory_space=pl.ANY)] * count,
        out_specs=[pl.BlockSpec(memory_space=pltpu.VMEM)] * count,
        scratch_shapes=Scatter.scratch(dims, pieces, width),
        compiler_params=params(collective_id=collective, has_side_effects=True),
    )(*parts)


def normalise(values):
    centre = values - jnp.mean(values, axis=-1, keepdims=True)
    inverse = lax.rsqrt(jnp.mean(centre * centre, axis=-1, keepdims=True) + 1e-06)
    return centre * inverse, inverse


def norm_back(values, gain, grad):
    unit, inverse = normalise(values)
    scaled = grad * gain
    inner = jnp.mean(scaled, axis=-1, keepdims=True) + unit * jnp.mean(scaled * unit, axis=-1, keepdims=True)
    return inverse * (scaled - inner), unit


def attend_kernel(factor, block, tokens, gain, shift, weight, time_rows, table, onehot, mask_q, mask_k,
                  normed_out, q_out, k_out, v_out, o_out, p_out, keys):
    rows = tokens.shape[0]

    @pl.when(pl.program_id(0) == 0)
    def _():
        for start in range(0, rows, block):
            span = pl.ds(start, block)
            unit, _ = normalise(tokens[span].astype(F32))
            normed_out[span] = (unit * gain[...] + shift[...]).astype(BF16)

    per = time_rows.shape[1] // 2
    slot = rows // per
    for i in range(per):
        span = pl.ds(i * slot, slot)
        qkv = dot_nt(normed_out[span], weight[0])
        q_out[0, span] = (qkv[:, :LANES] + time_rows[0, i : i + 1]).astype(BF16)
        k_out[0, span] = qkv[:, LANES : 2 * LANES].astype(BF16)
        v_out[0, span] = (qkv[:, 2 * LANES :] + time_rows[0, per + i : per + i + 1]).astype(BF16)
    keys[:, :LANES] = k_out[0] + mask_k[...]
    keys[:, LANES:] = onehot[...]
    for start in range(0, rows, block):
        span = pl.ds(start, block)
        bias = dot_nn(onehot[span], table[0]).astype(BF16)
        query = jnp.concatenate([q_out[0, span] + mask_q[span], bias], axis=1)
        scores = dot_nt(query, keys[...])
        top = jnp.max(scores, axis=1, keepdims=True)
        weights = jnp.exp2((scores - top) * factor)
        total = jnp.sum(weights, axis=1, keepdims=True)
        low = (weights * (1.0 / total)).astype(BF16)
        p_out[0, span] = low
        o_out[span] = dot_nn(low, v_out[0]).astype(BF16)


def attend(tokens, gain, shift, weight, time_rows, table, onehot, mask_q, mask_k, factor):
    rows, width = tokens.shape
    block = min(256, rows)
    per_head = lambda *shape: pl.BlockSpec((1,) + shape, lambda h: (h, 0, 0))
    head_rows = jax.ShapeDtypeStruct((HEADS, rows, LANES), BF16)
    return pl.pallas_call(
        functools.partial(attend_kernel, factor, block),
        grid=(HEADS,),
        in_specs=[
            resident(tokens.shape),
            resident(gain.shape),
            resident(shift.shape),
            per_head(3 * LANES, width),
            per_head(*time_rows.shape[1:]),
            per_head(LANES, LANES),
            resident(onehot.shape),
            resident(mask_q.shape),
            resident(mask_k.shape),
        ],
        out_specs=[
            resident(tokens.shape),
            per_head(rows, LANES),
            per_head(rows, LANES),
            per_head(rows, LANES),
            pl.BlockSpec((rows, LANES), lambda h: (0, h)),
            per_head(rows, rows),
        ],
        out_shape=[
            jax.ShapeDtypeStruct(tokens.shape, BF16),
            head_rows,
            head_rows,
            head_rows,
            jax.ShapeDtypeStruct((rows, HEADS * LANES), BF16),
            jax.ShapeDtypeStruct((HEADS, rows, rows), BF16),
        ],
        scratch_shapes=[pltpu.VMEM((rows, 2 * LANES), BF16)],
        compiler_params=params(),
        name="attend",
    )(tokens, gain, shift, weight, time_rows, table, onehot, mask_q, mask_k)


def attend_back_kernel(block, scale, normed, p, q, k, v, do, o, onehot,
                       dqkv_out, dw_out, sums_out, pair_out, keys, grads, dk_sum, dv_sum):
    rows = normed.shape[0]
    lane = lax.broadcasted_iota(jnp.int32, (rows, LANES), 1)
    head = 72
    delta = jnp.sum(do[...].astype(F32) * o[...].astype(F32), axis=1, keepdims=True)
    high = delta.astype(BF16).astype(F32)
    more = jnp.where(lane == head, -high, jnp.where(lane == head + 1, high - delta, 0.0))
    grads[...] = (do[...].astype(F32) + more).astype(BF16)
    values = v[0] + jnp.where((lane == head) | (lane == head + 1), 1.0, 0.0).astype(BF16)
    keys[:, :LANES] = k[0]
    keys[:, LANES:] = onehot[...]
    pair = jnp.zeros((LANES, LANES), F32)
    for start in range(0, rows, block):
        span = pl.ds(start, block)
        centred = dot_nt(grads[span], values)
        ds = (p[0, span].astype(F32) * centred).astype(BF16)
        both = dot_nn(ds, keys[...])
        dqkv_out[span, :LANES] = (both[:, :LANES] * scale).astype(BF16)
        pair = pair + lax.dot_general(
            onehot[span].astype(F32), both[:, LANES:], (((0,), (0,)), ((), ())),
            preferred_element_type=F32, precision=HIGHEST,
        )
        dk = dot_tn(ds, q[0, span])
        dv = dot_tn(p[0, span], do[span])
        if start == 0:
            dk_sum[...] = dk
            dv_sum[...] = dv
        else:
            dk_sum[...] += dk
            dv_sum[...] += dv
    dqkv_out[:, LANES : 2 * LANES] = (dk_sum[...] * scale).astype(BF16)
    dqkv_out[:, 2 * LANES :] = dv_sum[...].astype(BF16)
    pair_out[0] = pair
    per = sums_out.shape[1]
    slot = rows // per
    for i in range(per):
        sums_out[0, i : i + 1] = jnp.sum(
            dqkv_out[pl.ds(i * slot, slot)].astype(F32), axis=0, keepdims=True
        )
    dw_out[0] = dot_tn(dqkv_out[...], normed[...]).astype(BF16)


def attend_back(normed, p, q, k, v, do, o, onehot, scale, per):
    rows, width = normed.shape
    block = min(256, rows)
    per_head = lambda *shape: pl.BlockSpec((1,) + shape, lambda h: (h, 0, 0))
    head_cols = pl.BlockSpec((rows, LANES), lambda h: (0, h))
    return pl.pallas_call(
        functools.partial(attend_back_kernel, block, scale),
        grid=(HEADS,),
        in_specs=[
            resident(normed.shape),
            per_head(rows, rows),
            per_head(rows, LANES),
            per_head(rows, LANES),
            per_head(rows, LANES),
            head_cols,
            head_cols,
            resident(onehot.shape),
        ],
        out_specs=[
            pl.BlockSpec((rows, 3 * LANES), lambda h: (0, h)),
            per_head(3 * LANES, width),
            per_head(per, 3 * LANES),
            per_head(LANES, LANES),
        ],
        out_shape=[
            jax.ShapeDtypeStruct((rows, HEADS * 3 * LANES), BF16),
            jax.ShapeDtypeStruct((HEADS, 3 * LANES, width), BF16),
            jax.ShapeDtypeStruct((HEADS, per, 3 * LANES), F32),
            jax.ShapeDtypeStruct((HEADS, LANES, LANES), F32),
        ],
        scratch_shapes=[
            pltpu.VMEM((rows, 2 * LANES), BF16),
            pltpu.VMEM((rows, LANES), BF16),
            pltpu.VMEM((rows, LANES), F32),
            pltpu.VMEM((rows, LANES), F32),
        ],
        compiler_params=params(),
        name="attend_back",
    )(normed, p, q, k, v, do, o, onehot)


def project_kernel(tokens, o, weight, bias, gain, shift, hidden_out, normed_out):
    hidden = tokens[...].astype(F32) + (dot_nn(o[...], weight[...]) + bias[...])
    hidden_out[...] = hidden
    unit, _ = normalise(hidden)
    normed_out[...] = (unit * gain[...] + shift[...]).astype(BF16)


def project(tokens, o, weight, bias, gain, shift):
    rows, width = tokens.shape
    block = min(256, rows)
    by_rows = lambda cols: pl.BlockSpec((block, cols), lambda i: (i, 0))
    return pl.pallas_call(
        project_kernel,
        grid=(rows // block,),
        in_specs=[by_rows(width), by_rows(o.shape[1]), resident(weight.shape)] + [resident((1, width))] * 3,
        out_specs=[by_rows(width), by_rows(width)],
        out_shape=[jax.ShapeDtypeStruct(tokens.shape, F32), jax.ShapeDtypeStruct(tokens.shape, BF16)],
        compiler_params=params(),
        name="project",
    )(tokens, o, weight, bias, gain, shift)


def normal_parts(u):
    size = jnp.abs(u)
    bell = jnp.exp(-0.5 * u * u)
    t = 1.0 / (1.0 + (0.3275911 * math.sqrt(0.5)) * size)
    poly = t * (
        0.5 * 0.254829592
        + t * (0.5 * -0.284496736 + t * (0.5 * 1.421413741 + t * (0.5 * -1.453152027 + t * (0.5 * 1.061405429))))
    )
    tail = poly * bell
    return jnp.where(u >= 0.0, 1.0 - tail, tail), bell * (1.0 / math.sqrt(2.0 * math.pi))


def mlp_kernel(normed, dy, up, down, bias, y_out, dn_out, dup_out, ddown_out, dbias_out):
    rows = normed.shape[0]
    first = pl.program_id(0) == 0
    u = dot_nt(normed[...], up[...]) + bias[...]
    phi, density = normal_parts(u)
    act = (u * phi).astype(BF16)
    slope = phi + u * density
    du = (slope * dot_nt(dy[...], down[...])).astype(BF16)
    dbias_out[...] = jnp.sum(du.astype(F32), axis=0, keepdims=True)
    y = dot_nn(act, down[...])
    dn = dot_nn(du, up[...])

    @pl.when(first)
    def _():
        y_out[...] = y
        dn_out[...] = dn

    @pl.when(jnp.logical_not(first))
    def _():
        y_out[...] += y
        dn_out[...] += dn

    ddown_out[...] = dot_tn(act, dy[...]).astype(BF16)
    dup_out[...] = dot_tn(du, normed[...]).astype(BF16)


def mlp(normed, dy, up, down, bias):
    rows, width = normed.shape
    units = up.shape[0]
    block = 512
    by_units = pl.BlockSpec((block, width), lambda i: (i, 0))
    by_bias = pl.BlockSpec((1, block), lambda i: (0, i))
    return pl.pallas_call(
        mlp_kernel,
        grid=(units // block,),
        in_specs=[resident(normed.shape), resident(dy.shape), by_units, by_units, by_bias],
        out_specs=[resident(normed.shape), resident(normed.shape), by_units, by_units, by_bias],
        out_shape=[
            jax.ShapeDtypeStruct(normed.shape, F32),
            jax.ShapeDtypeStruct(normed.shape, F32),
            jax.ShapeDtypeStruct(up.shape, BF16),
            jax.ShapeDtypeStruct(down.shape, BF16),
            jax.ShapeDtypeStruct((1, units), F32),
        ],
        compiler_params=params(),
        name="mlp",
    )(normed, dy, up, down, bias)


def turn_kernel(hidden, y, bias, dn, dy, gain, weight, o, out, dh_out, do_out, dw_out, vec_out, dw_sum):
    first = pl.program_id(0) == 0
    last = pl.program_id(0) == pl.num_programs(0) - 1
    out[...] = (hidden[...] + (y[...] + bias[...])).astype(BF16)
    back, unit = norm_back(hidden[...], gain[...], dn[...])
    dyf = dy[...].astype(F32)
    dh = dyf + back
    dh_out[...] = dh
    da = dh.astype(BF16)
    do_out[...] = dot_nt(da, weight[...]).astype(BF16)
    dw = dot_tn(o[...], da)
    sums = jnp.concatenate(
        [
            jnp.sum(dn[...] * unit, axis=0, keepdims=True),
            jnp.sum(dn[...], axis=0, keepdims=True),
            jnp.sum(da.astype(F32), axis=0, keepdims=True),
            jnp.sum(dyf, axis=0, keepdims=True),
        ],
        axis=0,
    )

    @pl.when(first)
    def _():
        dw_sum[...] = dw
        vec_out[...] = sums

    @pl.when(jnp.logical_not(first))
    def _():
        dw_sum[...] += dw
        vec_out[...] += sums

    @pl.when(last)
    def _():
        dw_out[...] = dw_sum[...].astype(BF16)


def turn(hidden, y, bias, dn, dy, gain, weight, o):
    rows, width = hidden.shape
    block = min(256, rows)
    by_rows = lambda cols: pl.BlockSpec((block, cols), lambda i: (i, 0))
    wide = weight.shape[0]
    return pl.pallas_call(
        turn_kernel,
        grid=(rows // block,),
        in_specs=[
            by_rows(width),
            by_rows(width),
            resident((1, width)),
            by_rows(width),
            by_rows(width),
            resident((1, width)),
            resident(weight.shape),
            by_rows(wide),
        ],
        out_specs=[by_rows(width), by_rows(width), by_rows(wide), resident(weight.shape), resident((4, width))],
        out_shape=[
            jax.ShapeDtypeStruct(hidden.shape, BF16),
            jax.ShapeDtypeStruct(hidden.shape, F32),
            jax.ShapeDtypeStruct((rows, wide), BF16),
            jax.ShapeDtypeStruct(weight.shape, BF16),
            jax.ShapeDtypeStruct((4, width), F32),
        ],
        scratch_shapes=[pltpu.VMEM(weight.shape, F32)],
        compiler_params=params(),
        name="turn",
    )(hidden, y, bias, dn, dy, gain, weight, o)


def end_kernel(tokens, dqkv, weight, gain, dh, out, vec_out):
    first = pl.program_id(0) == 0
    dn = dot_nn(dqkv[...], weight[...])
    back, unit = norm_back(tokens[...].astype(F32), gain[...], dn)
    out[...] = (dh[...] + back).astype(BF16)
    sums = jnp.concatenate(
        [jnp.sum(dn * unit, axis=0, keepdims=True), jnp.sum(dn, axis=0, keepdims=True)], axis=0
    )

    @pl.when(first)
    def _():
        vec_out[...] = sums

    @pl.when(jnp.logical_not(first))
    def _():
        vec_out[...] += sums


def end(tokens, dqkv, weight, gain, dh):
    rows, width = tokens.shape
    block = min(256, rows)
    by_rows = lambda cols: pl.BlockSpec((block, cols), lambda i: (i, 0))
    return pl.pallas_call(
        end_kernel,
        grid=(rows // block,),
        in_specs=[
            by_rows(width), by_rows(dqkv.shape[1]), resident(weight.shape), resident((1, width)), by_rows(width)
        ],
        out_specs=[by_rows(width), resident((2, width))],
        out_shape=[jax.ShapeDtypeStruct(tokens.shape, BF16), jax.ShapeDtypeStruct((2, width), F32)],
        compiler_params=params(),
        name="end",
    )(tokens, dqkv, weight, gain, dh)


def time_embed(stamps, feat_width):
    half_width = feat_width // 2
    frequency = jnp.exp(-math.log(10000.0) * jnp.arange(half_width, dtype=F32) / half_width)
    angles = stamps.astype(F32)[:, None] * frequency[None, :]
    return jnp.concatenate([jnp.cos(angles), jnp.sin(angles)], axis=1)


def local(
    tokens,
    image_lengths,
    timesteps,
    patch_cells,
    norm1_gain,
    norm1_bias,
    qkv_weight,
    time_weight,
    out_weight,
    out_bias,
    norm2_gain,
    norm2_bias,
    fc1_weight,
    fc1_bias,
    fc2_weight,
    fc2_bias,
    row_table,
    col_table,
    cotangent,
):
    rows, width = tokens.shape
    head_dim = width // HEADS
    slot_rows = SMALL * SMALL
    per = image_lengths.shape[0]
    assert rows == GRID * GRID and per * slot_rows == rows
    fsdp = lax.axis_size("fsdp")
    devices = lax.axis_size("dp") * fsdp
    dims = split_dp(lax.axis_size("dp"))
    spread = (dims[0], 2, dims[1], 2, 2)

    qkv_share, out_share = qkv_weight.shape[1], out_weight.shape[0]
    unit_share = fc1_weight.shape[1]
    mixed_shard = pad_rows(jnp.concatenate([qkv_weight.T, out_weight], axis=0))
    (mixed,) = gather([mixed_shard], dims, 1)
    up, down = gather([pad_rows(fc1_weight.T), pad_rows(fc2_weight)], dims, 2)
    mixed = mixed.reshape((devices,) + mixed_shard.shape)
    units = devices * unit_share
    up = up.reshape(devices, -1, width)[:, :unit_share].reshape(units, width)
    down = down.reshape(devices, -1, width)[:, :unit_share].reshape(units, width)
    qkv_rows = mixed[:, :qkv_share].reshape(3, HEADS, head_dim, width)
    qkv_rows = jnp.pad(qkv_rows, ((0, 0), (0, 0), (0, LANES - head_dim), (0, 0)))
    qkv_full = qkv_rows.transpose(1, 0, 2, 3).reshape(HEADS, 3 * LANES, width)
    out_full = mixed[:, qkv_share : qkv_share + out_share].reshape(HEADS, head_dim, width)
    out_full = jnp.pad(out_full, ((0, 0), (0, LANES - head_dim), (0, 0))).reshape(HEADS * LANES, width)

    embedded = time_embed(timesteps, width).astype(BF16)
    vectors = (norm1_gain, norm1_bias, out_bias, norm2_gain, norm2_bias, fc2_bias, fc1_bias)
    small = jnp.concatenate([*vectors, embedded.reshape(-1), row_table.reshape(-1), col_table.reshape(-1)])
    small = lax.all_gather(small[None], AXES, axis=0, tiled=True)
    found, start = [], 0
    for vector in vectors:
        share = vector.shape[0]
        found.append(small[:, start : start + share].reshape(1, -1).astype(F32))
        start += share
    gain_one, shift_one, b_out, gain_two, shift_two, b_down, b_up = found
    embedded_all = small[:, start : start + per * width].reshape(devices * per, width)
    start += per * width
    table_size = row_table.size
    row_full = small[:fsdp, start : start + table_size].reshape(HEADS, -1)
    col_full = small[:fsdp, start + table_size : start + 2 * table_size].reshape(HEADS, -1)

    lengths = image_lengths
    large = lengths[0] > slot_rows
    local_rows = jnp.arange(rows, dtype=jnp.int32)
    slot = jnp.where(large, 0, local_rows // slot_rows)
    spots = jnp.arange(per, dtype=jnp.int32)
    slot_pick = slot[:, None] == spots[None, :]
    slot_length = jnp.sum(jnp.where(slot_pick, lengths[None, :], 0), axis=1)
    valid = local_rows - slot * slot_rows < slot_length
    grid_index = jnp.arange(GRID, dtype=jnp.int32)
    row_hot = ((patch_cells // GRID)[:, None] == grid_index[None, :]).astype(BF16)
    col_hot = ((patch_cells % GRID)[:, None] == grid_index[None, :]).astype(BF16)
    onehot = jnp.concatenate([row_hot, col_hot, row_hot, col_hot], axis=1)
    lanes_left = ((0, 0), (head_dim, LANES - head_dim - per - 1))
    mask_q = jnp.concatenate(
        [jnp.where(slot_pick, 0.0, BIG), jnp.full((rows, 1), BIG, F32)], axis=1
    ).astype(BF16)
    mask_k = jnp.concatenate([slot_pick, jnp.logical_not(valid)[:, None]], axis=1).astype(BF16)
    mask_q, mask_k = jnp.pad(mask_q, lanes_left), jnp.pad(mask_k, lanes_left)

    offsets = grid_index[:, None] - grid_index[None, :] + GRID - 1
    diagonal = offsets[:, :, None] == jnp.arange(2 * GRID - 1, dtype=jnp.int32)[None, None, :]
    diagonal = diagonal.reshape(GRID * GRID, 2 * GRID - 1)
    both_tables = jnp.concatenate([row_full, col_full], axis=0)
    toeplitz = dot_nt(both_tables, diagonal.astype(BF16)).reshape(2, HEADS, GRID, GRID) * math.sqrt(head_dim)
    high = lax.reduce_precision(toeplitz, 8, 7)
    low = toeplitz - high
    zero = jnp.zeros((HEADS, GRID, GRID), F32)
    table = jnp.concatenate(
        [
            jnp.concatenate([high[0], zero, low[0], zero], axis=2),
            jnp.concatenate([zero, high[1], zero, low[1]], axis=2),
            jnp.zeros((HEADS, 2 * GRID, LANES), F32),
        ],
        axis=1,
    ).astype(BF16)

    share = time_weight.shape[1]
    time_part = jnp.dot(embedded_all, time_weight, preferred_element_type=F32)
    time_proj = lax.all_to_all(time_part.reshape(devices, per, share), AXES, 0, 0, tiled=True)
    time_proj = time_proj.transpose(1, 0, 2).reshape(per, 2, HEADS, head_dim)
    time_proj = jnp.where(large, time_proj[0:1], time_proj)
    time_proj = jnp.pad(time_proj, ((0, 0), (0, 0), (0, 0), (0, LANES - head_dim)))
    time_rows = time_proj.transpose(2, 1, 0, 3).reshape(HEADS, 2 * per, LANES)

    scale = 1.0 / math.sqrt(head_dim)
    normed_one, q, k, v, o, p = attend(
        tokens, gain_one, shift_one, qkv_full, time_rows, table, onehot, mask_q, mask_k, scale * math.log2(math.e)
    )
    hidden, normed_two = project(tokens, o, out_full, b_out, gain_two, shift_two)
    dy = jnp.where(valid[:, None], cotangent, jnp.zeros_like(cotangent))
    y, dn_two, d_up, d_down, db_up = mlp(normed_two, dy, up, down, b_up)
    layer_out, dh, do, d_out, vec_two = turn(hidden, y, b_down, dn_two, dy, gain_two, out_full, o)

    def shares(full, share):
        full = full.reshape(devices, share, width)
        full = jnp.pad(full, ((0, 0), (0, -share % PIECE), (0, 0)))
        return full.reshape(spread + full.shape[1:])

    up_sum, down_sum = scatter([shares(d_up, unit_share), shares(d_down, unit_share)], dims, 3)
    dqkv, d_qkv, slot_sums, pair = attend_back(normed_one, p, q, k, v, do, o, onehot, scale, per)
    d_qkv = d_qkv.reshape(HEADS, 3, LANES, width)[:, :, :head_dim].transpose(1, 0, 2, 3)
    d_out = d_out.reshape(HEADS, LANES, width)[:, :head_dim]
    d_mixed = jnp.concatenate(
        [d_qkv.reshape(devices, qkv_share, width), d_out.reshape(devices, out_share, width)], axis=1
    )
    (mixed_sum,) = scatter([shares(d_mixed, qkv_share + out_share)], dims, 4)
    input_grad, vec_one = end(tokens, dqkv, qkv_full.reshape(HEADS * 3 * LANES, width), gain_one, dh)

    slot_sums = slot_sums.reshape(HEADS, per, 3, LANES)[:, :, ::2, :head_dim]
    slot_sums = slot_sums.transpose(1, 2, 0, 3).reshape(per, 2 * width)
    merged = jnp.where(spots[:, None] == 0, jnp.sum(slot_sums, axis=0, keepdims=True), 0.0)
    slot_sums = jnp.where(large, merged, slot_sums)
    slot_sums = slot_sums.reshape(per, devices, share).transpose(1, 0, 2)
    slot_sums = lax.all_to_all(slot_sums, AXES, 0, 0, tiled=True).reshape(devices * per, share)
    time_grad = lax.dot_general(
        embedded_all.astype(F32), slot_sums, (((0,), (0,)), ((), ())), precision=HIGHEST
    )

    picked = pair[:, : 2 * GRID, : 2 * GRID]
    pairs = jnp.stack([picked[:, :GRID, :GRID], picked[:, GRID:, GRID:]]).reshape(2 * HEADS, GRID * GRID)
    tables = jnp.dot(pairs, diagonal.astype(F32), precision=HIGHEST)
    packed = [vec_one.reshape(-1), vec_two.reshape(-1), db_up.reshape(-1), tables.reshape(-1)]
    sizes = [part.shape[0] for part in packed]
    packed = lax.psum(jnp.concatenate(packed), AXES)
    place = lax.axis_index("dp") * fsdp + lax.axis_index("fsdp")
    small_share = width // devices
    vec_sum = packed[: 6 * width].reshape(6, devices, small_share)
    vec_sum = lax.dynamic_index_in_dim(vec_sum, place, 1, keepdims=False)
    up_bias = lax.dynamic_slice_in_dim(packed, 6 * width + place * unit_share, unit_share)
    tables = packed[6 * width + units :].reshape(2, fsdp, HEADS // fsdp, 2 * GRID - 1)
    tables = lax.dynamic_index_in_dim(tables, lax.axis_index("fsdp"), 1, keepdims=False)

    return (
        layer_out,
        input_grad,
        vec_sum[0],
        vec_sum[1],
        mixed_sum[:qkv_share].T,
        time_grad,
        mixed_sum[qkv_share : qkv_share + out_share],
        vec_sum[4],
        vec_sum[2],
        vec_sum[3],
        up_sum[:unit_share].T,
        up_bias,
        down_sum[:unit_share],
        vec_sum[5],
        tables[0],
        tables[1],
    )


def solution(mesh):
    rows = P(AXES, None)
    cols = P(None, AXES)
    vector = P(AXES)
    heads = P("fsdp", None)
    in_specs = (
        rows, vector, vector, vector, vector, vector, cols, cols, rows, vector, vector, vector,
        cols, vector, rows, vector, heads, heads, rows,
    )
    out_specs = (
        rows, rows, vector, vector, cols, cols, rows, vector, vector, vector, cols, vector, rows, vector,
        heads, heads,
    )
    return jax.shard_map(local, mesh=mesh, in_specs=in_specs, out_specs=out_specs, check_vma=False)
```

```python
import functools
import math

import jax
import jax.numpy as jnp
from jax import lax
from jax.experimental import pallas as pl
from jax.experimental.pallas import tpu as pltpu
from jax.sharding import PartitionSpec as P

HEADS = 16
GRID = 32
SMALL = 16
AXES = ("dp", "fsdp")
LANES = 128
PIECE = 48
BIG = -1e30
F32 = jnp.float32
BF16 = jnp.bfloat16
HIGHEST = lax.Precision.HIGHEST
MESH_ID = pl.DeviceIdType.MESH
VMEM_LIMIT = 62 * 1024 * 1024


def dot_nn(a, b):
    return lax.dot_general(a, b, (((1,), (0,)), ((), ())), preferred_element_type=F32)


def dot_nt(a, b):
    return lax.dot_general(a, b, (((1,), (1,)), ((), ())), preferred_element_type=F32)


def dot_tn(a, b):
    return lax.dot_general(a, b, (((0,), (0,)), ((), ())), preferred_element_type=F32)


def params(**more):
    return pltpu.CompilerParams(vmem_limit_bytes=VMEM_LIMIT, **more)


def resident(shape):
    zeros = (0,) * len(shape)
    return pl.BlockSpec(shape, lambda *_: zeros, pipeline_mode=pl.Buffered(1))


def split_dp(dp):
    g2 = 1 if dp <= 16 else 4
    return dp // 4 // g2, g2


class Place:
    def __init__(self, dims):
        self.G1, self.G2 = dims
        dp, self.q = lax.axis_index("dp"), lax.axis_index("fsdp")
        self.c = dp % 2
        rest = dp // 2
        self.g2 = rest % self.G2
        rest = rest // self.G2
        self.p = rest % 2
        self.g1 = rest // 2
        c, p, q = self.c, self.p, self.q
        self.ap, self.aq = (1 - p) * (1 - c) + p * c, q * (1 - c) + (1 - q) * c
        self.bp, self.bq = p * (1 - c) + (1 - p) * c, (1 - q) * (1 - c) + q * c
        self.whole = (pl.ds(0, self.G1), pl.ds(0, self.G2))

    def device(self, g1, p, g2, c, q):
        return (((g1 * 2 + p) * self.G2 + g2) * 2 + c, q)

    def line(self):
        found = []
        for step in range(1, self.G1 * self.G2):
            found.append(((self.g1 + step // self.G2) % self.G1, (self.g2 + step % self.G2) % self.G2))
        return found

    def on_line(self, spot):
        return self.device(spot[0], self.p, spot[1], self.c, self.q)

    def first(self):
        return self.device(self.g1, self.ap, self.g2, self.c, self.aq)

    def second(self):
        return self.device(self.g1, self.bp, self.g2, self.c, self.bq)

    def sibling(self):
        return self.device(self.g1, self.p, self.g2, 1 - self.c, self.q)

    def barrier_all(self):
        semaphore = pltpu.get_barrier_semaphore()
        count = self.count()

        def body(i, carry):
            pl.semaphore_signal(semaphore, inc=1, device_id=self.other(i), device_id_type=MESH_ID)
            return carry

        lax.fori_loop(1, count, body, 0)
        pl.semaphore_wait(semaphore, count - 1)

    def count(self):
        return self.G1 * self.G2 * 8

    def index(self):
        return lax.axis_index("dp") * 2 + self.q

    def other(self, i):
        to = (self.index() + i) % self.count()
        return (to // 2, to % 2)

    def barrier(self):
        partners = [self.on_line(spot) for spot in self.line()] + [self.first(), self.second(), self.sibling()]
        semaphore = pltpu.get_barrier_semaphore()
        for partner in partners:
            pl.semaphore_signal(semaphore, inc=1, device_id=partner, device_id_type=MESH_ID)
        pl.semaphore_wait(semaphore, len(partners))


def wait_for(view, semaphore):
    pltpu.make_async_copy(view, view, semaphore).wait()


class Gather:
    STAGES = 5

    def __init__(self, dims, pieces, sources, results, sems, own_sems):
        self.at = Place(dims)
        self.pieces, self.sources, self.results = pieces, sources, results
        self.sems, self.own_sems = sems, own_sems

    @staticmethod
    def scratch(dims, pieces):
        return [
            pltpu.SemaphoreType.DMA((len(pieces), 7 + dims[0] * dims[1], 2)),
            pltpu.SemaphoreType.DMA((len(pieces),)),
        ]

    def send(self, k, kind, source, target, to):
        pltpu.make_async_remote_copy(
            src_ref=source,
            dst_ref=target,
            send_sem=self.sems.at[k, kind, 0],
            recv_sem=self.sems.at[k, kind, 1],
            device_id=to,
            device_id_type=MESH_ID,
        ).start()

    def finish(self, k, kind, view):
        wait_for(view, self.sems.at[k, kind, 1])
        wait_for(view, self.sems.at[k, kind, 0])

    def stage(self, k, number):
        at = self.at
        array, start, count = self.pieces[k]
        rows = pl.ds(start, count)
        result = self.results[array]
        every, every2 = at.whole
        source = self.sources[array].at[rows]
        own = result.at[at.g1, at.p, at.g2, at.c, at.q, rows]

        def plane(p, q):
            return result.at[every, p, every2, at.c, q, rows]

        if number == 0:
            pltpu.make_async_copy(source, own, self.own_sems.at[k]).start()
            for i, spot in enumerate(at.line()):
                self.send(k, 8 + i, source, own, at.on_line(spot))
        if number == 1:
            pltpu.make_async_copy(source, own, self.own_sems.at[k]).wait()
            for i in range(len(at.line())):
                self.finish(k, 8 + i, own)
            mine = plane(at.p, at.q)
            self.send(k, 1, mine, mine, at.first())
            self.send(k, 3, mine, mine, at.sibling())
        if number == 2:
            mine, came = plane(at.p, at.q), plane(at.ap, at.aq)
            self.finish(k, 1, came)
            self.send(k, 2, mine, mine, at.second())
            self.send(k, 4, came, came, at.second())
            self.send(k, 5, came, came, at.sibling())
        if number == 3:
            for kind, came in ((2, plane(at.bp, at.bq)), (4, plane(1 - at.p, 1 - at.q))):
                self.finish(k, kind, came)
                self.send(k, 6 + kind // 4, came, came, at.sibling())
        if number == 4:
            for kind in (3, 5, 6, 7):
                self.finish(k, kind, plane(at.p, at.q))

    def round(self, number):
        for k in range(len(self.pieces)):
            if 0 <= number - k < self.STAGES:
                self.stage(k, number - k)

    def rounds(self):
        return len(self.pieces) + self.STAGES - 1


class Scatter:
    STAGES = 5

    def __init__(self, dims, pieces, sources, results, held, from_core, from_second, from_first, from_line, sems):
        self.at = Place(dims)
        self.pieces, self.sources, self.results = pieces, sources, results
        self.held, self.from_core, self.from_second = held, from_core, from_second
        self.from_first, self.from_line, self.sems = from_first, from_line, sems

    @staticmethod
    def scratch(dims, pieces, width, in_place=False):
        G1, G2 = dims
        n = len(pieces)
        return [
            pltpu.VMEM((8, LANES) if in_place else (n, G1, 2, G2, 2, PIECE, width), BF16),
            pltpu.VMEM((n, G1, 2, G2, 2, PIECE, width), BF16),
            pltpu.VMEM((n, 2, G1, G2, PIECE, width), BF16),
            pltpu.VMEM((n, G1, G2, PIECE, width), BF16),
            pltpu.VMEM((n, G1 * G2 - 1, PIECE, width), BF16),
            pltpu.SemaphoreType.DMA((n, 5 + G1 * G2, 2)),
        ]

    def send(self, k, kind, source, target, to):
        pltpu.make_async_remote_copy(
            src_ref=source,
            dst_ref=target,
            send_sem=self.sems.at[k, kind, 0],
            recv_sem=self.sems.at[k, kind, 1],
            device_id=to,
            device_id_type=MESH_ID,
        ).start()

    def add(self, target, addend):
        at = self.at

        def body(i, carry):
            g1, g2 = i // at.G2, i % at.G2
            total = target[g1, g2].astype(F32) + addend[g1, g2].astype(F32)
            target[g1, g2] = total.astype(BF16)
            return carry

        lax.fori_loop(0, at.G1 * at.G2, body, 0)

    def stage(self, k, number):
        at = self.at
        array, start, count = self.pieces[k]
        rows = pl.ds(start, count)
        source = self.sources[array]
        every, every2 = at.whole
        both = pl.ds(0, 2)
        in_place = len(self.held.shape) == 2

        def plane(p, q):
            if in_place:
                return source.at[every, p, every2, at.c, q, rows]
            return self.held.at[k, every, p, every2, q]

        local_copy = lambda: pltpu.make_async_copy(
            source.at[every, both, every2, at.c, both, rows], self.held.at[k], self.sems.at[k, 4, 0]
        )
        if number == 0:
            self.send(k, 0, source.at[every, both, every2, 1 - at.c, both, rows], self.from_core.at[k], at.sibling())
            if not in_place:
                local_copy().start()
        if number == 1:
            if not in_place:
                local_copy().wait()
            wait_for(self.from_core.at[k], self.sems.at[k, 0, 1])
            core = self.from_core.at[k]
            for p, q in ((at.bp, at.bq), (1 - at.p, 1 - at.q)):
                self.add(plane(p, q), core.at[every, p, every2, q])
            self.send(k, 1, plane(at.bp, at.bq), self.from_second.at[k, 0], at.second())
            self.send(k, 2, plane(1 - at.p, 1 - at.q), self.from_second.at[k, 1], at.second())
            for p, q in ((at.p, at.q), (at.ap, at.aq)):
                self.add(plane(p, q), core.at[every, p, every2, q])
        if number == 2:
            for kind in (1, 2):
                wait_for(self.from_second.at[k, kind - 1], self.sems.at[k, kind, 1])
            self.add(plane(at.ap, at.aq), self.from_second.at[k, 1])
            self.send(k, 3, plane(at.ap, at.aq), self.from_first.at[k], at.first())
            self.add(plane(at.p, at.q), self.from_second.at[k, 0])
        if number == 3:
            wait_for(self.from_first.at[k], self.sems.at[k, 3, 1])
            self.add(plane(at.p, at.q), self.from_first.at[k])
            mine = plane(at.p, at.q)
            for i, spot in enumerate(at.line()):
                self.send(k, 5 + i, mine.at[spot[0], spot[1]], self.from_line.at[k, i], at.on_line(spot))
        if number == 4:
            total = plane(at.p, at.q)[at.g1, at.g2].astype(F32)
            for i in range(at.G1 * at.G2 - 1):
                wait_for(self.from_line.at[k, i], self.sems.at[k, 5 + i, 1])
                total = total + self.from_line[k, i].astype(F32)
            self.results[array][rows] = total
            wait_for(self.from_core.at[k], self.sems.at[k, 0, 0])
            for kind in (1, 2):
                wait_for(self.from_second.at[k, kind - 1], self.sems.at[k, kind, 0])
            wait_for(self.from_first.at[k], self.sems.at[k, 3, 0])
            for i in range(at.G1 * at.G2 - 1):
                wait_for(self.from_line.at[k, i], self.sems.at[k, 5 + i, 0])

    def round(self, number):
        for k in range(len(self.pieces)):
            if 0 <= number - k < self.STAGES:
                self.stage(k, number - k)

    def rounds(self):
        return len(self.pieces) + self.STAGES - 1


def pieces_of(shards):
    per = [(array, start, PIECE) for array, shard in enumerate(shards) for start in range(0, shard, PIECE)]
    return sorted(per, key=lambda piece: piece[1])


def pad_rows(shard):
    rows = shard.shape[0]
    return jnp.pad(shard, ((0, -rows % PIECE), (0, 0)))


def spread_of(dims):
    return (dims[0], 2, dims[1], 2, 2)


def exchange(at, source, target, sems):
    me = at.index()

    def body(i, carry):
        to = (me + i) % at.count()
        pltpu.make_async_remote_copy(
            src_ref=source.at[to, pl.ds(0, 8)],
            dst_ref=target.at[me, pl.ds(0, 8)],
            send_sem=sems.at[0],
            recv_sem=sems.at[1],
            device_id=at.other(i),
            device_id_type=MESH_ID,
        ).start()
        return carry

    lax.fori_loop(1, at.count(), body, 0)


def exchanged(at, target, sems):
    view = target.at[pl.ds(0, at.count() - 1), pl.ds(0, 8)]
    wait_for(view, sems.at[1])
    wait_for(view, sems.at[0])


def begin_kernel(dims, pieces, shares, head_dim, mixed_shard, small_shard, time_weight, qkv_out, out_out, small_out,
                 time_out, mixed, small, time_all, time_got, sems, own_sems, time_sems):
    work = Gather(dims, pieces, (small_shard, mixed_shard), (small, mixed), sems, own_sems)
    at = work.at
    devices = at.count()
    width = mixed.shape[-1]
    at.barrier_all()
    for number in range(work.rounds()):
        work.round(number)
        if number == Gather.STAGES - 1:
            small_out[...] = small[...].reshape(small_out.shape)
            for start in range(0, devices, 32):
                span = pl.ds(start, 32)
                rows = small_out[span].reshape(32 * small_out.shape[1], width)
                time_all[span] = dot_nn(rows, time_weight[...]).reshape(32, small_out.shape[1], LANES)
            exchange(at, time_all, time_got, time_sems)
    exchanged(at, time_got, time_sems)
    time_got[at.index()] = time_all[at.index(), 0:8]
    time_out[...] = time_got[...]

    def rows_of(first, share, base):
        parts, left = [], head_dim
        while left:
            device, offset = divmod(first, share)
            count = min(left, share - offset)
            place = []
            for size in reversed(spread_of(dims)):
                device, digit = divmod(device, size)
                place.insert(0, digit)
            parts.append(mixed[(*place, slice(base + offset, base + offset + count))])
            first, left = first + count, left - count
        parts.append(jnp.zeros((LANES - head_dim, width), BF16))
        return jnp.concatenate(parts, axis=0)

    for head in range(HEADS):
        for kind in range(3):
            qkv_out[head, kind * LANES : (kind + 1) * LANES] = rows_of((kind * HEADS + head) * head_dim, shares[0], 0)
        out_out[head * LANES : (head + 1) * LANES] = rows_of(head * head_dim, shares[1], shares[0])


def begin(mixed_shard, small_shard, time_weight, dims, shares, head_dim):
    width = mixed_shard.shape[1]
    small_rows = small_shard.shape[0]
    devices = dims[0] * dims[1] * 8
    pieces = [(0, 0, small_rows)] + [(1, start, PIECE) for start in range(0, mixed_shard.shape[0], PIECE)]
    anywhere = pl.BlockSpec(memory_space=pl.ANY)
    vmem = pl.BlockSpec(memory_space=pltpu.VMEM)
    return pl.pallas_call(
        functools.partial(begin_kernel, dims, pieces, shares, head_dim),
        in_specs=[anywhere, anywhere, vmem],
        out_specs=[vmem] * 4,
        out_shape=[
            jax.ShapeDtypeStruct((HEADS, 3 * LANES, width), BF16),
            jax.ShapeDtypeStruct((HEADS * LANES, width), BF16),
            jax.ShapeDtypeStruct((devices, small_rows, width), BF16),
            jax.ShapeDtypeStruct((devices, 8, LANES), F32),
        ],
        scratch_shapes=[
            pltpu.VMEM(spread_of(dims) + mixed_shard.shape, BF16),
            pltpu.VMEM(spread_of(dims) + small_shard.shape, BF16),
            pltpu.VMEM((devices, small_rows, LANES), F32),
            pltpu.VMEM((devices, 8, LANES), F32),
            *Gather.scratch(dims, pieces),
            pltpu.SemaphoreType.DMA((2,)),
        ],
        compiler_params=params(collective_id=1, has_side_effects=True),
        name="begin",
    )(mixed_shard, small_shard, time_weight)


def normalise(values):
    centre = values - jnp.mean(values, axis=-1, keepdims=True)
    inverse = lax.rsqrt(jnp.mean(centre * centre, axis=-1, keepdims=True) + 1e-06)
    return centre * inverse, inverse


def norm_back(values, gain, grad):
    unit, inverse = normalise(values)
    scaled = grad * gain
    inner = jnp.mean(scaled, axis=-1, keepdims=True) + unit * jnp.mean(scaled * unit, axis=-1, keepdims=True)
    return inverse * (scaled - inner), unit


def spaced(work, step, steps):
    last = work.rounds() - 1
    for number in range(last):
        at_step = number * steps // last

        @pl.when(step == at_step)
        def _(number=number):
            work.round(number)


def attend_kernel(factor, block, dims, pieces, tokens, gain, shift, weight, time_q, time_v, large, table, onehot,
                  mask_q, mask_k, up_shard, down_shard,
                  normed_out, q_out, k_out, v_out, o_out, p_out, up_out, down_out, keys, sems, own_sems):
    rows = tokens.shape[0]
    work = Gather(dims, pieces, (up_shard, down_shard), (up_out, down_out), sems, own_sems)
    step = pl.program_id(0)

    @pl.when(step == 0)
    def _():
        work.at.barrier()

    spaced(work, step, HEADS)

    @pl.when(pl.program_id(0) == 0)
    def _():
        for start in range(0, rows, block):
            span = pl.ds(start, block)
            unit, _ = normalise(tokens[span].astype(F32))
            normed_out[span] = (unit * gain[...] + shift[...]).astype(BF16)

    per = rows // (SMALL * SMALL)
    slot = rows // per
    one = large[...] > 0.0
    for i in range(per):
        span = pl.ds(i * slot, slot)
        qkv = dot_nt(normed_out[span], weight[0])
        add_q = jnp.where(one, time_q[0, 0:1], time_q[0, i : i + 1])
        add_v = jnp.where(one, time_v[0, 0:1], time_v[0, i : i + 1])
        q_out[0, span] = (qkv[:, :LANES] + add_q).astype(BF16)
        k_out[0, span] = qkv[:, LANES : 2 * LANES].astype(BF16)
        v_out[0, span] = (qkv[:, 2 * LANES :] + add_v).astype(BF16)
    keys[:, :LANES] = k_out[0] + mask_k[...]
    keys[:, LANES:] = onehot[...]
    for start in range(0, rows, block):
        span = pl.ds(start, block)
        bias = dot_nn(onehot[span], table[0]).astype(BF16)
        query = jnp.concatenate([q_out[0, span] + mask_q[span], bias], axis=1)
        scores = dot_nt(query, keys[...])
        top = jnp.max(scores, axis=1, keepdims=True)
        weights = jnp.exp2((scores - top) * factor)
        total = jnp.sum(weights, axis=1, keepdims=True)
        low = (weights * (1.0 / total)).astype(BF16)
        p_out[0, span] = low
        o_out[span] = dot_nn(low, v_out[0]).astype(BF16)

    @pl.when(step == HEADS - 1)
    def _():
        work.round(work.rounds() - 1)


def attend(tokens, gain, shift, weight, times, large, table, onehot, mask_q, mask_k, factor, shards, dims):
    rows, width = tokens.shape
    block = min(256, rows)
    pieces = pieces_of([shard.shape[0] for shard in shards])
    anywhere = pl.BlockSpec(memory_space=pl.ANY)
    per_head = lambda *shape: pl.BlockSpec((1,) + shape, lambda h: (h, 0, 0))
    head_rows = jax.ShapeDtypeStruct((HEADS, rows, LANES), BF16)
    return pl.pallas_call(
        functools.partial(attend_kernel, factor, block, dims, pieces),
        grid=(HEADS,),
        in_specs=[
            resident(tokens.shape),
            resident(gain.shape),
            resident(shift.shape),
            per_head(3 * LANES, width),
            pl.BlockSpec((1, 8, LANES), lambda h: (h, 0, 0)),
            pl.BlockSpec((1, 8, LANES), lambda h: (HEADS + h, 0, 0)),
            resident(large.shape),
            per_head(LANES, LANES),
            resident(onehot.shape),
            resident(mask_q.shape),
            resident(mask_k.shape),
            anywhere,
            anywhere,
        ],
        out_specs=[
            resident(tokens.shape),
            per_head(rows, LANES),
            per_head(rows, LANES),
            per_head(rows, LANES),
            pl.BlockSpec((rows, LANES), lambda h: (0, h)),
            per_head(rows, rows),
            anywhere,
            anywhere,
        ],
        out_shape=[
            jax.ShapeDtypeStruct(tokens.shape, BF16),
            head_rows,
            head_rows,
            head_rows,
            jax.ShapeDtypeStruct((rows, HEADS * LANES), BF16),
            jax.ShapeDtypeStruct((HEADS, rows, rows), BF16),
            *[jax.ShapeDtypeStruct(spread_of(dims) + s.shape, BF16) for s in shards],
        ],
        scratch_shapes=[pltpu.VMEM((rows, 2 * LANES), BF16), *Gather.scratch(dims, pieces)],
        compiler_params=params(collective_id=2, has_side_effects=True),
        name="attend",
    )(tokens, gain, shift, weight, times, times, large, table, onehot, mask_q, mask_k, *shards)


def attend_back_kernel(block, scale, dims, pieces, normed, p, q, k, v, do, o, onehot, large, d_up, d_down,
                       dqkv_out, dw_out, sums_q, sums_v, pair_out, up_out, down_out,
                       keys, grads, dk_sum, dv_sum, *buffers):
    rows = normed.shape[0]
    work = Scatter(dims, pieces, (d_up, d_down), (up_out, down_out), *buffers)
    step = pl.program_id(0)

    @pl.when(step == 0)
    def _():
        work.at.barrier()

    spaced(work, step, HEADS)
    lane = lax.broadcasted_iota(jnp.int32, (rows, LANES), 1)
    head = 72
    delta = jnp.sum(do[...].astype(F32) * o[...].astype(F32), axis=1, keepdims=True)
    high = delta.astype(BF16).astype(F32)
    more = jnp.where(lane == head, -high, jnp.where(lane == head + 1, high - delta, 0.0))
    grads[...] = (do[...].astype(F32) + more).astype(BF16)
    values = v[0] + jnp.where((lane == head) | (lane == head + 1), 1.0, 0.0).astype(BF16)
    keys[:, :LANES] = k[0]
    keys[:, LANES:] = onehot[...]
    pair = jnp.zeros((LANES, LANES), F32)
    for start in range(0, rows, block):
        span = pl.ds(start, block)
        centred = dot_nt(grads[span], values)
        ds = (p[0, span].astype(F32) * centred).astype(BF16)
        both = dot_nn(ds, keys[...])
        dqkv_out[span, :LANES] = (both[:, :LANES] * scale).astype(BF16)
        pair = pair + lax.dot_general(
            onehot[span].astype(F32), both[:, LANES:], (((0,), (0,)), ((), ())),
            preferred_element_type=F32, precision=HIGHEST,
        )
        dk = dot_tn(ds, q[0, span])
        dv = dot_tn(p[0, span], do[span])
        if start == 0:
            dk_sum[...] = dk
            dv_sum[...] = dv
        else:
            dk_sum[...] += dk
            dv_sum[...] += dv
    dqkv_out[:, LANES : 2 * LANES] = (dk_sum[...] * scale).astype(BF16)
    dqkv_out[:, 2 * LANES :] = dv_sum[...].astype(BF16)
    pair_out[0] = pair
    slot = SMALL * SMALL
    one = large[...] > 0.0
    for target, base in ((sums_q, 0), (sums_v, 2 * LANES)):
        sums = []
        for start in range(0, rows, slot):
            part = dqkv_out[pl.ds(start, slot), base : base + LANES]
            sums.append(jnp.sum(part.astype(F32), axis=0, keepdims=True))
        total = functools.reduce(jnp.add, sums)
        sums = [jnp.where(one, total if i == 0 else jnp.zeros_like(total), part) for i, part in enumerate(sums)]
        sums.append(jnp.zeros((8 - len(sums), LANES), F32))
        target[0] = jnp.concatenate(sums, axis=0)
    dw_out[0] = dot_tn(dqkv_out[...], normed[...]).astype(BF16)

    @pl.when(step == HEADS - 1)
    def _():
        work.round(work.rounds() - 1)


def attend_back(normed, p, q, k, v, do, o, onehot, large, scale, parts, dims):
    rows, width = normed.shape
    block = min(256, rows)
    pieces = pieces_of([part.shape[5] for part in parts])
    anywhere = pl.BlockSpec(memory_space=pl.ANY)
    per_head = lambda *shape: pl.BlockSpec((1,) + shape, lambda h: (h, 0, 0))
    head_cols = pl.BlockSpec((rows, LANES), lambda h: (0, h))
    return pl.pallas_call(
        functools.partial(attend_back_kernel, block, scale, dims, pieces),
        grid=(HEADS,),
        in_specs=[
            resident(normed.shape),
            per_head(rows, rows),
            per_head(rows, LANES),
            per_head(rows, LANES),
            per_head(rows, LANES),
            head_cols,
            head_cols,
            resident(onehot.shape),
            resident(large.shape),
            anywhere,
            anywhere,
        ],
        out_specs=[
            pl.BlockSpec((rows, 3 * LANES), lambda h: (0, h)),
            per_head(3 * LANES, width),
            per_head(8, LANES),
            per_head(8, LANES),
            per_head(LANES, LANES),
            *[resident(part.shape[5:]) for part in parts],
        ],
        out_shape=[
            jax.ShapeDtypeStruct((rows, HEADS * 3 * LANES), BF16),
            jax.ShapeDtypeStruct((HEADS, 3 * LANES, width), BF16),
            jax.ShapeDtypeStruct((HEADS, 8, LANES), F32),
            jax.ShapeDtypeStruct((HEADS, 8, LANES), F32),
            jax.ShapeDtypeStruct((HEADS, LANES, LANES), F32),
            *[jax.ShapeDtypeStruct(part.shape[5:], F32) for part in parts],
        ],
        scratch_shapes=[
            pltpu.VMEM((rows, 2 * LANES), BF16),
            pltpu.VMEM((rows, LANES), BF16),
            pltpu.VMEM((rows, LANES), F32),
            pltpu.VMEM((rows, LANES), F32),
            *Scatter.scratch(dims, pieces, width),
        ],
        compiler_params=params(collective_id=3, has_side_effects=True),
        name="attend_back",
    )(normed, p, q, k, v, do, o, onehot, large, *parts)


def project_kernel(tokens, o, weight, bias, gain, shift, hidden_out, normed_out):
    hidden = tokens[...].astype(F32) + (dot_nn(o[...], weight[...]) + bias[...])
    hidden_out[...] = hidden
    unit, _ = normalise(hidden)
    normed_out[...] = (unit * gain[...] + shift[...]).astype(BF16)


def project(tokens, o, weight, bias, gain, shift):
    rows, width = tokens.shape
    block = min(256, rows)
    by_rows = lambda cols: pl.BlockSpec((block, cols), lambda i: (i, 0))
    return pl.pallas_call(
        project_kernel,
        grid=(rows // block,),
        in_specs=[by_rows(width), by_rows(o.shape[1]), resident(weight.shape)] + [resident((1, width))] * 3,
        out_specs=[by_rows(width), by_rows(width)],
        out_shape=[jax.ShapeDtypeStruct(tokens.shape, F32), jax.ShapeDtypeStruct(tokens.shape, BF16)],
        compiler_params=params(),
        name="project",
    )(tokens, o, weight, bias, gain, shift)


def normal_parts(u):
    size = jnp.abs(u)
    bell = jnp.exp(-0.5 * u * u)
    t = 1.0 / (1.0 + (0.3275911 * math.sqrt(0.5)) * size)
    poly = t * (
        0.5 * 0.254829592
        + t * (0.5 * -0.284496736 + t * (0.5 * 1.421413741 + t * (0.5 * -1.453152027 + t * (0.5 * 1.061405429))))
    )
    tail = poly * bell
    return jnp.where(u >= 0.0, 1.0 - tail, tail), bell * (1.0 / math.sqrt(2.0 * math.pi))


def mlp_kernel(normed, dy, up, down, bias, y_out, dn_out, dup_out, ddown_out, dbias_out):
    rows = normed.shape[0]
    first = pl.program_id(0) == 0
    u = dot_nt(normed[...], up[...]) + bias[...]
    phi, density = normal_parts(u)
    act = (u * phi).astype(BF16)
    slope = phi + u * density
    du = (slope * dot_nt(dy[...], down[...])).astype(BF16)
    dbias_out[...] = jnp.sum(du.astype(F32), axis=0, keepdims=True)
    y = dot_nn(act, down[...])
    dn = dot_nn(du, up[...])

    @pl.when(first)
    def _():
        y_out[...] = y
        dn_out[...] = dn

    @pl.when(jnp.logical_not(first))
    def _():
        y_out[...] += y
        dn_out[...] += dn

    ddown_out[...] = dot_tn(act, dy[...]).astype(BF16)
    dup_out[...] = dot_tn(du, normed[...]).astype(BF16)


def mlp(normed, dy, up, down, bias):
    rows, width = normed.shape
    units = up.shape[0]
    block = 512
    by_units = pl.BlockSpec((block, width), lambda i: (i, 0))
    by_bias = pl.BlockSpec((1, block), lambda i: (0, i))
    return pl.pallas_call(
        mlp_kernel,
        grid=(units // block,),
        in_specs=[resident(normed.shape), resident(dy.shape), by_units, by_units, by_bias],
        out_specs=[resident(normed.shape), resident(normed.shape), by_units, by_units, by_bias],
        out_shape=[
            jax.ShapeDtypeStruct(normed.shape, F32),
            jax.ShapeDtypeStruct(normed.shape, F32),
            jax.ShapeDtypeStruct(up.shape, BF16),
            jax.ShapeDtypeStruct(down.shape, BF16),
            jax.ShapeDtypeStruct((1, units), F32),
        ],
        compiler_params=params(),
        name="mlp",
    )(normed, dy, up, down, bias)


def turn_kernel(hidden, y, bias, dn, dy, gain, weight, o, out, dh_out, do_out, dw_out, vec_out, dw_sum):
    first = pl.program_id(0) == 0
    last = pl.program_id(0) == pl.num_programs(0) - 1
    out[...] = (hidden[...] + (y[...] + bias[...])).astype(BF16)
    back, unit = norm_back(hidden[...], gain[...], dn[...])
    dyf = dy[...].astype(F32)
    dh = dyf + back
    dh_out[...] = dh
    da = dh.astype(BF16)
    do_out[...] = dot_nt(da, weight[...]).astype(BF16)
    dw = dot_tn(o[...], da)
    sums = jnp.concatenate(
        [
            jnp.sum(dn[...] * unit, axis=0, keepdims=True),
            jnp.sum(dn[...], axis=0, keepdims=True),
            jnp.sum(da.astype(F32), axis=0, keepdims=True),
            jnp.sum(dyf, axis=0, keepdims=True),
        ],
        axis=0,
    )

    @pl.when(first)
    def _():
        dw_sum[...] = dw
        vec_out[...] = sums

    @pl.when(jnp.logical_not(first))
    def _():
        dw_sum[...] += dw
        vec_out[...] += sums

    @pl.when(last)
    def _():
        dw_out[...] = dw_sum[...].astype(BF16)


def turn(hidden, y, bias, dn, dy, gain, weight, o):
    rows, width = hidden.shape
    block = min(256, rows)
    by_rows = lambda cols: pl.BlockSpec((block, cols), lambda i: (i, 0))
    wide = weight.shape[0]
    return pl.pallas_call(
        turn_kernel,
        grid=(rows // block,),
        in_specs=[
            by_rows(width),
            by_rows(width),
            resident((1, width)),
            by_rows(width),
            by_rows(width),
            resident((1, width)),
            resident(weight.shape),
            by_rows(wide),
        ],
        out_specs=[by_rows(width), by_rows(width), by_rows(wide), resident(weight.shape), resident((4, width))],
        out_shape=[
            jax.ShapeDtypeStruct(hidden.shape, BF16),
            jax.ShapeDtypeStruct(hidden.shape, F32),
            jax.ShapeDtypeStruct((rows, wide), BF16),
            jax.ShapeDtypeStruct(weight.shape, BF16),
            jax.ShapeDtypeStruct((4, width), F32),
        ],
        scratch_shapes=[pltpu.VMEM(weight.shape, F32)],
        compiler_params=params(),
        name="turn",
    )(hidden, y, bias, dn, dy, gain, weight, o)


class SumAll:
    STAGES = 5

    def __init__(self, at, total, send, got, sems):
        self.at, self.total, self.send, self.got, self.sems = at, total, send, got, sems

    @staticmethod
    def scratch(dims, shape):
        copies = 2 + dims[0] * dims[1]
        return [
            pltpu.VMEM(shape, F32),
            pltpu.VMEM((4,) + shape, F32),
            pltpu.VMEM((copies,) + shape, F32),
            pltpu.SemaphoreType.DMA((copies, 2)),
        ]

    def start(self, stage, kind, to):
        pltpu.make_async_remote_copy(
            src_ref=self.send.at[stage],
            dst_ref=self.got.at[kind],
            send_sem=self.sems.at[kind, 0],
            recv_sem=self.sems.at[kind, 1],
            device_id=to,
            device_id_type=MESH_ID,
        ).start()

    def take(self, kind):
        wait_for(self.got.at[kind], self.sems.at[kind, 1])
        wait_for(self.got.at[kind], self.sems.at[kind, 0])

    def stage(self, number):
        at = self.at
        p_next = at.device(at.g1, 1 - at.p, at.g2, at.c, at.q)
        q_next = at.device(at.g1, at.p, at.g2, at.c, 1 - at.q)
        if 0 < number < 4:
            self.take(number - 1)
            self.total[...] += self.got[number - 1]
        if number < 4:
            self.send[number] = self.total[...]
        if number < 3:
            self.start(number, number, (at.sibling(), p_next, q_next)[number])
        if number == 3:
            line = at.G1 * at.G2
            mine = at.g1 * at.G2 + at.g2
            for i, spot in enumerate(at.line()):
                self.start(3, 3 + i, at.on_line(spot))
        if number == 4:
            line = at.G1 * at.G2
            mine = at.g1 * at.G2 + at.g2
            for i in range(line - 1):
                self.take(3 + i)
            spots = [spot[0] * at.G2 + spot[1] for spot in at.line()]
            parts = [self.got[3 + i] for i in range(line - 1)] + [self.send[3]]
            spots.append(mine)
            total = jnp.zeros_like(parts[0])
            for place in range(line):
                chosen = jnp.zeros_like(parts[0])
                for spot, part in zip(spots, parts):
                    chosen = jnp.where(spot == place, part, chosen)
                total = total + chosen
            self.total[...] = total


def end_kernel(dims, pieces, shares, head_dim, tokens, dqkv, weight, gain, dh, small, time_send, vec_in, dw, dw_out,
               out, vec_out, time_out, mixed_out, mixed, dw_buffer, dw_sems, time_got, time_sems,
               vec_total, vec_send, vec_got, vec_sems, *buffers):
    step = pl.program_id(0)
    steps = pl.num_programs(0)
    work = Scatter(dims, pieces, (mixed,), (mixed_out,), *buffers)
    at = work.at
    sums = SumAll(at, vec_total, vec_send, vec_got, vec_sems)
    width = tokens.shape[1]
    fetches = HEADS + HEADS // 2
    pair = 2 * LANES

    def fetch(number):
        slot = number % 2
        if number < HEADS:
            return pltpu.make_async_copy(dw.at[number], dw_buffer.at[slot], dw_sems.at[slot])
        source = dw_out.at[pl.ds((number - HEADS) * pair, pair)]
        return pltpu.make_async_copy(source, dw_buffer.at[slot, pl.ds(0, pair)], dw_sems.at[slot])

    def place_of(device):
        place = []
        for size in reversed(spread_of(dims)):
            device, digit = divmod(device, size)
            place.insert(0, digit)
        return tuple(place)

    def put(first, share, base, value):
        done = 0
        while done < head_dim:
            device, offset = divmod(first + done, share)
            count = min(head_dim - done, share - offset)
            mixed[(*place_of(device), slice(base + offset, base + offset + count))] = value[done : done + count]
            done += count

    @pl.when(step == 0)
    def _():
        fetch(0).start()
        time_got[...] = jnp.zeros_like(time_got)
        at.barrier_all()
        exchange(at, time_send, time_got, time_sems)
        vec_total[...] = vec_in[...]
        for number in range(fetches):
            if number + 1 < fetches:
                fetch(number + 1).start()
            fetch(number).wait()
            if number < HEADS:
                for kind in range(3):
                    value = dw_buffer[number % 2, kind * LANES : kind * LANES + head_dim]
                    put((kind * HEADS + number) * head_dim, shares[0], 0, value)
            else:
                for i in range(2):
                    head = (number - HEADS) * 2 + i
                    value = dw_buffer[number % 2, i * LANES : i * LANES + head_dim]
                    put(head * head_dim, shares[1], shares[0], value)
        work.round(0)

    @pl.when(step == 3)
    def _():
        work.round(1)

    @pl.when(step == 6)
    def _():
        work.round(2)

    dn = dot_nn(dqkv[...], weight[...])
    back, unit = norm_back(tokens[...].astype(F32), gain[...], dn)
    out[...] = (dh[...] + back).astype(BF16)
    vec_total[0:1] += jnp.sum(dn * unit, axis=0, keepdims=True)
    vec_total[1:2] += jnp.sum(dn, axis=0, keepdims=True)

    @pl.when(step == steps - 1)
    def _():
        sums.stage(0)
        exchanged(at, time_got, time_sems)
        time_got[at.index(), 0:8] = time_send[at.index()]
        for number in range(3, max(work.rounds(), 7)):
            if number < work.rounds():
                work.round(number)
            if number < 7:
                sums.stage(number - 2)
        vec_out[...] = vec_total[...]
        times = time_got[...].reshape(small.shape[0], LANES)
        high = times.astype(BF16)
        low = (times - high.astype(F32)).astype(BF16)
        time_out[...] = dot_tn(small[...], high) + dot_tn(small[...], low)


def end(tokens, dqkv, weight, gain, dh, small, time_send, vec_in, dw, dw_out, dims, shares, head_dim):
    rows, width = tokens.shape
    block = rows // 8
    by_rows = lambda cols: pl.BlockSpec((block, cols), lambda i: (i, 0))
    shard_rows = -(-sum(shares) // PIECE) * PIECE
    pieces = pieces_of([shard_rows])
    anywhere = pl.BlockSpec(memory_space=pl.ANY)
    devices = time_send.shape[0]
    return pl.pallas_call(
        functools.partial(end_kernel, dims, pieces, shares, head_dim),
        grid=(rows // block,),
        in_specs=[
            by_rows(width),
            by_rows(dqkv.shape[1]),
            resident(weight.shape),
            resident((1, width)),
            by_rows(width),
            resident(small.shape),
            resident(time_send.shape),
            resident(vec_in.shape),
            anywhere,
            anywhere,
        ],
        out_specs=[
            by_rows(width),
            resident(vec_in.shape),
            resident((width, LANES)),
            resident((shard_rows, width)),
        ],
        out_shape=[
            jax.ShapeDtypeStruct(tokens.shape, BF16),
            jax.ShapeDtypeStruct(vec_in.shape, F32),
            jax.ShapeDtypeStruct((width, LANES), F32),
            jax.ShapeDtypeStruct((shard_rows, width), F32),
        ],
        scratch_shapes=[
            pltpu.VMEM(spread_of(dims) + (shard_rows, width), BF16),
            pltpu.VMEM((2,) + dw.shape[1:], BF16),
            pltpu.SemaphoreType.DMA((2,)),
            pltpu.VMEM((devices, small.shape[0] // devices, LANES), F32),
            pltpu.SemaphoreType.DMA((2,)),
            *SumAll.scratch(dims, vec_in.shape),
            *Scatter.scratch(dims, pieces, width, in_place=True),
        ],
        compiler_params=params(collective_id=4, has_side_effects=True),
        name="end",
    )(tokens, dqkv, weight, gain, dh, small, time_send, vec_in, dw, dw_out)


def time_embed(stamps, feat_width):
    half_width = feat_width // 2
    frequency = jnp.exp(-math.log(10000.0) * jnp.arange(half_width, dtype=F32) / half_width)
    angles = stamps.astype(F32)[:, None] * frequency[None, :]
    return jnp.concatenate([jnp.cos(angles), jnp.sin(angles)], axis=1)


def local(
    tokens,
    image_lengths,
    timesteps,
    patch_cells,
    norm1_gain,
    norm1_bias,
    qkv_weight,
    time_weight,
    out_weight,
    out_bias,
    norm2_gain,
    norm2_bias,
    fc1_weight,
    fc1_bias,
    fc2_weight,
    fc2_bias,
    row_table,
    col_table,
    cotangent,
):
    rows, width = tokens.shape
    head_dim = width // HEADS
    slot_rows = SMALL * SMALL
    per = image_lengths.shape[0]
    assert rows == GRID * GRID and per * slot_rows == rows
    fsdp = lax.axis_size("fsdp")
    devices = lax.axis_size("dp") * fsdp
    dims = split_dp(lax.axis_size("dp"))

    qkv_share, out_share = qkv_weight.shape[1], out_weight.shape[0]
    unit_share, time_share = fc1_weight.shape[1], time_weight.shape[1]
    units = devices * unit_share
    mixed_shard = pad_rows(jnp.concatenate([qkv_weight.T, out_weight], axis=0))
    embedded = time_embed(timesteps, width).astype(BF16)
    vectors = jnp.concatenate([norm1_gain, norm1_bias, out_bias, norm2_gain, norm2_bias, fc2_bias, fc1_bias])
    table_size = row_table.size
    to_row = lambda flat: jnp.pad(flat, (0, width - flat.shape[0]))[None]
    both_tables = jnp.concatenate([row_table.reshape(-1), col_table.reshape(-1)])
    small_shard = jnp.concatenate([embedded, to_row(vectors), to_row(both_tables)], axis=0)
    small_shard = jnp.pad(small_shard, ((0, -small_shard.shape[0] % 16), (0, 0)))
    time_padded = jnp.pad(time_weight, ((0, 0), (0, LANES - time_share)))
    shares = (qkv_share, out_share)
    qkv_full, out_full, small, times = begin(mixed_shard, small_shard, time_padded, dims, shares, head_dim)
    gathered = small[:, per]
    vector_share = norm1_gain.shape[0]
    vectors = gathered[:, : 6 * vector_share].reshape(devices, 6, vector_share).transpose(1, 0, 2)
    vectors = vectors.reshape(6, width).astype(F32)
    gain_one, shift_one, b_out, gain_two, shift_two, b_down = (vectors[i : i + 1] for i in range(6))
    b_up = gathered[:, 6 * vector_share : 6 * vector_share + unit_share].reshape(1, units).astype(F32)
    tables = small[:fsdp, per + 1, : 2 * table_size].reshape(fsdp, 2, HEADS // fsdp, 2 * GRID - 1)
    tables = tables.transpose(1, 0, 2, 3).reshape(2 * HEADS, 2 * GRID - 1)

    lengths = image_lengths
    large = lengths[0] > slot_rows
    local_rows = jnp.arange(rows, dtype=jnp.int32)
    slot = jnp.where(large, 0, local_rows // slot_rows)
    spots = jnp.arange(per, dtype=jnp.int32)
    slot_pick = slot[:, None] == spots[None, :]
    slot_length = jnp.sum(jnp.where(slot_pick, lengths[None, :], 0), axis=1)
    valid = local_rows - slot * slot_rows < slot_length
    grid_index = jnp.arange(GRID, dtype=jnp.int32)
    row_hot = ((patch_cells // GRID)[:, None] == grid_index[None, :]).astype(BF16)
    col_hot = ((patch_cells % GRID)[:, None] == grid_index[None, :]).astype(BF16)
    onehot = jnp.concatenate([row_hot, col_hot, row_hot, col_hot], axis=1)
    lanes_left = ((0, 0), (head_dim, LANES - head_dim - per - 1))
    mask_q = jnp.concatenate(
        [jnp.where(slot_pick, 0.0, BIG), jnp.full((rows, 1), BIG, F32)], axis=1
    ).astype(BF16)
    mask_k = jnp.concatenate([slot_pick, jnp.logical_not(valid)[:, None]], axis=1).astype(BF16)
    mask_q, mask_k = jnp.pad(mask_q, lanes_left), jnp.pad(mask_k, lanes_left)

    offsets = grid_index[:, None] - grid_index[None, :] + GRID - 1
    diagonal = offsets[:, :, None] == jnp.arange(2 * GRID - 1, dtype=jnp.int32)[None, None, :]
    diagonal = diagonal.reshape(GRID * GRID, 2 * GRID - 1)
    toeplitz = dot_nt(tables, diagonal.astype(BF16)).reshape(2, HEADS, GRID, GRID) * math.sqrt(head_dim)
    high = lax.reduce_precision(toeplitz, 8, 7)
    low = toeplitz - high
    zero = jnp.zeros((HEADS, GRID, GRID), F32)
    table = jnp.concatenate(
        [
            jnp.concatenate([high[0], zero, low[0], zero], axis=2),
            jnp.concatenate([zero, high[1], zero, low[1]], axis=2),
            jnp.zeros((HEADS, 2 * GRID, LANES), F32),
        ],
        axis=1,
    ).astype(BF16)

    if time_share != head_dim:
        times = times[:, :per, :time_share].transpose(1, 0, 2).reshape(per, 2 * HEADS, head_dim)
        times = jnp.pad(times.transpose(1, 0, 2), ((0, 0), (0, 8 - per), (0, LANES - head_dim)))

    scale = 1.0 / math.sqrt(head_dim)
    large_lanes = jnp.broadcast_to(large.astype(F32), (1, LANES))
    normed_one, q, k, v, o, p, up, down = attend(
        tokens, gain_one, shift_one, qkv_full, times, large_lanes, table, onehot, mask_q, mask_k,
        scale * math.log2(math.e), (pad_rows(fc1_weight.T), pad_rows(fc2_weight)), dims,
    )
    up = up.reshape(devices, -1, width)[:, :unit_share].reshape(units, width)
    down = down.reshape(devices, -1, width)[:, :unit_share].reshape(units, width)
    hidden, normed_two = project(tokens, o, out_full, b_out, gain_two, shift_two)
    dy = jnp.where(valid[:, None], cotangent, jnp.zeros_like(cotangent))
    y, dn_two, d_up, d_down, db_up = mlp(normed_two, dy, up, down, b_up)
    layer_out, dh, do, d_out, vec_two = turn(hidden, y, b_down, dn_two, dy, gain_two, out_full, o)

    def by_device(full, share):
        full = full.reshape(devices, share, width)
        full = jnp.pad(full, ((0, 0), (0, -share % PIECE), (0, 0)))
        return full.reshape(spread_of(dims) + full.shape[1:])

    dqkv, d_qkv, sums_q, sums_v, pair, up_sum, down_sum = attend_back(
        normed_one, p, q, k, v, do, o, onehot, large_lanes, scale,
        (by_device(d_up, unit_share), by_device(d_down, unit_share)), dims,
    )
    time_send = jnp.concatenate([sums_q, sums_v], axis=0)
    if time_share != head_dim:
        time_send = time_send[:, :per, :head_dim].transpose(1, 0, 2).reshape(per, devices, time_share)
        time_send = jnp.pad(time_send.transpose(1, 0, 2), ((0, 0), (0, 8 - per), (0, LANES - time_share)))
    pairs = jnp.concatenate([pair[:, :GRID, :GRID], pair[:, GRID : 2 * GRID, GRID : 2 * GRID]])
    tables = jnp.dot(pairs.reshape(2 * HEADS, GRID * GRID), diagonal.astype(F32), precision=HIGHEST)
    tables = tables.reshape(2, HEADS * (2 * GRID - 1))
    vec_in = jnp.concatenate(
        [
            jnp.zeros((2, width), F32),
            vec_two,
            db_up.reshape(units // width, width),
            jnp.pad(tables, ((0, 0), (0, width - tables.shape[1]))),
        ],
        axis=0,
    )
    vec_in = jnp.pad(vec_in, ((0, -vec_in.shape[0] % 8), (0, 0)))
    input_grad, vec_all, time_grad, mixed_sum = end(
        tokens, dqkv, qkv_full.reshape(HEADS * 3 * LANES, width), gain_one, dh,
        small.reshape(-1, width), time_send, vec_in, d_qkv, d_out, dims, shares, head_dim,
    )

    place = lax.axis_index("dp") * fsdp + lax.axis_index("fsdp")
    vec_sum = lax.dynamic_slice_in_dim(vec_all[:6], place * vector_share, vector_share, 1)
    up_bias = vec_all[6 : 6 + units // width].reshape(units)
    up_bias = lax.dynamic_slice_in_dim(up_bias, place * unit_share, unit_share)
    tables = vec_all[6 + units // width :][:2, : HEADS * (2 * GRID - 1)].reshape(2, fsdp, -1, 2 * GRID - 1)
    tables = lax.dynamic_index_in_dim(tables, lax.axis_index("fsdp"), 1, keepdims=False)

    return (
        layer_out,
        input_grad,
        vec_sum[0],
        vec_sum[1],
        mixed_sum[:qkv_share].T,
        time_grad[:, :time_share],
        mixed_sum[qkv_share : qkv_share + out_share],
        vec_sum[4],
        vec_sum[2],
        vec_sum[3],
        up_sum[:unit_share].T,
        up_bias,
        down_sum[:unit_share],
        vec_sum[5],
        tables[0],
        tables[1],
    )


def solution(mesh):
    rows = P(AXES, None)
    cols = P(None, AXES)
    vector = P(AXES)
    heads = P("fsdp", None)
    in_specs = (
        rows, vector, vector, vector, vector, vector, cols, cols, rows, vector, vector, vector,
        cols, vector, rows, vector, heads, heads, rows,
    )
    out_specs = (
        rows, rows, vector, vector, cols, cols, rows, vector, vector, vector, cols, vector, rows, vector,
        heads, heads,
    )
    return jax.shard_map(local, mesh=mesh, in_specs=in_specs, out_specs=out_specs, check_vma=False)
```

```python
import functools
import math

import jax
import jax.numpy as jnp
from jax import lax
from jax.experimental import pallas as pl
from jax.experimental.pallas import tpu as pltpu
from jax.sharding import PartitionSpec as P

HEADS = 16
GRID = 32
SMALL = 16
AXES = ("dp", "fsdp")
LANES = 128
PIECE = 48
BIG = -1e30
F32 = jnp.float32
BF16 = jnp.bfloat16
HIGHEST = lax.Precision.HIGHEST
MESH_ID = pl.DeviceIdType.MESH
VMEM_LIMIT = 62 * 1024 * 1024


BEGIN_ROWS = (32, 32, 32, 16, 16, 16)
BEGIN_ORDER = ((
    10, 0, 1, 40, 11, 30, 60, 2, 41, 12, 20, 42, 31, 61, 21, 13, 62, 3, 43, 32, 4, 50, 44, 63, 22, 51, 52, 33, 34,
    14, 64, 23, 53, 24, 54,
),)
ATTEND_ORDER = (
    (0,), (30,), (), (), (10, 1), (31,), (2,), (11, 32, 20), (), (), (21,), (12, 33, 3), (22,), (), (),
    (13, 23, 4), (14, 24, 34),
)
MLP_ORDER = (
    (10,), (), (11, 0), (12,), (1,), (2, 30, 13, 20), (31, 14, 3), (21, 4), (32,), (22, 33), (23,), (), (34, 24),
)
BACK_ORDER = (
    (0,), (30, 10, 20, 1), (), (11,), (2,), (21,), (), (12, 31, 3), (22,), (4,), (13,), (), (23, 32), (), (33, 14),
    (), (34, 24),
)
END_ORDER = (
    (0,), (), (20, 1), (10, 2), (21,), (30, 11, 22, 40), (12, 50, 31), (), (), (51, 32, 41, 23), (), (3,), (13, 42),
    (), (24, 52, 33), (43, 4), (53, 34, 44, 14, 54),
)
BACK_ORDER = (
    (0,), (1, 50), (51, 30), (31,), (), (2, 20), (21, 52, 10, 32), (3, 40), (41, 53), (), (22, 33, 54, 42), (11, 23),
    (43,), (12, 34), (4, 24, 13), (44,), (14,),
)
END_ORDER = (
    (20,), (0, 21, 10), (1, 50), (), (22, 11), (30, 2), (23,), (51, 3, 12),
    (52, 31, 40, 13, 60, 41, 53, 24, 4, 32, 61, 42, 33, 54, 43, 62, 63, 14, 34, 44, 64),
)
STAGES = 5


def rounds_order(count, places, extra=False):
    order = [[] for _ in range(places)]
    last = count + STAGES - 2
    for number in range(last + 1):
        for k in range(count):
            if 0 <= number - k < STAGES:
                order[number * (places - 1) // last].append(k * 10 + number - k)
    if extra:
        order[-1] += [count * 10 + number for number in range(STAGES)]
    return order


def dot_nn(a, b):
    return lax.dot_general(a, b, (((1,), (0,)), ((), ())), preferred_element_type=F32)


def dot_nt(a, b):
    return lax.dot_general(a, b, (((1,), (1,)), ((), ())), preferred_element_type=F32)


def dot_tn(a, b):
    return lax.dot_general(a, b, (((0,), (0,)), ((), ())), preferred_element_type=F32)


def params(**more):
    return pltpu.CompilerParams(vmem_limit_bytes=VMEM_LIMIT, **more)


def resident(shape):
    zeros = (0,) * len(shape)
    return pl.BlockSpec(shape, lambda *_: zeros, pipeline_mode=pl.Buffered(1))


def split_dp(dp):
    g2 = 1 if dp <= 16 else 4
    return dp // 4 // g2, g2


class Place:
    def __init__(self, dims):
        self.G1, self.G2 = dims
        dp, self.q = lax.axis_index("dp"), lax.axis_index("fsdp")
        self.c = dp % 2
        rest = dp // 2
        self.g2 = rest % self.G2
        rest = rest // self.G2
        self.p = rest % 2
        self.g1 = rest // 2
        c, p, q = self.c, self.p, self.q
        self.ap, self.aq = (1 - p) * (1 - c) + p * c, q * (1 - c) + (1 - q) * c
        self.bp, self.bq = p * (1 - c) + (1 - p) * c, (1 - q) * (1 - c) + q * c
        self.whole = (pl.ds(0, self.G1), pl.ds(0, self.G2))

    def device(self, g1, p, g2, c, q):
        return (((g1 * 2 + p) * self.G2 + g2) * 2 + c, q)

    def line(self):
        found = []
        for step in range(1, self.G1 * self.G2):
            found.append(((self.g1 + step // self.G2) % self.G1, (self.g2 + step % self.G2) % self.G2))
        return found

    def on_line(self, spot):
        return self.device(spot[0], self.p, spot[1], self.c, self.q)

    def first(self):
        return self.device(self.g1, self.ap, self.g2, self.c, self.aq)

    def second(self):
        return self.device(self.g1, self.bp, self.g2, self.c, self.bq)

    def sibling(self):
        return self.device(self.g1, self.p, self.g2, 1 - self.c, self.q)

    def barrier_all(self):
        semaphore = pltpu.get_barrier_semaphore()
        count = self.count()

        def body(i, carry):
            pl.semaphore_signal(semaphore, inc=1, device_id=self.other(i), device_id_type=MESH_ID)
            return carry

        lax.fori_loop(1, count, body, 0)
        pl.semaphore_wait(semaphore, count - 1)

    def count(self):
        return self.G1 * self.G2 * 8

    def index(self):
        return lax.axis_index("dp") * 2 + self.q

    def other(self, i):
        to = (self.index() + i) % self.count()
        return (to // 2, to % 2)

    def barrier(self):
        partners = [self.on_line(spot) for spot in self.line()] + [self.first(), self.second(), self.sibling()]
        semaphore = pltpu.get_barrier_semaphore()
        for partner in partners:
            pl.semaphore_signal(semaphore, inc=1, device_id=partner, device_id_type=MESH_ID)
        pl.semaphore_wait(semaphore, len(partners))


def wait_for(view, semaphore):
    pltpu.make_async_copy(view, view, semaphore).wait()


class Gather:
    def __init__(self, dims, pieces, sources, results, sems, own_sems):
        self.at = Place(dims)
        self.pieces, self.sources, self.results = pieces, sources, results
        self.sems, self.own_sems = sems, own_sems

    @staticmethod
    def scratch(dims, pieces):
        return [
            pltpu.SemaphoreType.DMA((len(pieces), 7 + dims[0] * dims[1], 2)),
            pltpu.SemaphoreType.DMA((len(pieces),)),
        ]

    def send(self, k, kind, source, target, to):
        pltpu.make_async_remote_copy(
            src_ref=source,
            dst_ref=target,
            send_sem=self.sems.at[k, kind, 0],
            recv_sem=self.sems.at[k, kind, 1],
            device_id=to,
            device_id_type=MESH_ID,
        ).start()

    def finish(self, k, kind, view):
        wait_for(view, self.sems.at[k, kind, 1])
        wait_for(view, self.sems.at[k, kind, 0])

    def stage(self, k, number):
        at = self.at
        array, start, count = self.pieces[k]
        rows = pl.ds(start, count)
        result = self.results[array]
        every, every2 = at.whole
        source = self.sources[array].at[rows]
        own = result.at[at.g1, at.p, at.g2, at.c, at.q, rows]

        def plane(p, q):
            return result.at[every, p, every2, at.c, q, rows]

        if number == 0:
            pltpu.make_async_copy(source, own, self.own_sems.at[k]).start()
            for i, spot in enumerate(at.line()):
                self.send(k, 8 + i, source, own, at.on_line(spot))
        if number == 1:
            pltpu.make_async_copy(source, own, self.own_sems.at[k]).wait()
            for i in range(len(at.line())):
                self.finish(k, 8 + i, own)
            mine = plane(at.p, at.q)
            self.send(k, 1, mine, mine, at.first())
            self.send(k, 3, mine, mine, at.sibling())
        if number == 2:
            mine, came = plane(at.p, at.q), plane(at.ap, at.aq)
            self.finish(k, 1, came)
            self.send(k, 2, mine, mine, at.second())
            self.send(k, 4, came, came, at.second())
            self.send(k, 5, came, came, at.sibling())
        if number == 3:
            for kind, came in ((2, plane(at.bp, at.bq)), (4, plane(1 - at.p, 1 - at.q))):
                self.finish(k, kind, came)
                self.send(k, 6 + kind // 4, came, came, at.sibling())
        if number == 4:
            for kind in (3, 5, 6, 7):
                self.finish(k, kind, plane(at.p, at.q))


class Scatter:
    def __init__(
        self, dims, pieces, shift, sources, results, held, from_core, from_second, from_first, from_line, sems
    ):
        self.at = Place(dims)
        self.shift = shift
        self.pieces, self.sources, self.results = pieces, sources, results
        self.held, self.from_core, self.from_second = held, from_core, from_second
        self.from_first, self.from_line, self.sems = from_first, from_line, sems

    @staticmethod
    def scratch(dims, pieces, width, in_place=False):
        G1, G2 = dims
        n = len(pieces)
        most = max(piece[2] for piece in pieces)
        return [
            pltpu.VMEM((8, LANES) if in_place else (n, G1, 2, G2, 2, most, width), BF16),
            pltpu.VMEM((n, G1, 2, G2, 2, most, width), BF16),
            pltpu.VMEM((n, 2, G1, G2, most, width), BF16),
            pltpu.VMEM((n, G1, G2, most, width), BF16),
            pltpu.VMEM((n, G1 * G2 - 1, most, width), BF16),
            pltpu.SemaphoreType.DMA((n, 5 + G1 * G2, 2)),
        ]

    def send(self, k, kind, source, target, to):
        pltpu.make_async_remote_copy(
            src_ref=source,
            dst_ref=target,
            send_sem=self.sems.at[k, kind, 0],
            recv_sem=self.sems.at[k, kind, 1],
            device_id=to,
            device_id_type=MESH_ID,
        ).start()

    def add(self, target, addend):
        at = self.at

        def body(i, carry):
            g1, g2 = i // at.G2, i % at.G2
            total = target[g1, g2].astype(F32) + addend[g1, g2].astype(F32)
            target[g1, g2] = total.astype(BF16)
            return carry

        lax.fori_loop(0, at.G1 * at.G2, body, 0)

    def stage(self, k, number):
        at = self.at
        array, start, count = self.pieces[k]
        rows = pl.ds(start, count)
        source = self.sources[array]
        every, every2 = at.whole
        both = pl.ds(0, 2)
        in_place = len(self.held.shape) == 2
        some = pl.ds(0, count)
        from_core = self.from_core.at[k, every, both, every2, both, some]
        from_second = [self.from_second.at[k, i, every, every2, some] for i in range(2)]
        from_first = self.from_first.at[k, every, every2, some]
        from_line = [self.from_line.at[k, i, some] for i in range(at.G1 * at.G2 - 1)]

        def plane(p, q):
            if in_place:
                return source.at[every, p, every2, at.c, q, rows]
            return self.held.at[k, every, p, every2, q, some]

        local_copy = lambda: pltpu.make_async_copy(
            source.at[every, both, every2, at.c, both, rows],
            self.held.at[k, every, both, every2, both, some],
            self.sems.at[k, 4, 0],
        )
        if number == 0:
            self.send(k, 0, source.at[every, both, every2, 1 - at.c, both, rows], from_core, at.sibling())
            if not in_place:
                local_copy().start()
        if number == 1:
            if not in_place:
                local_copy().wait()
            wait_for(from_core, self.sems.at[k, 0, 1])
            for p, q in ((at.bp, at.bq), (1 - at.p, 1 - at.q)):
                self.add(plane(p, q), from_core.at[every, p, every2, q])
            self.send(k, 1, plane(at.bp, at.bq), from_second[0], at.second())
            self.send(k, 2, plane(1 - at.p, 1 - at.q), from_second[1], at.second())
            for p, q in ((at.p, at.q), (at.ap, at.aq)):
                self.add(plane(p, q), from_core.at[every, p, every2, q])
        if number == 2:
            for kind in (1, 2):
                wait_for(from_second[kind - 1], self.sems.at[k, kind, 1])
            self.add(plane(at.ap, at.aq), from_second[1])
            self.send(k, 3, plane(at.ap, at.aq), from_first, at.first())
            self.add(plane(at.p, at.q), from_second[0])
        if number == 3:
            wait_for(from_first, self.sems.at[k, 3, 1])
            self.add(plane(at.p, at.q), from_first)
            mine = plane(at.p, at.q)
            for i, spot in enumerate(at.line()):
                self.send(k, 5 + i, mine.at[spot[0], spot[1]], from_line[i], at.on_line(spot))
        if number == 4:
            total = plane(at.p, at.q)[at.g1, at.g2].astype(F32)
            for i in range(at.G1 * at.G2 - 1):
                wait_for(from_line[i], self.sems.at[k, 5 + i, 1])
                total = total + from_line[i][...].astype(F32)
            self.results[array][pl.ds(start - self.shift, count)] = total
            wait_for(from_core, self.sems.at[k, 0, 0])
            for kind in (1, 2):
                wait_for(from_second[kind - 1], self.sems.at[k, kind, 0])
            wait_for(from_first, self.sems.at[k, 3, 0])
            for i in range(at.G1 * at.G2 - 1):
                wait_for(from_line[i], self.sems.at[k, 5 + i, 0])


def pieces_of(first, last):
    return [(array, start, PIECE) for start in range(first, last, PIECE) for array in range(2)]


def early_rows(rows):
    return max(PIECE, rows - PIECE)


def summed_rows(rows):
    return PIECE if rows > PIECE else 0


def cut(array, rows, sizes):
    if sum(sizes) != rows:
        sizes = (PIECE,) * (rows // PIECE)
    return [(array, sum(sizes[:i]), size) for i, size in enumerate(sizes)]


def order_for(order, pieces, places, extra=False):
    count = len(pieces) + extra
    if sum(len(place) for place in order) == count * STAGES:
        return order
    return rounds_order(len(pieces), places, extra)


def pad_rows(shard):
    rows = shard.shape[0]
    return jnp.pad(shard, ((0, -rows % PIECE), (0, 0)))


def spread_of(dims):
    return (dims[0], 2, dims[1], 2, 2)


def exchange(at, source, target, sems):
    me = at.index()

    def body(i, carry):
        to = (me + i) % at.count()
        pltpu.make_async_remote_copy(
            src_ref=source.at[to, pl.ds(0, 8)],
            dst_ref=target.at[me, pl.ds(0, 8)],
            send_sem=sems.at[0],
            recv_sem=sems.at[1],
            device_id=at.other(i),
            device_id_type=MESH_ID,
        ).start()
        return carry

    lax.fori_loop(1, at.count(), body, 0)


def exchanged(at, target, sems):
    view = target.at[pl.ds(0, at.count() - 1), pl.ds(0, 8)]
    wait_for(view, sems.at[1])
    wait_for(view, sems.at[0])


def begin_kernel(dims, pieces, order, shares, head_dim, mixed_shard, small_shard, time_weight, qkv_out, out_out, small_out,
                 time_out, mixed, small, time_all, time_got, sems, own_sems, time_sems):
    work = Gather(dims, pieces, (small_shard, mixed_shard), (small, mixed), sems, own_sems)
    at = work.at
    devices = at.count()
    width = mixed.shape[-1]
    at.barrier_all()
    for event in order:
        work.stage(*divmod(event, 10))
        if event == STAGES - 1:
            small_out[...] = small[...].reshape(small_out.shape)
            for start in range(0, devices, 32):
                span = pl.ds(start, 32)
                rows = small_out[span].reshape(32 * small_out.shape[1], width)
                time_all[span] = dot_nn(rows, time_weight[...]).reshape(32, small_out.shape[1], LANES)
            exchange(at, time_all, time_got, time_sems)
    exchanged(at, time_got, time_sems)
    time_got[at.index()] = time_all[at.index(), 0:8]
    time_out[...] = time_got[...]

    def rows_of(first, share, base):
        parts, left = [], head_dim
        while left:
            device, offset = divmod(first, share)
            count = min(left, share - offset)
            place = []
            for size in reversed(spread_of(dims)):
                device, digit = divmod(device, size)
                place.insert(0, digit)
            parts.append(mixed[(*place, slice(base + offset, base + offset + count))])
            first, left = first + count, left - count
        parts.append(jnp.zeros((LANES - head_dim, width), BF16))
        return jnp.concatenate(parts, axis=0)

    for head in range(HEADS):
        for kind in range(3):
            qkv_out[head, kind * LANES : (kind + 1) * LANES] = rows_of((kind * HEADS + head) * head_dim, shares[0], 0)
        out_out[head * LANES : (head + 1) * LANES] = rows_of(head * head_dim, shares[1], shares[0])


def begin(mixed_shard, small_shard, time_weight, dims, shares, head_dim):
    width = mixed_shard.shape[1]
    small_rows = small_shard.shape[0]
    devices = dims[0] * dims[1] * 8
    pieces = [(0, 0, small_rows)] + cut(1, mixed_shard.shape[0], BEGIN_ROWS)
    (order,) = order_for(BEGIN_ORDER, pieces, 1)
    anywhere = pl.BlockSpec(memory_space=pl.ANY)
    vmem = pl.BlockSpec(memory_space=pltpu.VMEM)
    return pl.pallas_call(
        functools.partial(begin_kernel, dims, pieces, order, shares, head_dim),
        in_specs=[anywhere, anywhere, vmem],
        out_specs=[vmem] * 4,
        out_shape=[
            jax.ShapeDtypeStruct((HEADS, 3 * LANES, width), BF16),
            jax.ShapeDtypeStruct((HEADS * LANES, width), BF16),
            jax.ShapeDtypeStruct((devices, small_rows, width), BF16),
            jax.ShapeDtypeStruct((devices, 8, LANES), F32),
        ],
        scratch_shapes=[
            pltpu.VMEM(spread_of(dims) + mixed_shard.shape, BF16),
            pltpu.VMEM(spread_of(dims) + small_shard.shape, BF16),
            pltpu.VMEM((devices, small_rows, LANES), F32),
            pltpu.VMEM((devices, 8, LANES), F32),
            *Gather.scratch(dims, pieces),
            pltpu.SemaphoreType.DMA((2,)),
        ],
        compiler_params=params(collective_id=1, has_side_effects=True),
        name="begin",
    )(mixed_shard, small_shard, time_weight)


def normalise(values):
    centre = values - jnp.mean(values, axis=-1, keepdims=True)
    inverse = lax.rsqrt(jnp.mean(centre * centre, axis=-1, keepdims=True) + 1e-06)
    return centre * inverse, inverse


def norm_back(values, gain, grad):
    unit, inverse = normalise(values)
    scaled = grad * gain
    inner = jnp.mean(scaled, axis=-1, keepdims=True) + unit * jnp.mean(scaled * unit, axis=-1, keepdims=True)
    return inverse * (scaled - inner), unit


def events(order, step, work, place):
    if order[place]:

        @pl.when(step == place)
        def _():
            for event in order[place]:
                work.stage(*divmod(event, 10))


def attend_kernel(factor, block, dims, pieces, order, tokens, gain, shift, weight, time_q, time_v, large, table, onehot,
                  mask_q, mask_k, up_shard, down_shard,
                  normed_out, q_out, k_out, v_out, o_out, p_out, up_out, down_out, keys, sems, own_sems):
    rows = tokens.shape[0]
    work = Gather(dims, pieces, (up_shard, down_shard), (up_out, down_out), sems, own_sems)
    step = pl.program_id(0)

    @pl.when(step == 0)
    def _():
        work.at.barrier()

    for place in range(HEADS):
        events(order, step, work, place)

    @pl.when(pl.program_id(0) == 0)
    def _():
        for start in range(0, rows, block):
            span = pl.ds(start, block)
            unit, _ = normalise(tokens[span].astype(F32))
            normed_out[span] = (unit * gain[...] + shift[...]).astype(BF16)

    per = rows // (SMALL * SMALL)
    slot = rows // per
    one = large[...] > 0.0
    for i in range(per):
        span = pl.ds(i * slot, slot)
        qkv = dot_nt(normed_out[span], weight[0])
        add_q = jnp.where(one, time_q[0, 0:1], time_q[0, i : i + 1])
        add_v = jnp.where(one, time_v[0, 0:1], time_v[0, i : i + 1])
        q_out[0, span] = (qkv[:, :LANES] + add_q).astype(BF16)
        k_out[0, span] = qkv[:, LANES : 2 * LANES].astype(BF16)
        v_out[0, span] = (qkv[:, 2 * LANES :] + add_v).astype(BF16)
    keys[:, :LANES] = k_out[0] + mask_k[...]
    keys[:, LANES:] = onehot[...]
    for start in range(0, rows, block):
        span = pl.ds(start, block)
        bias = dot_nn(onehot[span], table[0]).astype(BF16)
        query = jnp.concatenate([q_out[0, span] + mask_q[span], bias], axis=1)
        scores = dot_nt(query, keys[...])
        top = jnp.max(scores, axis=1, keepdims=True)
        weights = jnp.exp2((scores - top) * factor)
        total = jnp.sum(weights, axis=1, keepdims=True)
        low = (weights * (1.0 / total)).astype(BF16)
        p_out[0, span] = low
        o_out[span] = dot_nn(low, v_out[0]).astype(BF16)

    @pl.when(step == HEADS - 1)
    def _():
        for event in order[HEADS]:
            work.stage(*divmod(event, 10))


def attend(tokens, gain, shift, weight, times, large, table, onehot, mask_q, mask_k, factor, shards, dims):
    rows, width = tokens.shape
    block = min(256, rows)
    pieces = pieces_of(0, early_rows(shards[0].shape[0]))
    anywhere = pl.BlockSpec(memory_space=pl.ANY)
    per_head = lambda *shape: pl.BlockSpec((1,) + shape, lambda h: (h, 0, 0))
    head_rows = jax.ShapeDtypeStruct((HEADS, rows, LANES), BF16)
    return pl.pallas_call(
        functools.partial(attend_kernel, factor, block, dims, pieces, order_for(ATTEND_ORDER, pieces, HEADS + 1)),
        grid=(HEADS,),
        in_specs=[
            resident(tokens.shape),
            resident(gain.shape),
            resident(shift.shape),
            per_head(3 * LANES, width),
            pl.BlockSpec((1, 8, LANES), lambda h: (h, 0, 0)),
            pl.BlockSpec((1, 8, LANES), lambda h: (HEADS + h, 0, 0)),
            resident(large.shape),
            per_head(LANES, LANES),
            resident(onehot.shape),
            resident(mask_q.shape),
            resident(mask_k.shape),
            anywhere,
            anywhere,
        ],
        out_specs=[
            resident(tokens.shape),
            per_head(rows, LANES),
            per_head(rows, LANES),
            per_head(rows, LANES),
            pl.BlockSpec((rows, LANES), lambda h: (0, h)),
            per_head(rows, rows),
            anywhere,
            anywhere,
        ],
        out_shape=[
            jax.ShapeDtypeStruct(tokens.shape, BF16),
            head_rows,
            head_rows,
            head_rows,
            jax.ShapeDtypeStruct((rows, HEADS * LANES), BF16),
            jax.ShapeDtypeStruct((HEADS, rows, rows), BF16),
            *[jax.ShapeDtypeStruct(spread_of(dims) + s.shape, BF16) for s in shards],
        ],
        scratch_shapes=[pltpu.VMEM((rows, 2 * LANES), BF16), *Gather.scratch(dims, pieces)],
        compiler_params=params(collective_id=2, has_side_effects=True),
        name="attend",
    )(tokens, gain, shift, weight, times, times, large, table, onehot, mask_q, mask_k, *shards)


def attend_back_kernel(block, scale, dims, pieces, shift, order, normed, p, q, k, v, do, o, onehot, large, d_up, d_down,
                       dqkv_out, dw_out, sums_q, sums_v, pair_out, up_out, down_out,
                       keys, grads, dk_sum, dv_sum, *buffers):
    rows = normed.shape[0]
    work = Scatter(dims, pieces, shift, (d_up, d_down), (up_out, down_out), *buffers)
    step = pl.program_id(0)

    @pl.when(step == 0)
    def _():
        work.at.barrier()

    for place in range(HEADS):
        events(order, step, work, place)
    lane = lax.broadcasted_iota(jnp.int32, (rows, LANES), 1)
    head = 72
    delta = jnp.sum(do[...].astype(F32) * o[...].astype(F32), axis=1, keepdims=True)
    high = delta.astype(BF16).astype(F32)
    more = jnp.where(lane == head, -high, jnp.where(lane == head + 1, high - delta, 0.0))
    grads[...] = (do[...].astype(F32) + more).astype(BF16)
    values = v[0] + jnp.where((lane == head) | (lane == head + 1), 1.0, 0.0).astype(BF16)
    keys[:, :LANES] = k[0]
    keys[:, LANES:] = onehot[...]
    pair = jnp.zeros((LANES, LANES), F32)
    for start in range(0, rows, block):
        span = pl.ds(start, block)
        centred = dot_nt(grads[span], values)
        ds = (p[0, span].astype(F32) * centred).astype(BF16)
        both = dot_nn(ds, keys[...])
        dqkv_out[span, :LANES] = (both[:, :LANES] * scale).astype(BF16)
        pair = pair + lax.dot_general(
            onehot[span].astype(F32), both[:, LANES:], (((0,), (0,)), ((), ())),
            preferred_element_type=F32, precision=HIGHEST,
        )
        dk = dot_tn(ds, q[0, span])
        dv = dot_tn(p[0, span], do[span])
        if start == 0:
            dk_sum[...] = dk
            dv_sum[...] = dv
        else:
            dk_sum[...] += dk
            dv_sum[...] += dv
    dqkv_out[:, LANES : 2 * LANES] = (dk_sum[...] * scale).astype(BF16)
    dqkv_out[:, 2 * LANES :] = dv_sum[...].astype(BF16)
    pair_out[0] = pair
    slot = SMALL * SMALL
    one = large[...] > 0.0
    for target, base in ((sums_q, 0), (sums_v, 2 * LANES)):
        sums = []
        for start in range(0, rows, slot):
            part = dqkv_out[pl.ds(start, slot), base : base + LANES]
            sums.append(jnp.sum(part.astype(F32), axis=0, keepdims=True))
        total = functools.reduce(jnp.add, sums)
        sums = [jnp.where(one, total if i == 0 else jnp.zeros_like(total), part) for i, part in enumerate(sums)]
        sums.append(jnp.zeros((8 - len(sums), LANES), F32))
        target[0] = jnp.concatenate(sums, axis=0)
    dw_out[0] = dot_tn(dqkv_out[...], normed[...]).astype(BF16)

    @pl.when(step == HEADS - 1)
    def _():
        for event in order[HEADS]:
            work.stage(*divmod(event, 10))


def attend_back(normed, p, q, k, v, do, o, onehot, large, scale, parts, dims):
    rows, width = normed.shape
    block = min(256, rows)
    shift = summed_rows(parts[0].shape[5])
    pieces = pieces_of(shift, parts[0].shape[5])
    sum_shape = (parts[0].shape[5] - shift, width)
    anywhere = pl.BlockSpec(memory_space=pl.ANY)
    per_head = lambda *shape: pl.BlockSpec((1,) + shape, lambda h: (h, 0, 0))
    head_cols = pl.BlockSpec((rows, LANES), lambda h: (0, h))
    return pl.pallas_call(
        functools.partial(
            attend_back_kernel, block, scale, dims, pieces, shift, order_for(BACK_ORDER, pieces, HEADS + 1)
        ),
        grid=(HEADS,),
        in_specs=[
            resident(normed.shape),
            per_head(rows, rows),
            per_head(rows, LANES),
            per_head(rows, LANES),
            per_head(rows, LANES),
            head_cols,
            head_cols,
            resident(onehot.shape),
            resident(large.shape),
            anywhere,
            anywhere,
        ],
        out_specs=[
            pl.BlockSpec((rows, 3 * LANES), lambda h: (0, h)),
            per_head(3 * LANES, width),
            per_head(8, LANES),
            per_head(8, LANES),
            per_head(LANES, LANES),
            *[resident(sum_shape) for _ in parts],
        ],
        out_shape=[
            jax.ShapeDtypeStruct((rows, HEADS * 3 * LANES), BF16),
            jax.ShapeDtypeStruct((HEADS, 3 * LANES, width), BF16),
            jax.ShapeDtypeStruct((HEADS, 8, LANES), F32),
            jax.ShapeDtypeStruct((HEADS, 8, LANES), F32),
            jax.ShapeDtypeStruct((HEADS, LANES, LANES), F32),
            *[jax.ShapeDtypeStruct(sum_shape, F32) for _ in parts],
        ],
        scratch_shapes=[
            pltpu.VMEM((rows, 2 * LANES), BF16),
            pltpu.VMEM((rows, LANES), BF16),
            pltpu.VMEM((rows, LANES), F32),
            pltpu.VMEM((rows, LANES), F32),
            *Scatter.scratch(dims, pieces, width),
        ],
        compiler_params=params(collective_id=3, has_side_effects=True),
        name="attend_back",
    )(normed, p, q, k, v, do, o, onehot, large, *parts)


def project_kernel(tokens, o, weight, bias, gain, shift, hidden_out, normed_out):
    hidden = tokens[...].astype(F32) + (dot_nn(o[...], weight[...]) + bias[...])
    hidden_out[...] = hidden
    unit, _ = normalise(hidden)
    normed_out[...] = (unit * gain[...] + shift[...]).astype(BF16)


def project(tokens, o, weight, bias, gain, shift):
    rows, width = tokens.shape
    block = min(256, rows)
    by_rows = lambda cols: pl.BlockSpec((block, cols), lambda i: (i, 0))
    return pl.pallas_call(
        project_kernel,
        grid=(rows // block,),
        in_specs=[by_rows(width), by_rows(o.shape[1]), resident(weight.shape)] + [resident((1, width))] * 3,
        out_specs=[by_rows(width), by_rows(width)],
        out_shape=[jax.ShapeDtypeStruct(tokens.shape, F32), jax.ShapeDtypeStruct(tokens.shape, BF16)],
        compiler_params=params(),
        name="project",
    )(tokens, o, weight, bias, gain, shift)


def normal_parts(u):
    size = jnp.abs(u)
    bell = jnp.exp(-0.5 * u * u)
    t = 1.0 / (1.0 + (0.3275911 * math.sqrt(0.5)) * size)
    poly = t * (
        0.5 * 0.254829592
        + t * (0.5 * -0.284496736 + t * (0.5 * 1.421413741 + t * (0.5 * -1.453152027 + t * (0.5 * 1.061405429))))
    )
    tail = poly * bell
    return jnp.where(u >= 0.0, 1.0 - tail, tail), bell * (1.0 / math.sqrt(2.0 * math.pi))


BLOCK = (2, 2, 1, 2, 2)
BLOCK_DEVICES = 16


def block_of(ref, i, rows):
    whole = [pl.ds(0, size) for size in BLOCK]
    if len(ref.shape) == 7:
        return ref.at[(pl.ds(2 * i, 2), *whole[1:], rows)]
    return ref.at[(i, *whole, rows)]


def mlp_kernel(dims, block, blocks, gathers, sums, order, *refs):
    refs = list(refs)
    take = lambda count: [refs.pop(0) for _ in range(count)]
    normed, dy, bias, *early = take(5)
    shards = take(2) if gathers else None
    y_out, dn_out, dbias_out, *grads_out = take(5)
    late = take(2) if gathers else None
    totals = take(2) if sums else None
    weights, grads, act_all, du_all, weight_sems, grad_sems = take(6)
    if gathers:
        first_late = early[0].shape[-2] - PIECE
        shards = [shard.at[pl.ds(first_late, PIECE)] for shard in shards]
        gather = Gather(dims, gathers, shards, late, *take(2))
    if sums:
        scatter = Scatter(dims, sums, 0, grads_out, totals, *refs)
    rows = normed.shape[0]
    units = act_all.shape[1]
    step = pl.program_id(0)
    steps = pl.num_programs(0)
    late_step = steps - blocks if gathers else steps

    def copies(target_step, source):
        slot = target_step % 2
        i = target_step % blocks
        rows_of = pl.ds(pl.multiple_of(target_step // blocks * PIECE, PIECE), PIECE)
        return [
            pltpu.make_async_copy(block_of(source[array], i, rows_of), weights.at[slot, array], weight_sems.at[slot, array])
            for array in range(2)
        ]

    def late_copies(target_step):
        slot = target_step % 2
        i = target_step % blocks
        return [
            pltpu.make_async_copy(
                block_of(late[array], i, pl.ds(0, PIECE)), weights.at[slot, array], weight_sems.at[slot, array]
            )
            for array in range(2)
        ]

    def write_copies(target_step):
        slot = target_step % 2
        i = target_step % blocks
        rows_of = pl.ds(pl.multiple_of(target_step // blocks * PIECE, PIECE), PIECE)
        return [
            pltpu.make_async_copy(grads.at[slot, array], block_of(grads_out[array], i, rows_of), grad_sems.at[slot, array])
            for array in range(2)
        ]

    def happen(place, at_step):
        if gathers and order[place]:

            @pl.when(step == at_step)
            def _():
                for event in order[place]:
                    k, number = divmod(event, 10)
                    if k < len(gathers):
                        gather.stage(k, number)
                    else:
                        scatter.stage(k - len(gathers), number)

    @pl.when(step == 0)
    def _():
        if gathers:
            gather.at.barrier()
        for copy in copies(0, early):
            copy.start()
        y_out[...] = jnp.zeros_like(y_out)
        dn_out[...] = jnp.zeros_like(dn_out)

    for place in range(0, len(order) - 1, 2):
        happen(place, place // 2)
    for copy in copies(step, early):
        copy.wait()

    @pl.when(step + 1 < late_step)
    def _():
        for copy in copies(step + 1, early):
            copy.start()

    if gathers:

        @pl.when((step + 1 > late_step) & (step + 1 < steps))
        def _():
            for copy in late_copies(step + 1):
                copy.start()

    slot = step % 2
    up = weights[slot, 0].reshape(units, -1)
    down = weights[slot, 1].reshape(units, -1)
    total = jnp.zeros((1, units), F32)
    for start in range(0, rows, block):
        span = pl.ds(start, block)
        if start == rows // 2:

            @pl.when(step >= 1)
            def _():
                for copy in write_copies(step - 1):
                    copy.wait()

            for place in range(1, len(order) - 1, 2):
                happen(place, place // 2)
            if gathers:

                @pl.when(step + 1 == late_step)
                def _():
                    for copy in late_copies(step + 1):
                        copy.start()

        u = dot_nt(normed[span], up) + bias[0]
        phi, density = normal_parts(u)
        act = (u * phi).astype(BF16)
        slope = phi + u * density
        du = (slope * dot_nt(dy[span], down)).astype(BF16)
        total = total + jnp.sum(du.astype(F32), axis=0, keepdims=True)
        act_all[span] = act
        du_all[span] = du
        y_out[span] += dot_nn(act, down)
        dn_out[span] += dot_nn(du, up)
    dbias_out[0] = total
    grads[slot, 0] = dot_tn(du_all[...], normed[...]).astype(BF16).reshape(grads.shape[2:])
    grads[slot, 1] = dot_tn(act_all[...], dy[...]).astype(BF16).reshape(grads.shape[2:])
    for copy in write_copies(step):
        copy.start()

    @pl.when(step == steps - 1)
    def _():
        for copy in write_copies(step):
            copy.wait()

    happen(len(order) - 1, steps - 1)


def mlp(normed, dy, bias, weights, shards, dims):
    rows, width = normed.shape
    shard_rows = shards[0].shape[0]
    devices = dims[0] * dims[1] * 8
    blocks = devices // BLOCK_DEVICES
    steps = blocks * shard_rows // PIECE
    units = BLOCK_DEVICES * PIECE
    overlap = shard_rows > PIECE
    gathers = pieces_of(0, PIECE) if overlap else []
    sums = pieces_of(0, PIECE) if overlap else []
    anywhere = pl.BlockSpec(memory_space=pl.ANY)
    by_step = pl.BlockSpec((1, 1, units), lambda i: (i, 0, 0))
    spread = spread_of(dims)
    if dims[1] > 1:
        weights = [weight.reshape((blocks,) + BLOCK + (shard_rows, width)) for weight in weights]
    landing = jax.ShapeDtypeStruct(spread + (PIECE, width), BF16)
    total = jax.ShapeDtypeStruct((PIECE, width), F32)
    order = order_for(MLP_ORDER, gathers + sums, 2 * steps + 1)
    y, dn, dbias, d_up, d_down, *rest = pl.pallas_call(
        functools.partial(mlp_kernel, dims, min(256, rows), blocks, gathers, sums, order),
        grid=(steps,),
        in_specs=[resident(normed.shape), resident(dy.shape), by_step, anywhere, anywhere]
        + [anywhere, anywhere] * overlap,
        out_specs=[resident(normed.shape), resident(normed.shape), by_step, anywhere, anywhere]
        + ([anywhere] * 2 + [resident((PIECE, width))] * 2) * overlap,
        out_shape=[
            jax.ShapeDtypeStruct(normed.shape, F32),
            jax.ShapeDtypeStruct(normed.shape, F32),
            jax.ShapeDtypeStruct(bias.shape, F32),
            *[jax.ShapeDtypeStruct(weight.shape, BF16) for weight in weights],
            *([landing] * 2 + [total] * 2) * overlap,
        ],
        scratch_shapes=[
            pltpu.VMEM((2, 2) + BLOCK + (PIECE, width), BF16),
            pltpu.VMEM((2, 2) + BLOCK + (PIECE, width), BF16),
            pltpu.VMEM((rows, units), BF16),
            pltpu.VMEM((rows, units), BF16),
            pltpu.SemaphoreType.DMA((2, 2)),
            pltpu.SemaphoreType.DMA((2, 2)),
            *(Gather.scratch(dims, gathers) + Scatter.scratch(dims, sums, width) if overlap else []),
        ],
        compiler_params=params(collective_id=5, has_side_effects=True) if overlap else params(),
        name="mlp",
    )(normed, dy, bias, *weights, *(shards if overlap else []))
    whole = spread + (shard_rows, width)
    return y, dn, dbias, d_up.reshape(whole), d_down.reshape(whole), rest[2:]


def turn_kernel(hidden, y, bias, dn, dy, gain, weight, o, out, dh_out, do_out, dw_out, vec_out, dw_sum):
    first = pl.program_id(0) == 0
    last = pl.program_id(0) == pl.num_programs(0) - 1
    out[...] = (hidden[...] + (y[...] + bias[...])).astype(BF16)
    back, unit = norm_back(hidden[...], gain[...], dn[...])
    dyf = dy[...].astype(F32)
    dh = dyf + back
    dh_out[...] = dh
    da = dh.astype(BF16)
    do_out[...] = dot_nt(da, weight[...]).astype(BF16)
    dw = dot_tn(o[...], da)
    sums = jnp.concatenate(
        [
            jnp.sum(dn[...] * unit, axis=0, keepdims=True),
            jnp.sum(dn[...], axis=0, keepdims=True),
            jnp.sum(da.astype(F32), axis=0, keepdims=True),
            jnp.sum(dyf, axis=0, keepdims=True),
        ],
        axis=0,
    )

    @pl.when(first)
    def _():
        dw_sum[...] = dw
        vec_out[...] = sums

    @pl.when(jnp.logical_not(first))
    def _():
        dw_sum[...] += dw
        vec_out[...] += sums

    @pl.when(last)
    def _():
        dw_out[...] = dw_sum[...].astype(BF16)


def turn(hidden, y, bias, dn, dy, gain, weight, o):
    rows, width = hidden.shape
    block = min(256, rows)
    by_rows = lambda cols: pl.BlockSpec((block, cols), lambda i: (i, 0))
    wide = weight.shape[0]
    return pl.pallas_call(
        turn_kernel,
        grid=(rows // block,),
        in_specs=[
            by_rows(width),
            by_rows(width),
            resident((1, width)),
            by_rows(width),
            by_rows(width),
            resident((1, width)),
            resident(weight.shape),
            by_rows(wide),
        ],
        out_specs=[by_rows(width), by_rows(width), by_rows(wide), resident(weight.shape), resident((4, width))],
        out_shape=[
            jax.ShapeDtypeStruct(hidden.shape, BF16),
            jax.ShapeDtypeStruct(hidden.shape, F32),
            jax.ShapeDtypeStruct((rows, wide), BF16),
            jax.ShapeDtypeStruct(weight.shape, BF16),
            jax.ShapeDtypeStruct((4, width), F32),
        ],
        scratch_shapes=[pltpu.VMEM(weight.shape, F32)],
        compiler_params=params(),
        name="turn",
    )(hidden, y, bias, dn, dy, gain, weight, o)


class SumAll:
    def __init__(self, at, total, send, got, sems):
        self.at, self.total, self.send, self.got, self.sems = at, total, send, got, sems

    @staticmethod
    def scratch(dims, shape):
        copies = 2 + dims[0] * dims[1]
        return [
            pltpu.VMEM(shape, F32),
            pltpu.VMEM((4,) + shape, F32),
            pltpu.VMEM((copies,) + shape, F32),
            pltpu.SemaphoreType.DMA((copies, 2)),
        ]

    def start(self, stage, kind, to):
        pltpu.make_async_remote_copy(
            src_ref=self.send.at[stage],
            dst_ref=self.got.at[kind],
            send_sem=self.sems.at[kind, 0],
            recv_sem=self.sems.at[kind, 1],
            device_id=to,
            device_id_type=MESH_ID,
        ).start()

    def take(self, kind):
        wait_for(self.got.at[kind], self.sems.at[kind, 1])
        wait_for(self.got.at[kind], self.sems.at[kind, 0])

    def stage(self, number):
        at = self.at
        p_next = at.device(at.g1, 1 - at.p, at.g2, at.c, at.q)
        q_next = at.device(at.g1, at.p, at.g2, at.c, 1 - at.q)
        if 0 < number < 4:
            self.take(number - 1)
            self.total[...] += self.got[number - 1]
        if number < 4:
            self.send[number] = self.total[...]
        if number < 3:
            self.start(number, number, (at.sibling(), p_next, q_next)[number])
        if number == 3:
            line = at.G1 * at.G2
            mine = at.g1 * at.G2 + at.g2
            for i, spot in enumerate(at.line()):
                self.start(3, 3 + i, at.on_line(spot))
        if number == 4:
            line = at.G1 * at.G2
            mine = at.g1 * at.G2 + at.g2
            for i in range(line - 1):
                self.take(3 + i)
            spots = [spot[0] * at.G2 + spot[1] for spot in at.line()]
            parts = [self.got[3 + i] for i in range(line - 1)] + [self.send[3]]
            spots.append(mine)
            total = jnp.zeros_like(parts[0])
            for place in range(line):
                chosen = jnp.zeros_like(parts[0])
                for spot, part in zip(spots, parts):
                    chosen = jnp.where(spot == place, part, chosen)
                total = total + chosen
            self.total[...] = total


def end_kernel(dims, pieces, order, shares, head_dim, tokens, dqkv, weight, gain, dh, small, time_send, vec_in, dw, dw_out,
               out, vec_out, time_out, mixed_out, mixed, dw_buffer, dw_sems, time_got, time_sems,
               vec_total, vec_send, vec_got, vec_sems, *buffers):
    step = pl.program_id(0)
    steps = pl.num_programs(0)
    work = Scatter(dims, pieces, 0, (mixed,), (mixed_out,), *buffers)
    at = work.at
    sums = SumAll(at, vec_total, vec_send, vec_got, vec_sems)
    width = tokens.shape[1]
    fetches = HEADS + HEADS // 2
    pair = 2 * LANES

    def fetch(number):
        slot = number % 2
        if number < HEADS:
            return pltpu.make_async_copy(dw.at[number], dw_buffer.at[slot], dw_sems.at[slot])
        source = dw_out.at[pl.ds((number - HEADS) * pair, pair)]
        return pltpu.make_async_copy(source, dw_buffer.at[slot, pl.ds(0, pair)], dw_sems.at[slot])

    def place_of(device):
        place = []
        for size in reversed(spread_of(dims)):
            device, digit = divmod(device, size)
            place.insert(0, digit)
        return tuple(place)

    def put(first, share, base, value):
        done = 0
        while done < head_dim:
            device, offset = divmod(first + done, share)
            count = min(head_dim - done, share - offset)
            mixed[(*place_of(device), slice(base + offset, base + offset + count))] = value[done : done + count]
            done += count

    @pl.when(step == 0)
    def _():
        fetch(0).start()
        time_got[...] = jnp.zeros_like(time_got)
        at.barrier_all()
        exchange(at, time_send, time_got, time_sems)
        vec_total[...] = vec_in[...]
        for number in range(fetches):
            if number + 1 < fetches:
                fetch(number + 1).start()
            fetch(number).wait()
            if number < HEADS:
                for kind in range(3):
                    value = dw_buffer[number % 2, kind * LANES : kind * LANES + head_dim]
                    put((kind * HEADS + number) * head_dim, shares[0], 0, value)
            else:
                for i in range(2):
                    head = (number - HEADS) * 2 + i
                    value = dw_buffer[number % 2, i * LANES : i * LANES + head_dim]
                    put(head * head_dim, shares[1], shares[0], value)

    for place in range(len(order) - 1):
        events(order, step, work, place)

    dn = dot_nn(dqkv[...], weight[...])
    back, unit = norm_back(tokens[...].astype(F32), gain[...], dn)
    out[...] = (dh[...] + back).astype(BF16)
    vec_total[0:1] += jnp.sum(dn * unit, axis=0, keepdims=True)
    vec_total[1:2] += jnp.sum(dn, axis=0, keepdims=True)

    @pl.when(step == steps - 1)
    def _():
        for event in order[-1]:
            k, number = divmod(event, 10)
            if k == len(pieces):
                sums.stage(number)
            else:
                work.stage(k, number)
        exchanged(at, time_got, time_sems)
        time_got[at.index(), 0:8] = time_send[at.index()]
        vec_out[...] = vec_total[...]
        times = time_got[...].reshape(small.shape[0], LANES)
        high = times.astype(BF16)
        low = (times - high.astype(F32)).astype(BF16)
        time_out[...] = dot_tn(small[...], high) + dot_tn(small[...], low)


def end(tokens, dqkv, weight, gain, dh, small, time_send, vec_in, dw, dw_out, dims, shares, head_dim):
    rows, width = tokens.shape
    block = rows // 8
    by_rows = lambda cols: pl.BlockSpec((block, cols), lambda i: (i, 0))
    shard_rows = -(-sum(shares) // PIECE) * PIECE
    pieces = cut(0, shard_rows, BEGIN_ROWS)
    order = order_for(END_ORDER, pieces, rows // block + 1, True)
    anywhere = pl.BlockSpec(memory_space=pl.ANY)
    devices = time_send.shape[0]
    return pl.pallas_call(
        functools.partial(end_kernel, dims, pieces, order, shares, head_dim),
        grid=(rows // block,),
        in_specs=[
            by_rows(width),
            by_rows(dqkv.shape[1]),
            resident(weight.shape),
            resident((1, width)),
            by_rows(width),
            resident(small.shape),
            resident(time_send.shape),
            resident(vec_in.shape),
            anywhere,
            anywhere,
        ],
        out_specs=[
            by_rows(width),
            resident(vec_in.shape),
            resident((width, LANES)),
            resident((shard_rows, width)),
        ],
        out_shape=[
            jax.ShapeDtypeStruct(tokens.shape, BF16),
            jax.ShapeDtypeStruct(vec_in.shape, F32),
            jax.ShapeDtypeStruct((width, LANES), F32),
            jax.ShapeDtypeStruct((shard_rows, width), F32),
        ],
        scratch_shapes=[
            pltpu.VMEM(spread_of(dims) + (shard_rows, width), BF16),
            pltpu.VMEM((2,) + dw.shape[1:], BF16),
            pltpu.SemaphoreType.DMA((2,)),
            pltpu.VMEM((devices, small.shape[0] // devices, LANES), F32),
            pltpu.SemaphoreType.DMA((2,)),
            *SumAll.scratch(dims, vec_in.shape),
            *Scatter.scratch(dims, pieces, width, in_place=True),
        ],
        compiler_params=params(collective_id=4, has_side_effects=True),
        name="end",
    )(tokens, dqkv, weight, gain, dh, small, time_send, vec_in, dw, dw_out)


def time_embed(stamps, feat_width):
    half_width = feat_width // 2
    frequency = jnp.exp(-math.log(10000.0) * jnp.arange(half_width, dtype=F32) / half_width)
    angles = stamps.astype(F32)[:, None] * frequency[None, :]
    return jnp.concatenate([jnp.cos(angles), jnp.sin(angles)], axis=1)


def local(
    tokens,
    image_lengths,
    timesteps,
    patch_cells,
    norm1_gain,
    norm1_bias,
    qkv_weight,
    time_weight,
    out_weight,
    out_bias,
    norm2_gain,
    norm2_bias,
    fc1_weight,
    fc1_bias,
    fc2_weight,
    fc2_bias,
    row_table,
    col_table,
    cotangent,
):
    rows, width = tokens.shape
    head_dim = width // HEADS
    slot_rows = SMALL * SMALL
    per = image_lengths.shape[0]
    assert rows == GRID * GRID and per * slot_rows == rows
    fsdp = lax.axis_size("fsdp")
    devices = lax.axis_size("dp") * fsdp
    dims = split_dp(lax.axis_size("dp"))

    qkv_share, out_share = qkv_weight.shape[1], out_weight.shape[0]
    unit_share, time_share = fc1_weight.shape[1], time_weight.shape[1]
    units = devices * unit_share
    mixed_shard = pad_rows(jnp.concatenate([qkv_weight.T, out_weight], axis=0))
    embedded = time_embed(timesteps, width).astype(BF16)
    vectors = jnp.concatenate([norm1_gain, norm1_bias, out_bias, norm2_gain, norm2_bias, fc2_bias, fc1_bias])
    table_size = row_table.size
    to_row = lambda flat: jnp.pad(flat, (0, width - flat.shape[0]))[None]
    both_tables = jnp.concatenate([row_table.reshape(-1), col_table.reshape(-1)])
    small_shard = jnp.concatenate([embedded, to_row(vectors), to_row(both_tables)], axis=0)
    small_shard = jnp.pad(small_shard, ((0, -small_shard.shape[0] % 16), (0, 0)))
    time_padded = jnp.pad(time_weight, ((0, 0), (0, LANES - time_share)))
    shares = (qkv_share, out_share)
    qkv_full, out_full, small, times = begin(mixed_shard, small_shard, time_padded, dims, shares, head_dim)
    gathered = small[:, per]
    vector_share = norm1_gain.shape[0]
    vectors = gathered[:, : 6 * vector_share].reshape(devices, 6, vector_share).transpose(1, 0, 2)
    vectors = vectors.reshape(6, width).astype(F32)
    gain_one, shift_one, b_out, gain_two, shift_two, b_down = (vectors[i : i + 1] for i in range(6))
    b_up = gathered[:, 6 * vector_share : 6 * vector_share + unit_share].astype(F32)
    b_up = jnp.pad(b_up, ((0, 0), (0, -unit_share % PIECE)))
    b_up = b_up.reshape(devices // BLOCK_DEVICES, BLOCK_DEVICES, b_up.shape[1] // PIECE, PIECE)
    b_up = b_up.transpose(2, 0, 1, 3).reshape(-1, 1, BLOCK_DEVICES * PIECE)
    unit_shards = (pad_rows(fc1_weight.T), pad_rows(fc2_weight))
    tables = small[:fsdp, per + 1, : 2 * table_size].reshape(fsdp, 2, HEADS // fsdp, 2 * GRID - 1)
    tables = tables.transpose(1, 0, 2, 3).reshape(2 * HEADS, 2 * GRID - 1)

    lengths = image_lengths
    large = lengths[0] > slot_rows
    local_rows = jnp.arange(rows, dtype=jnp.int32)
    slot = jnp.where(large, 0, local_rows // slot_rows)
    spots = jnp.arange(per, dtype=jnp.int32)
    slot_pick = slot[:, None] == spots[None, :]
    slot_length = jnp.sum(jnp.where(slot_pick, lengths[None, :], 0), axis=1)
    valid = local_rows - slot * slot_rows < slot_length
    grid_index = jnp.arange(GRID, dtype=jnp.int32)
    row_hot = ((patch_cells // GRID)[:, None] == grid_index[None, :]).astype(BF16)
    col_hot = ((patch_cells % GRID)[:, None] == grid_index[None, :]).astype(BF16)
    onehot = jnp.concatenate([row_hot, col_hot, row_hot, col_hot], axis=1)
    lanes_left = ((0, 0), (head_dim, LANES - head_dim - per - 1))
    mask_q = jnp.concatenate(
        [jnp.where(slot_pick, 0.0, BIG), jnp.full((rows, 1), BIG, F32)], axis=1
    ).astype(BF16)
    mask_k = jnp.concatenate([slot_pick, jnp.logical_not(valid)[:, None]], axis=1).astype(BF16)
    mask_q, mask_k = jnp.pad(mask_q, lanes_left), jnp.pad(mask_k, lanes_left)

    offsets = grid_index[:, None] - grid_index[None, :] + GRID - 1
    diagonal = offsets[:, :, None] == jnp.arange(2 * GRID - 1, dtype=jnp.int32)[None, None, :]
    diagonal = diagonal.reshape(GRID * GRID, 2 * GRID - 1)
    toeplitz = dot_nt(tables, diagonal.astype(BF16)).reshape(2, HEADS, GRID, GRID) * math.sqrt(head_dim)
    high = lax.reduce_precision(toeplitz, 8, 7)
    low = toeplitz - high
    zero = jnp.zeros((HEADS, GRID, GRID), F32)
    table = jnp.concatenate(
        [
            jnp.concatenate([high[0], zero, low[0], zero], axis=2),
            jnp.concatenate([zero, high[1], zero, low[1]], axis=2),
            jnp.zeros((HEADS, 2 * GRID, LANES), F32),
        ],
        axis=1,
    ).astype(BF16)

    if time_share != head_dim:
        times = times[:, :per, :time_share].transpose(1, 0, 2).reshape(per, 2 * HEADS, head_dim)
        times = jnp.pad(times.transpose(1, 0, 2), ((0, 0), (0, 8 - per), (0, LANES - head_dim)))

    scale = 1.0 / math.sqrt(head_dim)
    large_lanes = jnp.broadcast_to(large.astype(F32), (1, LANES))
    normed_one, q, k, v, o, p, up, down = attend(
        tokens, gain_one, shift_one, qkv_full, times, large_lanes, table, onehot, mask_q, mask_k,
        scale * math.log2(math.e), unit_shards, dims,
    )
    hidden, normed_two = project(tokens, o, out_full, b_out, gain_two, shift_two)
    dy = jnp.where(valid[:, None], cotangent, jnp.zeros_like(cotangent))
    y, dn_two, db_up, d_up, d_down, first_sums = mlp(normed_two, dy, b_up, (up, down), unit_shards, dims)
    db_up = db_up.reshape(-1, devices // BLOCK_DEVICES, BLOCK_DEVICES, PIECE).transpose(1, 2, 0, 3)
    db_up = db_up.reshape(devices, -1)[:, :unit_share]
    layer_out, dh, do, d_out, vec_two = turn(hidden, y, b_down, dn_two, dy, gain_two, out_full, o)

    dqkv, d_qkv, sums_q, sums_v, pair, up_sum, down_sum = attend_back(
        normed_one, p, q, k, v, do, o, onehot, large_lanes, scale,
        (d_up, d_down), dims,
    )
    if first_sums:
        up_sum = jnp.concatenate([first_sums[0], up_sum], axis=0)
        down_sum = jnp.concatenate([first_sums[1], down_sum], axis=0)
    time_send = jnp.concatenate([sums_q, sums_v], axis=0)
    if time_share != head_dim:
        time_send = time_send[:, :per, :head_dim].transpose(1, 0, 2).reshape(per, devices, time_share)
        time_send = jnp.pad(time_send.transpose(1, 0, 2), ((0, 0), (0, 8 - per), (0, LANES - time_share)))
    pairs = jnp.concatenate([pair[:, :GRID, :GRID], pair[:, GRID : 2 * GRID, GRID : 2 * GRID]])
    tables = jnp.dot(pairs.reshape(2 * HEADS, GRID * GRID), diagonal.astype(F32), precision=HIGHEST)
    tables = tables.reshape(2, HEADS * (2 * GRID - 1))
    vec_in = jnp.concatenate(
        [
            jnp.zeros((2, width), F32),
            vec_two,
            db_up.reshape(units // width, width),
            jnp.pad(tables, ((0, 0), (0, width - tables.shape[1]))),
        ],
        axis=0,
    )
    vec_in = jnp.pad(vec_in, ((0, -vec_in.shape[0] % 8), (0, 0)))
    input_grad, vec_all, time_grad, mixed_sum = end(
        tokens, dqkv, qkv_full.reshape(HEADS * 3 * LANES, width), gain_one, dh,
        small.reshape(-1, width), time_send, vec_in, d_qkv, d_out, dims, shares, head_dim,
    )

    place = lax.axis_index("dp") * fsdp + lax.axis_index("fsdp")
    vec_sum = lax.dynamic_slice_in_dim(vec_all[:6], place * vector_share, vector_share, 1)
    up_bias = vec_all[6 : 6 + units // width].reshape(units)
    up_bias = lax.dynamic_slice_in_dim(up_bias, place * unit_share, unit_share)
    tables = vec_all[6 + units // width :][:2, : HEADS * (2 * GRID - 1)].reshape(2, fsdp, -1, 2 * GRID - 1)
    tables = lax.dynamic_index_in_dim(tables, lax.axis_index("fsdp"), 1, keepdims=False)

    return (
        layer_out,
        input_grad,
        vec_sum[0],
        vec_sum[1],
        mixed_sum[:qkv_share].T,
        time_grad[:, :time_share],
        mixed_sum[qkv_share : qkv_share + out_share],
        vec_sum[4],
        vec_sum[2],
        vec_sum[3],
        up_sum[:unit_share].T,
        up_bias,
        down_sum[:unit_share],
        vec_sum[5],
        tables[0],
        tables[1],
    )


def solution(mesh):
    rows = P(AXES, None)
    cols = P(None, AXES)
    vector = P(AXES)
    heads = P("fsdp", None)
    in_specs = (
        rows, vector, vector, vector, vector, vector, cols, cols, rows, vector, vector, vector,
        cols, vector, rows, vector, heads, heads, rows,
    )
    out_specs = (
        rows, rows, vector, vector, cols, cols, rows, vector, vector, vector, cols, vector, rows, vector,
        heads, heads,
    )
    return jax.shard_map(local, mesh=mesh, in_specs=in_specs, out_specs=out_specs, check_vma=False)
```

```python
import functools
import math

import jax
import jax.numpy as jnp
from jax import lax
from jax.experimental import pallas as pl
from jax.experimental.pallas import tpu as pltpu
from jax.sharding import PartitionSpec as P

HEADS = 16
GRID = 32
SMALL = 16
AXES = ("dp", "fsdp")
LANES = 128
PIECE = 48
BIG = -1e30
F32 = jnp.float32
BF16 = jnp.bfloat16
HIGHEST = lax.Precision.HIGHEST
MESH_ID = pl.DeviceIdType.MESH
VMEM_LIMIT = 62 * 1024 * 1024


BEGIN_ROWS = (32, 32, 32, 16, 16, 16)
BEGIN_ORDER = ((
    10, 0, 1, 40, 11, 30, 60, 2, 41, 12, 20, 42, 31, 61, 21, 13, 62, 3, 43, 32, 4, 50, 44, 63, 22, 51, 52, 33, 34,
    14, 64, 23, 53, 24, 54,
),)
ATTEND_ORDER = (
    (20,), (), (0,), (21,), (10, 1, 22), (), (11, 30, 2), (), (), (31,), (12,), (3,), (4, 32), (23,), (13,),
    (33,), (34, 24, 14),
)
MLP_ORDER = (
    (0,), (), (), (), (1, 10), (2,), (), (11, 3), (12,), (30, 20), (13, 21), (4, 14, 31), (22,), (23, 32),
    (33,), (), (34, 24),
)
BACK_ORDER = (
    (30, 10), (0,), (11,), (), (20,), (12,), (), (13, 31), (), (1,), (), (14,), (32,), (), (21, 33, 2), (), (),
    (), (22, 3), (), (23, 34), (), (), (4, 24), (),
)
END_ORDER = (
    (20,), (0, 21, 10), (1, 50), (), (22, 11), (30, 2), (23,), (51, 3, 12),
    (52, 31, 40, 13, 60, 41, 53, 24, 4, 32, 61, 42, 33, 54, 43, 62, 63, 14, 34, 44, 64),
)
STAGES = 5
PROJECTS = 4
TURNS = 8


def rounds_order(count, places, extra=False):
    order = [[] for _ in range(places)]
    last = count + STAGES - 2
    for number in range(last + 1):
        for k in range(count):
            if 0 <= number - k < STAGES:
                order[number * (places - 1) // last].append(k * 10 + number - k)
    if extra:
        order[-1] += [count * 10 + number for number in range(STAGES)]
    return order


def dot_nn(a, b):
    return lax.dot_general(a, b, (((1,), (0,)), ((), ())), preferred_element_type=F32)


def dot_nt(a, b):
    return lax.dot_general(a, b, (((1,), (1,)), ((), ())), preferred_element_type=F32)


def dot_tn(a, b):
    return lax.dot_general(a, b, (((0,), (0,)), ((), ())), preferred_element_type=F32)


def params(**more):
    return pltpu.CompilerParams(vmem_limit_bytes=VMEM_LIMIT, **more)


def resident(shape):
    zeros = (0,) * len(shape)
    return pl.BlockSpec(shape, lambda *_: zeros, pipeline_mode=pl.Buffered(1))


def split_dp(dp):
    g2 = 1 if dp <= 16 else 4
    return dp // 4 // g2, g2


class Place:
    def __init__(self, dims):
        self.G1, self.G2 = dims
        dp, self.q = lax.axis_index("dp"), lax.axis_index("fsdp")
        self.c = dp % 2
        rest = dp // 2
        self.g2 = rest % self.G2
        rest = rest // self.G2
        self.p = rest % 2
        self.g1 = rest // 2
        c, p, q = self.c, self.p, self.q
        self.ap, self.aq = (1 - p) * (1 - c) + p * c, q * (1 - c) + (1 - q) * c
        self.bp, self.bq = p * (1 - c) + (1 - p) * c, (1 - q) * (1 - c) + q * c
        self.whole = (pl.ds(0, self.G1), pl.ds(0, self.G2))

    def device(self, g1, p, g2, c, q):
        return (((g1 * 2 + p) * self.G2 + g2) * 2 + c, q)

    def line(self):
        found = []
        for step in range(1, self.G1 * self.G2):
            found.append(((self.g1 + step // self.G2) % self.G1, (self.g2 + step % self.G2) % self.G2))
        return found

    def on_line(self, spot):
        return self.device(spot[0], self.p, spot[1], self.c, self.q)

    def first(self):
        return self.device(self.g1, self.ap, self.g2, self.c, self.aq)

    def second(self):
        return self.device(self.g1, self.bp, self.g2, self.c, self.bq)

    def sibling(self):
        return self.device(self.g1, self.p, self.g2, 1 - self.c, self.q)

    def barrier_all(self):
        semaphore = pltpu.get_barrier_semaphore()
        count = self.count()

        def body(i, carry):
            pl.semaphore_signal(semaphore, inc=1, device_id=self.other(i), device_id_type=MESH_ID)
            return carry

        lax.fori_loop(1, count, body, 0)
        pl.semaphore_wait(semaphore, count - 1)

    def count(self):
        return self.G1 * self.G2 * 8

    def index(self):
        return lax.axis_index("dp") * 2 + self.q

    def other(self, i):
        to = (self.index() + i) % self.count()
        return (to // 2, to % 2)

    def barrier(self):
        partners = [self.on_line(spot) for spot in self.line()] + [self.first(), self.second(), self.sibling()]
        semaphore = pltpu.get_barrier_semaphore()
        for partner in partners:
            pl.semaphore_signal(semaphore, inc=1, device_id=partner, device_id_type=MESH_ID)
        pl.semaphore_wait(semaphore, len(partners))


def wait_for(view, semaphore):
    pltpu.make_async_copy(view, view, semaphore).wait()


class Gather:
    def __init__(self, dims, pieces, sources, results, sems, own_sems):
        self.at = Place(dims)
        self.pieces, self.sources, self.results = pieces, sources, results
        self.sems, self.own_sems = sems, own_sems

    @staticmethod
    def scratch(dims, pieces):
        return [
            pltpu.SemaphoreType.DMA((len(pieces), 7 + dims[0] * dims[1], 2)),
            pltpu.SemaphoreType.DMA((len(pieces),)),
        ]

    def send(self, k, kind, source, target, to):
        pltpu.make_async_remote_copy(
            src_ref=source,
            dst_ref=target,
            send_sem=self.sems.at[k, kind, 0],
            recv_sem=self.sems.at[k, kind, 1],
            device_id=to,
            device_id_type=MESH_ID,
        ).start()

    def finish(self, k, kind, view):
        wait_for(view, self.sems.at[k, kind, 1])
        wait_for(view, self.sems.at[k, kind, 0])

    def stage(self, k, number):
        at = self.at
        array, start, count = self.pieces[k]
        rows = pl.ds(start, count)
        result = self.results[array]
        every, every2 = at.whole
        source = self.sources[array].at[rows]
        own = result.at[at.g1, at.p, at.g2, at.c, at.q, rows]

        def plane(p, q):
            return result.at[every, p, every2, at.c, q, rows]

        if number == 0:
            pltpu.make_async_copy(source, own, self.own_sems.at[k]).start()
            for i, spot in enumerate(at.line()):
                self.send(k, 8 + i, source, own, at.on_line(spot))
        if number == 1:
            pltpu.make_async_copy(source, own, self.own_sems.at[k]).wait()
            for i in range(len(at.line())):
                self.finish(k, 8 + i, own)
            mine = plane(at.p, at.q)
            self.send(k, 1, mine, mine, at.first())
            self.send(k, 3, mine, mine, at.sibling())
        if number == 2:
            mine, came = plane(at.p, at.q), plane(at.ap, at.aq)
            self.finish(k, 1, came)
            self.send(k, 2, mine, mine, at.second())
            self.send(k, 4, came, came, at.second())
            self.send(k, 5, came, came, at.sibling())
        if number == 3:
            for kind, came in ((2, plane(at.bp, at.bq)), (4, plane(1 - at.p, 1 - at.q))):
                self.finish(k, kind, came)
                self.send(k, 6 + kind // 4, came, came, at.sibling())
        if number == 4:
            for kind in (3, 5, 6, 7):
                self.finish(k, kind, plane(at.p, at.q))


class Scatter:
    def __init__(
        self, dims, pieces, sources, put, held, from_core, from_second, from_first, from_line, sems
    ):
        self.at = Place(dims)
        self.pieces, self.sources, self.put = pieces, sources, put
        self.held, self.from_core, self.from_second = held, from_core, from_second
        self.from_first, self.from_line, self.sems = from_first, from_line, sems

    @staticmethod
    def scratch(dims, pieces, width, in_place=False):
        G1, G2 = dims
        n = len(pieces)
        most = max(piece[2] for piece in pieces)
        return [
            pltpu.VMEM((8, LANES) if in_place else (n, G1, 2, G2, 2, most, width), BF16),
            pltpu.VMEM((n, G1, 2, G2, 2, most, width), BF16),
            pltpu.VMEM((n, 2, G1, G2, most, width), BF16),
            pltpu.VMEM((n, G1, G2, most, width), BF16),
            pltpu.VMEM((n, G1 * G2 - 1, most, width), BF16),
            pltpu.SemaphoreType.DMA((n, 5 + G1 * G2, 2)),
        ]

    def send(self, k, kind, source, target, to):
        pltpu.make_async_remote_copy(
            src_ref=source,
            dst_ref=target,
            send_sem=self.sems.at[k, kind, 0],
            recv_sem=self.sems.at[k, kind, 1],
            device_id=to,
            device_id_type=MESH_ID,
        ).start()

    def add(self, target, addend):
        at = self.at

        def body(i, carry):
            g1, g2 = i // at.G2, i % at.G2
            total = target[g1, g2].astype(F32) + addend[g1, g2].astype(F32)
            target[g1, g2] = total.astype(BF16)
            return carry

        lax.fori_loop(0, at.G1 * at.G2, body, 0)

    def stage(self, k, number):
        at = self.at
        array, start, count = self.pieces[k]
        rows = pl.ds(start, count)
        source = self.sources[array]
        every, every2 = at.whole
        both = pl.ds(0, 2)
        in_place = len(self.held.shape) == 2
        some = pl.ds(0, count)
        from_core = self.from_core.at[k, every, both, every2, both, some]
        from_second = [self.from_second.at[k, i, every, every2, some] for i in range(2)]
        from_first = self.from_first.at[k, every, every2, some]
        from_line = [self.from_line.at[k, i, some] for i in range(at.G1 * at.G2 - 1)]

        def plane(p, q):
            if in_place:
                return source.at[every, p, every2, at.c, q, rows]
            return self.held.at[k, every, p, every2, q, some]

        local_copy = lambda: pltpu.make_async_copy(
            source.at[every, both, every2, at.c, both, rows],
            self.held.at[k, every, both, every2, both, some],
            self.sems.at[k, 4, 0],
        )
        if number == 0:
            self.send(k, 0, source.at[every, both, every2, 1 - at.c, both, rows], from_core, at.sibling())
            if not in_place:
                local_copy().start()
        if number == 1:
            if not in_place:
                local_copy().wait()
            wait_for(from_core, self.sems.at[k, 0, 1])
            for p, q in ((at.bp, at.bq), (1 - at.p, 1 - at.q)):
                self.add(plane(p, q), from_core.at[every, p, every2, q])
            self.send(k, 1, plane(at.bp, at.bq), from_second[0], at.second())
            self.send(k, 2, plane(1 - at.p, 1 - at.q), from_second[1], at.second())
            for p, q in ((at.p, at.q), (at.ap, at.aq)):
                self.add(plane(p, q), from_core.at[every, p, every2, q])
        if number == 2:
            for kind in (1, 2):
                wait_for(from_second[kind - 1], self.sems.at[k, kind, 1])
            self.add(plane(at.ap, at.aq), from_second[1])
            self.send(k, 3, plane(at.ap, at.aq), from_first, at.first())
            self.add(plane(at.p, at.q), from_second[0])
        if number == 3:
            wait_for(from_first, self.sems.at[k, 3, 1])
            self.add(plane(at.p, at.q), from_first)
            mine = plane(at.p, at.q)
            for i, spot in enumerate(at.line()):
                self.send(k, 5 + i, mine.at[spot[0], spot[1]], from_line[i], at.on_line(spot))
        if number == 4:
            total = plane(at.p, at.q)[at.g1, at.g2].astype(F32)
            for i in range(at.G1 * at.G2 - 1):
                wait_for(from_line[i], self.sems.at[k, 5 + i, 1])
                total = total + from_line[i][...].astype(F32)
            self.put(array, start, count, total)
            wait_for(from_core, self.sems.at[k, 0, 0])
            for kind in (1, 2):
                wait_for(from_second[kind - 1], self.sems.at[k, kind, 0])
            wait_for(from_first, self.sems.at[k, 3, 0])
            for i in range(at.G1 * at.G2 - 1):
                wait_for(from_line[i], self.sems.at[k, 5 + i, 0])


def pieces_of(first, last):
    return [(array, start, PIECE) for start in range(first, last, PIECE) for array in range(2)]


def early_rows(rows):
    return max(PIECE, rows - PIECE)


def summed_rows(rows):
    return PIECE if rows > PIECE else 0


def cut(array, rows, sizes):
    if sum(sizes) != rows:
        sizes = (PIECE,) * (rows // PIECE)
    return [(array, sum(sizes[:i]), size) for i, size in enumerate(sizes)]


def order_for(order, pieces, places, extra=False):
    count = len(pieces) + extra
    if len(order) == places and sum(len(place) for place in order) == count * STAGES:
        return order
    return rounds_order(len(pieces), places, extra)


def pad_rows(shard):
    rows = shard.shape[0]
    return jnp.pad(shard, ((0, -rows % PIECE), (0, 0)))


def spread_of(dims):
    return (dims[0], 2, dims[1], 2, 2)


def exchange(at, source, target, sems):
    me = at.index()

    def body(i, carry):
        to = (me + i) % at.count()
        pltpu.make_async_remote_copy(
            src_ref=source.at[to, pl.ds(0, 8)],
            dst_ref=target.at[me, pl.ds(0, 8)],
            send_sem=sems.at[0],
            recv_sem=sems.at[1],
            device_id=at.other(i),
            device_id_type=MESH_ID,
        ).start()
        return carry

    lax.fori_loop(1, at.count(), body, 0)


def exchanged(at, target, sems):
    view = target.at[pl.ds(0, at.count() - 1), pl.ds(0, 8)]
    wait_for(view, sems.at[1])
    wait_for(view, sems.at[0])


def begin_kernel(dims, pieces, order, shares, head_dim, mixed_shard, small_shard, time_weight, qkv_out, out_out, small_out,
                 time_out, mixed, small, time_all, time_got, sems, own_sems, time_sems):
    work = Gather(dims, pieces, (small_shard, mixed_shard), (small, mixed), sems, own_sems)
    at = work.at
    devices = at.count()
    width = mixed.shape[-1]
    at.barrier_all()
    for event in order:
        work.stage(*divmod(event, 10))
        if event == STAGES - 1:
            small_out[...] = small[...].reshape(small_out.shape)
            for start in range(0, devices, 32):
                span = pl.ds(start, 32)
                rows = small_out[span].reshape(32 * small_out.shape[1], width)
                time_all[span] = dot_nn(rows, time_weight[...]).reshape(32, small_out.shape[1], LANES)
            exchange(at, time_all, time_got, time_sems)
    exchanged(at, time_got, time_sems)
    time_got[at.index()] = time_all[at.index(), 0:8]
    time_out[...] = time_got[...]

    def rows_of(first, share, base):
        parts, left = [], head_dim
        while left:
            device, offset = divmod(first, share)
            count = min(left, share - offset)
            place = []
            for size in reversed(spread_of(dims)):
                device, digit = divmod(device, size)
                place.insert(0, digit)
            parts.append(mixed[(*place, slice(base + offset, base + offset + count))])
            first, left = first + count, left - count
        parts.append(jnp.zeros((LANES - head_dim, width), BF16))
        return jnp.concatenate(parts, axis=0)

    for head in range(HEADS):
        for kind in range(3):
            qkv_out[head, kind * LANES : (kind + 1) * LANES] = rows_of((kind * HEADS + head) * head_dim, shares[0], 0)
        out_out[head * LANES : (head + 1) * LANES] = rows_of(head * head_dim, shares[1], shares[0])


def begin(mixed_shard, small_shard, time_weight, dims, shares, head_dim):
    width = mixed_shard.shape[1]
    small_rows = small_shard.shape[0]
    devices = dims[0] * dims[1] * 8
    pieces = [(0, 0, small_rows)] + cut(1, mixed_shard.shape[0], BEGIN_ROWS)
    (order,) = order_for(BEGIN_ORDER, pieces, 1)
    anywhere = pl.BlockSpec(memory_space=pl.ANY)
    vmem = pl.BlockSpec(memory_space=pltpu.VMEM)
    return pl.pallas_call(
        functools.partial(begin_kernel, dims, pieces, order, shares, head_dim),
        in_specs=[anywhere, anywhere, vmem],
        out_specs=[vmem] * 4,
        out_shape=[
            jax.ShapeDtypeStruct((HEADS, 3 * LANES, width), BF16),
            jax.ShapeDtypeStruct((HEADS * LANES, width), BF16),
            jax.ShapeDtypeStruct((devices, small_rows, width), BF16),
            jax.ShapeDtypeStruct((devices, 8, LANES), F32),
        ],
        scratch_shapes=[
            pltpu.VMEM(spread_of(dims) + mixed_shard.shape, BF16),
            pltpu.VMEM(spread_of(dims) + small_shard.shape, BF16),
            pltpu.VMEM((devices, small_rows, LANES), F32),
            pltpu.VMEM((devices, 8, LANES), F32),
            *Gather.scratch(dims, pieces),
            pltpu.SemaphoreType.DMA((2,)),
        ],
        compiler_params=params(collective_id=1, has_side_effects=True),
        name="begin",
    )(mixed_shard, small_shard, time_weight)


def store_rows(results):
    def put(array, start, count, total):
        results[array][pl.ds(start, count)] = total

    return put


def scatter(part, dims, collective):
    shard = part.shape[5:]
    pieces = cut(0, shard[0], ())
    (order,) = rounds_order(len(pieces), 1)

    def kernel(source, result, *buffers):
        work = Scatter(dims, pieces, (source,), store_rows((result,)), *buffers)
        work.at.barrier()
        for event in order:
            work.stage(*divmod(event, 10))

    return pl.pallas_call(
        kernel,
        out_shape=jax.ShapeDtypeStruct(shard, F32),
        in_specs=[pl.BlockSpec(memory_space=pl.ANY)],
        out_specs=pl.BlockSpec(memory_space=pltpu.VMEM),
        scratch_shapes=Scatter.scratch(dims, pieces, shard[1]),
        compiler_params=params(collective_id=collective, has_side_effects=True),
    )(part)


def normalise(values):
    centre = values - jnp.mean(values, axis=-1, keepdims=True)
    inverse = lax.rsqrt(jnp.mean(centre * centre, axis=-1, keepdims=True) + 1e-06)
    return centre * inverse, inverse


def norm_back(values, gain, grad):
    unit, inverse = normalise(values)
    scaled = grad * gain
    inner = jnp.mean(scaled, axis=-1, keepdims=True) + unit * jnp.mean(scaled * unit, axis=-1, keepdims=True)
    return inverse * (scaled - inner), unit


def events(order, step, work, place):
    if order[place]:

        @pl.when(step == place)
        def _():
            for event in order[place]:
                work.stage(*divmod(event, 10))


def attend_kernel(factor, block, dims, pieces, order, tokens, vectors, weight, time_q, time_v, large, table, onehot,
                  mask_q, mask_k, up_shard, down_shard,
                  normed_out, q_out, k_out, v_out, o_out, p_out, up_out, down_out, keys, sems, own_sems):
    rows = tokens.shape[0]
    gain, shift = vectors.at[0:1], vectors.at[1:2]
    work = Gather(dims, pieces, (up_shard, down_shard), (up_out, down_out), sems, own_sems)
    step = pl.program_id(0)

    @pl.when(step == 0)
    def _():
        work.at.barrier()

    for place in range(HEADS):
        events(order, step, work, place)

    @pl.when(pl.program_id(0) == 0)
    def _():
        for start in range(0, rows, block):
            span = pl.ds(start, block)
            unit, _ = normalise(tokens[span].astype(F32))
            normed_out[span] = (unit * gain[...] + shift[...]).astype(BF16)

    per = rows // (SMALL * SMALL)
    slot = rows // per
    one = large[...] > 0.0
    for i in range(per):
        span = pl.ds(i * slot, slot)
        qkv = dot_nt(normed_out[span], weight[0])
        add_q = jnp.where(one, time_q[0, 0:1], time_q[0, i : i + 1])
        add_v = jnp.where(one, time_v[0, 0:1], time_v[0, i : i + 1])
        q_out[0, span] = (qkv[:, :LANES] + add_q).astype(BF16)
        k_out[0, span] = qkv[:, LANES : 2 * LANES].astype(BF16)
        v_out[0, span] = (qkv[:, 2 * LANES :] + add_v).astype(BF16)
    keys[:, :LANES] = k_out[0] + mask_k[...]
    keys[:, LANES:] = onehot[...]
    for start in range(0, rows, block):
        span = pl.ds(start, block)
        bias = dot_nn(onehot[span], table[0]).astype(BF16)
        query = jnp.concatenate([q_out[0, span] + mask_q[span], bias], axis=1)
        scores = dot_nt(query, keys[...])
        top = jnp.max(scores, axis=1, keepdims=True)
        weights = jnp.exp2((scores - top) * factor)
        total = jnp.sum(weights, axis=1, keepdims=True)
        low = (weights * (1.0 / total)).astype(BF16)
        p_out[0, span] = low
        o_out[span] = dot_nn(low, v_out[0]).astype(BF16)

    @pl.when(step == HEADS - 1)
    def _():
        for event in order[HEADS]:
            work.stage(*divmod(event, 10))


def attend(tokens, vectors, weight, times, large, table, onehot, mask_q, mask_k, factor, shards, dims):
    rows, width = tokens.shape
    block = min(512, rows)
    pieces = pieces_of(0, early_rows(shards[0].shape[0]))
    anywhere = pl.BlockSpec(memory_space=pl.ANY)
    per_head = lambda *shape: pl.BlockSpec((1,) + shape, lambda h: (h, 0, 0))
    head_rows = jax.ShapeDtypeStruct((HEADS, rows, LANES), BF16)
    return pl.pallas_call(
        functools.partial(attend_kernel, factor, block, dims, pieces, order_for(ATTEND_ORDER, pieces, HEADS + 1)),
        grid=(HEADS,),
        in_specs=[
            resident(tokens.shape),
            resident(vectors.shape),
            per_head(3 * LANES, width),
            pl.BlockSpec((1, 8, LANES), lambda h: (h, 0, 0)),
            pl.BlockSpec((1, 8, LANES), lambda h: (HEADS + h, 0, 0)),
            resident(large.shape),
            per_head(LANES, LANES),
            resident(onehot.shape),
            resident(mask_q.shape),
            resident(mask_k.shape),
            anywhere,
            anywhere,
        ],
        out_specs=[
            resident(tokens.shape),
            per_head(rows, LANES),
            per_head(rows, LANES),
            per_head(rows, LANES),
            pl.BlockSpec((rows, LANES), lambda h: (0, h)),
            per_head(rows, rows),
            anywhere,
            anywhere,
        ],
        out_shape=[
            jax.ShapeDtypeStruct(tokens.shape, BF16),
            head_rows,
            head_rows,
            head_rows,
            jax.ShapeDtypeStruct((rows, HEADS * LANES), BF16),
            jax.ShapeDtypeStruct((HEADS, rows, rows), BF16),
            *[jax.ShapeDtypeStruct(spread_of(dims) + s.shape, BF16) for s in shards],
        ],
        scratch_shapes=[pltpu.VMEM((rows, 2 * LANES), BF16), *Gather.scratch(dims, pieces)],
        compiler_params=params(collective_id=2, has_side_effects=True),
        name="attend",
    )(tokens, vectors, weight, times, times, large, table, onehot, mask_q, mask_k, *shards)


def turn_rows(hidden, y, dn, cotangent, mask, vectors, weight, span, out, dh_out, vec_out, da_all, do_all):
    out[...] = (hidden[...] + (y[...] + vectors[5:6])).astype(BF16)
    back, unit = norm_back(hidden[...], vectors[3:4], dn[...])
    dyf = only_valid(cotangent, mask).astype(F32)
    dh = dyf + back
    dh_out[...] = dh
    da = dh.astype(BF16)
    da_all[span] = da
    do = dot_nt(da, weight[...]).astype(BF16)
    for head in range(HEADS):
        do_all[head, span] = do[:, head * LANES : (head + 1) * LANES]
    vec_out[0:1] += jnp.sum(dn[...] * unit, axis=0, keepdims=True)
    vec_out[1:2] += jnp.sum(dn[...], axis=0, keepdims=True)
    vec_out[2:3] += jnp.sum(da.astype(F32), axis=0, keepdims=True)
    vec_out[3:4] += jnp.sum(dyf, axis=0, keepdims=True)


def attend_back_kernel(block, turns, scale, dims, pieces, ready, order, hidden, y, dn, cotangent, mask, vectors, weight,
                       normed, p, q, k, v, o, onehot, onehot_t, large, *refs):
    refs = list(refs)
    take = lambda count: [refs.pop(0) for _ in range(count)]
    parts = take(2 if pieces else 0)
    ready = take(ready)
    out, dh_out, vec_out, dqkv_out, dw_out, dwo_out, sums_out, pair_out = take(8)
    results = take(2 if pieces else 0)
    da_all, do_all, keys, grads, offsets, dk_sum, dv_sum = take(7)

    def put(array, start, count, total):
        if array == 0:
            results[0][:, start : start + count] = total.T
        else:
            results[1][start : start + count] = total

    work = Scatter(dims, pieces, parts, put, *refs) if pieces else None
    rows = normed.shape[0]
    step = pl.program_id(0)

    @pl.when(step == 0)
    def _():
        if pieces:
            work.at.barrier()
        vec_out[...] = jnp.zeros_like(vec_out)
        for array, part in enumerate(ready):
            put(array, 0, part.shape[0], part[...])

    for place in range(len(order) - 1):
        events(order, step, work, place)

    @pl.when(step < turns)
    def _():
        some = hidden.shape[0]
        span = pl.ds(pl.multiple_of(step * some, some), some)
        turn_rows(hidden, y, dn, cotangent, mask, vectors, weight, span, out, dh_out, vec_out, da_all, do_all)

    @pl.when(step >= turns)
    def _():
        do = do_all.at[step - turns]
        lane = lax.broadcasted_iota(jnp.int32, (rows, LANES), 1)
        head = 72
        delta = jnp.sum(do[...].astype(F32) * o[...].astype(F32), axis=1, keepdims=True)
        high = delta.astype(BF16).astype(F32)
        more = jnp.where(lane == head, -high, jnp.where(lane == head + 1, high - delta, 0.0))
        grads[...] = (do[...].astype(F32) + more).astype(BF16)
        values = v[0] + jnp.where((lane == head) | (lane == head + 1), 1.0, 0.0).astype(BF16)
        keys[:, :LANES] = k[0]
        keys[:, LANES:] = onehot[...]
        for start in range(0, rows, block):
            span = pl.ds(start, block)
            centred = dot_nt(grads[span], values)
            ds = (p[0, span].astype(F32) * centred).astype(BF16)
            both = dot_nn(ds, keys[...])
            dqkv_out[span, :LANES] = (both[:, :LANES] * scale).astype(BF16)
            by_place = both[:, LANES:]
            upper = by_place.astype(BF16)
            offsets[span, :LANES] = upper
            offsets[span, LANES:] = (by_place - upper.astype(F32)).astype(BF16)
            dk = dot_tn(q[0, span], ds)
            dv = dot_tn(do[span], p[0, span])
            if start == 0:
                dk_sum[...] = dk
                dv_sum[...] = dv
            else:
                dk_sum[...] += dk
                dv_sum[...] += dv
        dqkv_out[:, LANES : 2 * LANES] = (dk_sum[...] * scale).T.astype(BF16)
        dqkv_out[:, 2 * LANES :] = dv_sum[...].T.astype(BF16)
        pair = dot_nn(onehot_t[...], offsets[...])
        pair_out[0] = pair[:, :LANES] + pair[:, LANES:]
        slot = SMALL * SMALL
        one = large[...] > 0.0
        for kind, base in enumerate((0, 2 * LANES)):
            sums = []
            for start in range(0, rows, slot):
                part = dqkv_out[pl.ds(start, slot), base : base + LANES]
                sums.append(jnp.sum(part.astype(F32), axis=0, keepdims=True))
            total = functools.reduce(jnp.add, sums)
            sums = [jnp.where(one, total if i == 0 else jnp.zeros_like(total), part) for i, part in enumerate(sums)]
            sums.append(jnp.zeros((8 - len(sums), LANES), F32))
            sums_out[kind, 0] = jnp.concatenate(sums, axis=0)
        dw_out[0] = dot_tn(dqkv_out[...], normed[...]).astype(BF16)
        dwo_out[...] = dot_tn(o[...], da_all[...]).astype(BF16)

    if pieces:

        @pl.when(step == pl.num_programs(0) - 1)
        def _():
            for event in order[-1]:
                work.stage(*divmod(event, 10))


def attend_back(
    hidden, y, dn, cotangent, mask, vectors, weight, normed, p, q, k, v, o, onehot, onehot_t, large, scale, parts, ready, dims
):
    rows, width = normed.shape
    block = min(512, rows)
    turns = TURNS
    some = rows // turns
    pieces, sum_shapes = [], []
    if parts:
        shard_rows = parts[0].shape[5]
        pieces = pieces_of(summed_rows(shard_rows), shard_rows)
        sum_shapes = [(width, shard_rows), (shard_rows, width)]
    anywhere = pl.BlockSpec(memory_space=pl.ANY)
    head_of = lambda s: jnp.maximum(s - turns, 0)
    per_head = lambda *shape: pl.BlockSpec((1,) + shape, lambda s: (head_of(s), 0, 0))
    by_rows = pl.BlockSpec((some, width), lambda s: (jnp.minimum(s, turns - 1), 0))
    return pl.pallas_call(
        functools.partial(
            attend_back_kernel, block, turns, scale, dims, pieces, len(ready),
            order_for(BACK_ORDER, pieces, turns + HEADS + 1),
        ),
        grid=(turns + HEADS,),
        in_specs=[
            by_rows,
            by_rows,
            by_rows,
            by_rows,
            pl.BlockSpec((some, LANES), lambda s: (jnp.minimum(s, turns - 1), 0)),
            resident(vectors.shape),
            resident(weight.shape),
            resident(normed.shape),
            per_head(rows, rows),
            per_head(rows, LANES),
            per_head(rows, LANES),
            per_head(rows, LANES),
            pl.BlockSpec((rows, LANES), lambda s: (0, head_of(s))),
            resident(onehot.shape),
            resident(onehot_t.shape),
            resident(large.shape),
            *[anywhere for _ in parts],
            *[resident(part.shape) for part in ready],
        ],
        out_specs=[
            by_rows,
            by_rows,
            resident((4, width)),
            pl.BlockSpec((rows, 3 * LANES), lambda s: (0, head_of(s))),
            per_head(3 * LANES, width),
            pl.BlockSpec((LANES, width), lambda s: (head_of(s), 0)),
            pl.BlockSpec((2, 1, 8, LANES), lambda s: (0, head_of(s), 0, 0)),
            per_head(onehot_t.shape[0], LANES),
            *[resident(shape) for shape in sum_shapes],
        ],
        out_shape=[
            jax.ShapeDtypeStruct(hidden.shape, BF16),
            jax.ShapeDtypeStruct(hidden.shape, F32),
            jax.ShapeDtypeStruct((4, width), F32),
            jax.ShapeDtypeStruct((rows, HEADS * 3 * LANES), BF16),
            jax.ShapeDtypeStruct((HEADS, 3 * LANES, width), BF16),
            jax.ShapeDtypeStruct((HEADS * LANES, width), BF16),
            jax.ShapeDtypeStruct((2, HEADS, 8, LANES), F32),
            jax.ShapeDtypeStruct((HEADS, onehot_t.shape[0], LANES), F32),
            *[jax.ShapeDtypeStruct(shape, F32) for shape in sum_shapes],
        ],
        scratch_shapes=[
            pltpu.VMEM((rows, width), BF16),
            pltpu.VMEM((HEADS, rows, LANES), BF16),
            pltpu.VMEM((rows, 2 * LANES), BF16),
            pltpu.VMEM((rows, LANES), BF16),
            pltpu.VMEM((rows, 2 * LANES), BF16),
            pltpu.VMEM((LANES, rows), F32),
            pltpu.VMEM((LANES, rows), F32),
            *(Scatter.scratch(dims, pieces, width) if pieces else []),
        ],
        compiler_params=params(collective_id=3, has_side_effects=True) if pieces else params(),
        name="attend_back",
    )(hidden, y, dn, cotangent, mask, vectors, weight, normed, p, q, k, v, o, onehot, onehot_t, large, *parts, *ready)


def normal_parts(u):
    size = jnp.abs(u)
    bell = jnp.exp(-0.5 * u * u)
    t = 1.0 / (1.0 + (0.3275911 * math.sqrt(0.5)) * size)
    poly = t * (
        0.5 * 0.254829592
        + t * (0.5 * -0.284496736 + t * (0.5 * 1.421413741 + t * (0.5 * -1.453152027 + t * (0.5 * 1.061405429))))
    )
    tail = poly * bell
    return jnp.where(u >= 0.0, 1.0 - tail, tail), bell * (1.0 / math.sqrt(2.0 * math.pi))


BLOCK = (2, 2, 1, 2, 2)
BLOCK_DEVICES = 16


def block_of(ref, i, rows):
    whole = [pl.ds(0, size) for size in BLOCK]
    if len(ref.shape) == 7:
        return ref.at[(pl.ds(2 * i, 2), *whole[1:], rows)]
    return ref.at[(i, *whole, rows)]


def only_valid(cotangent, mask):
    lane = 72 + GRID * GRID // (SMALL * SMALL)
    return jnp.where(mask[:, lane : lane + 1].astype(F32) > 0.5, 0.0, cotangent[...].astype(F32)).astype(BF16)


def mlp_kernel(dims, block, projects, blocks, gathers, sums, order, *refs):
    refs = list(refs)
    take = lambda count: [refs.pop(0) for _ in range(count)]
    tokens, o, out_weight, vectors, cotangent, mask, bias, *early = take(9)
    out_bias, gain, offset = (vectors.at[i : i + 1] for i in (2, 3, 4))
    shards = take(2) if gathers else None
    hidden_out, y_out, dn_out, dbias_out, *grads_out = take(6)
    late = take(2) if gathers else None
    totals = take(2) if sums else None
    normed, dy, weights, grads, act_all, du_all, weight_sems, grad_sems = take(8)
    if gathers:
        first_late = early[0].shape[-2] - PIECE
        shards = [shard.at[pl.ds(first_late, PIECE)] for shard in shards]
        gather = Gather(dims, gathers, shards, late, *take(2))
    if sums:
        scatter = Scatter(dims, sums, grads_out, store_rows(totals), *refs)
    rows = normed.shape[0]
    units = act_all.shape[1]
    step = pl.program_id(0) - projects
    steps = pl.num_programs(0) - projects
    late_step = steps - blocks if gathers else steps

    def copies(target_step, source):
        slot = target_step % 2
        i = target_step % blocks
        rows_of = pl.ds(pl.multiple_of(target_step // blocks * PIECE, PIECE), PIECE)
        return [
            pltpu.make_async_copy(block_of(source[array], i, rows_of), weights.at[slot, array], weight_sems.at[slot, array])
            for array in range(2)
        ]

    def late_copies(target_step):
        slot = target_step % 2
        i = target_step % blocks
        return [
            pltpu.make_async_copy(
                block_of(late[array], i, pl.ds(0, PIECE)), weights.at[slot, array], weight_sems.at[slot, array]
            )
            for array in range(2)
        ]

    def write_copies(target_step):
        slot = target_step % 2
        i = target_step % blocks
        rows_of = pl.ds(pl.multiple_of(target_step // blocks * PIECE, PIECE), PIECE)
        return [
            pltpu.make_async_copy(grads.at[slot, array], block_of(grads_out[array], i, rows_of), grad_sems.at[slot, array])
            for array in range(2)
        ]

    def happen(place, at_step):
        if gathers and order[place]:

            @pl.when(step == at_step)
            def _():
                for event in order[place]:
                    k, number = divmod(event, 10)
                    if k < len(gathers):
                        gather.stage(k, number)
                    else:
                        scatter.stage(k - len(gathers), number)

    def mlp_step():
        for place in range(projects, len(order) - 1, 2):
            happen(place, (place - projects) // 2)
        for copy in copies(step, early):
            copy.wait()

        @pl.when(step + 1 < late_step)
        def _():
            for copy in copies(step + 1, early):
                copy.start()

        if gathers:

            @pl.when((step + 1 > late_step) & (step + 1 < steps))
            def _():
                for copy in late_copies(step + 1):
                    copy.start()

        slot = step % 2
        up = weights[slot, 0].reshape(units, -1)
        down = weights[slot, 1].reshape(units, -1)
        total = jnp.zeros((1, units), F32)
        for start in range(0, rows, block):
            span = pl.ds(start, block)
            if start == rows // 2:

                @pl.when(step >= 1)
                def _():
                    for copy in write_copies(step - 1):
                        copy.wait()

                for place in range(projects + 1, len(order) - 1, 2):
                    happen(place, (place - projects) // 2)
                if gathers:

                    @pl.when(step + 1 == late_step)
                    def _():
                        for copy in late_copies(step + 1):
                            copy.start()

            u = dot_nt(normed[span], up) + bias[0]
            phi, density = normal_parts(u)
            act = (u * phi).astype(BF16)
            slope = phi + u * density
            du = (slope * dot_nt(dy[span], down)).astype(BF16)
            total = total + jnp.sum(du.astype(F32), axis=0, keepdims=True)
            act_all[span] = act
            du_all[span] = du
            y_out[span] += dot_nn(act, down)
            dn_out[span] += dot_nn(du, up)
        dbias_out[0] = total
        grads[slot, 0] = dot_tn(du_all[...], normed[...]).astype(BF16).reshape(grads.shape[2:])
        grads[slot, 1] = dot_tn(act_all[...], dy[...]).astype(BF16).reshape(grads.shape[2:])
        for copy in write_copies(step):
            copy.start()

        @pl.when(step == steps - 1)
        def _():
            for copy in write_copies(step):
                copy.wait()

    @pl.when(step == -projects)
    def _():
        if gathers:
            gather.at.barrier()
        for copy in copies(0, early):
            copy.start()
        y_out[...] = jnp.zeros_like(y_out)
        dn_out[...] = jnp.zeros_like(dn_out)

    for place in range(projects):
        happen(place, place - projects)

    @pl.when(step < 0)
    def _():
        some = tokens.shape[0]
        span = pl.ds(pl.multiple_of(pl.program_id(0) * some, some), some)
        hidden = tokens[...].astype(F32) + (dot_nn(o[...], out_weight[...]) + out_bias[...])
        hidden_out[...] = hidden
        unit, _ = normalise(hidden)
        normed[span] = (unit * gain[...] + offset[...]).astype(BF16)
        dy[span] = only_valid(cotangent, mask)

    @pl.when(step >= 0)
    def _():
        mlp_step()

    happen(len(order) - 1, steps - 1)


def mlp(tokens, o, out_weight, vectors, cotangent, mask, bias, weights, shards, dims):
    rows, width = tokens.shape
    shard_rows = shards[0].shape[0]
    devices = dims[0] * dims[1] * 8
    blocks = devices // BLOCK_DEVICES
    steps = blocks * shard_rows // PIECE
    units = BLOCK_DEVICES * PIECE
    overlap = shard_rows > PIECE
    gathers = pieces_of(0, PIECE) if overlap else []
    sums = pieces_of(0, PIECE) if overlap else []
    anywhere = pl.BlockSpec(memory_space=pl.ANY)
    projects = PROJECTS
    some = rows // projects
    by_step = pl.BlockSpec((1, 1, units), lambda i: (jnp.maximum(i - projects, 0), 0, 0))
    by_rows = lambda cols: pl.BlockSpec((some, cols), lambda i: (jnp.minimum(i, projects - 1), 0))
    spread = spread_of(dims)
    if dims[1] > 1:
        weights = [weight.reshape((blocks,) + BLOCK + (shard_rows, width)) for weight in weights]
    landing = jax.ShapeDtypeStruct(spread + (PIECE, width), BF16)
    total = jax.ShapeDtypeStruct((PIECE, width), F32)
    full = jax.ShapeDtypeStruct(tokens.shape, F32)
    order = order_for(MLP_ORDER, gathers + sums, projects + 2 * steps + 1)
    hidden, y, dn, dbias, d_up, d_down, *rest = pl.pallas_call(
        functools.partial(mlp_kernel, dims, min(256, rows), projects, blocks, gathers, sums, order),
        grid=(projects + steps,),
        in_specs=[by_rows(width), by_rows(o.shape[1]), resident(out_weight.shape)]
        + [resident(vectors.shape), by_rows(width), by_rows(LANES), by_step, anywhere, anywhere]
        + [anywhere, anywhere] * overlap,
        out_specs=[by_rows(width), resident(tokens.shape), resident(tokens.shape), by_step, anywhere, anywhere]
        + ([anywhere] * 2 + [resident((PIECE, width))] * 2) * overlap,
        out_shape=[
            full,
            full,
            full,
            jax.ShapeDtypeStruct(bias.shape, F32),
            *[jax.ShapeDtypeStruct(weight.shape, BF16) for weight in weights],
            *([landing] * 2 + [total] * 2) * overlap,
        ],
        scratch_shapes=[
            pltpu.VMEM((rows, width), BF16),
            pltpu.VMEM((rows, width), BF16),
            pltpu.VMEM((2, 2) + BLOCK + (PIECE, width), BF16),
            pltpu.VMEM((2, 2) + BLOCK + (PIECE, width), BF16),
            pltpu.VMEM((rows, units), BF16),
            pltpu.VMEM((rows, units), BF16),
            pltpu.SemaphoreType.DMA((2, 2)),
            pltpu.SemaphoreType.DMA((2, 2)),
            *(Gather.scratch(dims, gathers) + Scatter.scratch(dims, sums, width) if overlap else []),
        ],
        compiler_params=params(collective_id=5, has_side_effects=True) if overlap else params(),
        name="mlp",
    )(tokens, o, out_weight, vectors, cotangent, mask, bias, *weights, *(shards if overlap else []))
    whole = spread + (shard_rows, width)
    return hidden, y, dn, dbias, d_up.reshape(whole), d_down.reshape(whole), rest[2:]


class SumAll:
    def __init__(self, at, total, send, got, sems):
        self.at, self.total, self.send, self.got, self.sems = at, total, send, got, sems

    @staticmethod
    def scratch(dims, shape):
        copies = 2 + dims[0] * dims[1]
        return [
            pltpu.VMEM(shape, F32),
            pltpu.VMEM((4,) + shape, F32),
            pltpu.VMEM((copies,) + shape, F32),
            pltpu.SemaphoreType.DMA((copies, 2)),
        ]

    def start(self, stage, kind, to):
        pltpu.make_async_remote_copy(
            src_ref=self.send.at[stage],
            dst_ref=self.got.at[kind],
            send_sem=self.sems.at[kind, 0],
            recv_sem=self.sems.at[kind, 1],
            device_id=to,
            device_id_type=MESH_ID,
        ).start()

    def take(self, kind):
        wait_for(self.got.at[kind], self.sems.at[kind, 1])
        wait_for(self.got.at[kind], self.sems.at[kind, 0])

    def stage(self, number):
        at = self.at
        p_next = at.device(at.g1, 1 - at.p, at.g2, at.c, at.q)
        q_next = at.device(at.g1, at.p, at.g2, at.c, 1 - at.q)
        if 0 < number < 4:
            self.take(number - 1)
            self.total[...] += self.got[number - 1]
        if number < 4:
            self.send[number] = self.total[...]
        if number < 3:
            self.start(number, number, (at.sibling(), p_next, q_next)[number])
        if number == 3:
            line = at.G1 * at.G2
            mine = at.g1 * at.G2 + at.g2
            for i, spot in enumerate(at.line()):
                self.start(3, 3 + i, at.on_line(spot))
        if number == 4:
            line = at.G1 * at.G2
            mine = at.g1 * at.G2 + at.g2
            for i in range(line - 1):
                self.take(3 + i)
            spots = [spot[0] * at.G2 + spot[1] for spot in at.line()]
            parts = [self.got[3 + i] for i in range(line - 1)] + [self.send[3]]
            spots.append(mine)
            total = jnp.zeros_like(parts[0])
            for place in range(line):
                chosen = jnp.zeros_like(parts[0])
                for spot, part in zip(spots, parts):
                    chosen = jnp.where(spot == place, part, chosen)
                total = total + chosen
            self.total[...] = total


def end_kernel(dims, pieces, order, shares, head_dim, tokens, dqkv, weight, vectors, dh, small, time_send, vec_in, dw, dw_out,
               out, vec_out, time_out, qkv_out, out_out, mixed, dw_buffer, dw_sems, time_got, time_sems,
               vec_total, vec_send, vec_got, vec_sems, *buffers):
    step = pl.program_id(0)
    steps = pl.num_programs(0)

    def put_sum(array, start, count, total):
        stop, cut_at = start + count, shares[0]
        if start < cut_at:
            qkv_out[:, start : min(stop, cut_at)] = total[: min(stop, cut_at) - start].T
        first, last = max(start, cut_at), min(stop, sum(shares))
        if first < last:
            out_out[first - cut_at : last - cut_at] = total[first - start : last - start]

    work = Scatter(dims, pieces, (mixed,), put_sum, *buffers)
    at = work.at
    sums = SumAll(at, vec_total, vec_send, vec_got, vec_sems)
    width = tokens.shape[1]
    fetches = HEADS + HEADS // 2
    pair = 2 * LANES

    def fetch(number):
        slot = number % 2
        if number < HEADS:
            return pltpu.make_async_copy(dw.at[number], dw_buffer.at[slot], dw_sems.at[slot])
        source = dw_out.at[pl.ds((number - HEADS) * pair, pair)]
        return pltpu.make_async_copy(source, dw_buffer.at[slot, pl.ds(0, pair)], dw_sems.at[slot])

    def place_of(device):
        place = []
        for size in reversed(spread_of(dims)):
            device, digit = divmod(device, size)
            place.insert(0, digit)
        return tuple(place)

    def put(first, share, base, value):
        done = 0
        while done < head_dim:
            device, offset = divmod(first + done, share)
            count = min(head_dim - done, share - offset)
            mixed[(*place_of(device), slice(base + offset, base + offset + count))] = value[done : done + count]
            done += count

    @pl.when(step == 0)
    def _():
        fetch(0).start()
        time_got[...] = jnp.zeros_like(time_got)
        at.barrier_all()
        exchange(at, time_send, time_got, time_sems)
        vec_total[...] = vec_in[...]
        for number in range(fetches):
            if number + 1 < fetches:
                fetch(number + 1).start()
            fetch(number).wait()
            if number < HEADS:
                for kind in range(3):
                    value = dw_buffer[number % 2, kind * LANES : kind * LANES + head_dim]
                    put((kind * HEADS + number) * head_dim, shares[0], 0, value)
            else:
                for i in range(2):
                    head = (number - HEADS) * 2 + i
                    value = dw_buffer[number % 2, i * LANES : i * LANES + head_dim]
                    put(head * head_dim, shares[1], shares[0], value)

    for place in range(len(order) - 1):
        events(order, step, work, place)

    dn = dot_nn(dqkv[...], weight[...])
    back, unit = norm_back(tokens[...].astype(F32), vectors[0:1], dn)
    out[...] = (dh[...] + back).astype(BF16)
    vec_total[0:1] += jnp.sum(dn * unit, axis=0, keepdims=True)
    vec_total[1:2] += jnp.sum(dn, axis=0, keepdims=True)

    @pl.when(step == steps - 1)
    def _():
        for event in order[-1]:
            k, number = divmod(event, 10)
            if k == len(pieces):
                sums.stage(number)
            else:
                work.stage(k, number)
        exchanged(at, time_got, time_sems)
        time_got[at.index(), 0:8] = time_send[at.index()]
        vec_out[...] = vec_total[...]
        times = time_got[...].reshape(small.shape[0], LANES)
        high = times.astype(BF16)
        low = (times - high.astype(F32)).astype(BF16)
        time_out[...] = dot_tn(small[...], high) + dot_tn(small[...], low)


def end(tokens, dqkv, weight, vectors, dh, small, time_send, vec_in, dw, dw_out, dims, shares, head_dim):
    rows, width = tokens.shape
    block = rows // 8
    by_rows = lambda cols: pl.BlockSpec((block, cols), lambda i: (i, 0))
    shard_rows = -(-sum(shares) // PIECE) * PIECE
    pieces = cut(0, shard_rows, BEGIN_ROWS)
    order = order_for(END_ORDER, pieces, rows // block + 1, True)
    anywhere = pl.BlockSpec(memory_space=pl.ANY)
    devices = time_send.shape[0]
    return pl.pallas_call(
        functools.partial(end_kernel, dims, pieces, order, shares, head_dim),
        grid=(rows // block,),
        in_specs=[
            by_rows(width),
            by_rows(dqkv.shape[1]),
            resident(weight.shape),
            resident(vectors.shape),
            by_rows(width),
            resident(small.shape),
            resident(time_send.shape),
            resident(vec_in.shape),
            anywhere,
            anywhere,
        ],
        out_specs=[
            by_rows(width),
            resident(vec_in.shape),
            resident((width, LANES)),
            resident((width, shares[0])),
            resident((shares[1], width)),
        ],
        out_shape=[
            jax.ShapeDtypeStruct(tokens.shape, BF16),
            jax.ShapeDtypeStruct(vec_in.shape, F32),
            jax.ShapeDtypeStruct((width, LANES), F32),
            jax.ShapeDtypeStruct((width, shares[0]), F32),
            jax.ShapeDtypeStruct((shares[1], width), F32),
        ],
        scratch_shapes=[
            pltpu.VMEM(spread_of(dims) + (shard_rows, width), BF16),
            pltpu.VMEM((2,) + dw.shape[1:], BF16),
            pltpu.SemaphoreType.DMA((2,)),
            pltpu.VMEM((devices, small.shape[0] // devices, LANES), F32),
            pltpu.SemaphoreType.DMA((2,)),
            *SumAll.scratch(dims, vec_in.shape),
            *Scatter.scratch(dims, pieces, width, in_place=True),
        ],
        compiler_params=params(collective_id=4, has_side_effects=True),
        name="end",
    )(tokens, dqkv, weight, vectors, dh, small, time_send, vec_in, dw, dw_out)


def time_embed(stamps, feat_width):
    half_width = feat_width // 2
    frequency = jnp.exp(-math.log(10000.0) * jnp.arange(half_width, dtype=F32) / half_width)
    angles = stamps.astype(F32)[:, None] * frequency[None, :]
    return jnp.concatenate([jnp.cos(angles), jnp.sin(angles)], axis=1)


def local(
    tokens,
    image_lengths,
    timesteps,
    patch_cells,
    norm1_gain,
    norm1_bias,
    qkv_weight,
    time_weight,
    out_weight,
    out_bias,
    norm2_gain,
    norm2_bias,
    fc1_weight,
    fc1_bias,
    fc2_weight,
    fc2_bias,
    row_table,
    col_table,
    cotangent,
):
    rows, width = tokens.shape
    head_dim = width // HEADS
    slot_rows = SMALL * SMALL
    per = image_lengths.shape[0]
    assert rows == GRID * GRID and per * slot_rows == rows
    fsdp = lax.axis_size("fsdp")
    devices = lax.axis_size("dp") * fsdp
    dims = split_dp(lax.axis_size("dp"))

    qkv_share, out_share = qkv_weight.shape[1], out_weight.shape[0]
    unit_share, time_share = fc1_weight.shape[1], time_weight.shape[1]
    units = devices * unit_share
    mixed_shard = pad_rows(jnp.concatenate([qkv_weight.T, out_weight], axis=0))
    embedded = time_embed(timesteps, width).astype(BF16)
    vectors = (norm1_gain, norm1_bias, out_bias, norm2_gain, norm2_bias, fc2_bias, fc1_bias)
    table_rows, table_width = row_table.shape
    small_rows, table_at = 16, 8
    put_at = lambda part, row, lane: jnp.pad(
        part, ((row, small_rows - row - part.shape[0]), (lane, width - lane - part.shape[1]))
    )
    spots_of = [put_at(embedded, 0, 0), put_at(row_table, table_at, 2 * LANES), put_at(col_table, table_at, 3 * LANES)]
    spots_of += [put_at(vector[None], per + i, 0) for i, vector in enumerate(vectors)]
    small_shard = functools.reduce(jnp.add, spots_of)
    time_padded = jnp.pad(time_weight, ((0, 0), (0, LANES - time_share)))
    shares = (qkv_share, out_share)
    qkv_full, out_full, small, times = begin(mixed_shard, small_shard, time_padded, dims, shares, head_dim)
    vector_share = norm1_gain.shape[0]
    vectors = small[:, per : per + 6, :vector_share].transpose(1, 0, 2).reshape(6, width).astype(F32)
    b_up = small[:, per + 6, :unit_share].astype(F32)
    b_up = jnp.pad(b_up, ((0, 0), (0, -unit_share % PIECE)))
    b_up = b_up.reshape(devices // BLOCK_DEVICES, BLOCK_DEVICES, b_up.shape[1] // PIECE, PIECE)
    b_up = b_up.transpose(2, 0, 1, 3).reshape(-1, 1, BLOCK_DEVICES * PIECE)
    unit_shards = (pad_rows(fc1_weight.T), pad_rows(fc2_weight))
    tables = small[:fsdp, table_at : table_at + table_rows, 2 * LANES : 4 * LANES].reshape(HEADS, 2, LANES)
    tables = tables.transpose(1, 0, 2).reshape(2 * HEADS, LANES)[:, :table_width]

    lengths = image_lengths
    large = lengths[0] > slot_rows
    local_rows = jnp.arange(rows, dtype=jnp.int32)
    slot = jnp.where(large, 0, local_rows // slot_rows)
    spots = jnp.arange(per, dtype=jnp.int32)
    slot_pick = slot[:, None] == spots[None, :]
    slot_length = jnp.sum(jnp.where(slot_pick, lengths[None, :], 0), axis=1)
    valid = local_rows - slot * slot_rows < slot_length
    grid_index = jnp.arange(GRID, dtype=jnp.int32)
    row_hot = ((patch_cells // GRID)[:, None] == grid_index[None, :]).astype(BF16)
    col_hot = ((patch_cells % GRID)[:, None] == grid_index[None, :]).astype(BF16)
    onehot = jnp.concatenate([row_hot, col_hot, row_hot, col_hot], axis=1)
    both_index = jnp.concatenate([grid_index, grid_index])[:, None]
    both_cells = jnp.where(jnp.arange(2 * GRID)[:, None] < GRID, patch_cells // GRID, patch_cells % GRID)
    onehot_t = (both_cells == both_index).astype(BF16)
    lanes_left = ((0, 0), (head_dim, LANES - head_dim - per - 1))
    mask_q = jnp.concatenate(
        [jnp.where(slot_pick, 0.0, BIG), jnp.full((rows, 1), BIG, F32)], axis=1
    ).astype(BF16)
    mask_k = jnp.concatenate([slot_pick, jnp.logical_not(valid)[:, None]], axis=1).astype(BF16)
    mask_q, mask_k = jnp.pad(mask_q, lanes_left), jnp.pad(mask_k, lanes_left)

    offsets = grid_index[:, None] - grid_index[None, :] + GRID - 1
    diagonal = offsets[:, :, None] == jnp.arange(2 * GRID - 1, dtype=jnp.int32)[None, None, :]
    diagonal = diagonal.reshape(GRID * GRID, 2 * GRID - 1)
    toeplitz = dot_nt(tables, diagonal.astype(BF16)).reshape(2, HEADS, GRID, GRID) * math.sqrt(head_dim)
    high = lax.reduce_precision(toeplitz, 8, 7)
    low = toeplitz - high
    zero = jnp.zeros((HEADS, GRID, GRID), F32)
    table = jnp.concatenate(
        [
            jnp.concatenate([high[0], zero, low[0], zero], axis=2),
            jnp.concatenate([zero, high[1], zero, low[1]], axis=2),
            jnp.zeros((HEADS, 2 * GRID, LANES), F32),
        ],
        axis=1,
    ).astype(BF16)

    if time_share != head_dim:
        times = times[:, :per, :time_share].transpose(1, 0, 2).reshape(per, 2 * HEADS, head_dim)
        times = jnp.pad(times.transpose(1, 0, 2), ((0, 0), (0, 8 - per), (0, LANES - head_dim)))

    scale = 1.0 / math.sqrt(head_dim)
    large_lanes = jnp.broadcast_to(large.astype(F32), (1, LANES))
    normed_one, q, k, v, o, p, up, down = attend(
        tokens, vectors, qkv_full, times, large_lanes, table, onehot, mask_q, mask_k,
        scale * math.log2(math.e), unit_shards, dims,
    )
    hidden, y, dn_two, db_up, d_up, d_down, first_sums = mlp(
        tokens, o, out_full, vectors, cotangent, mask_k, b_up, (up, down), unit_shards, dims
    )
    db_up = db_up.reshape(-1, devices // BLOCK_DEVICES, BLOCK_DEVICES, PIECE).transpose(1, 2, 0, 3)
    db_up = db_up.reshape(devices, -1)[:, :unit_share]

    beside = dims[1] == 1
    layer_out, dh, vec_two, dqkv, d_qkv, d_out, slot_sums, pair, *unit_sums = attend_back(
        hidden, y, dn_two, cotangent, mask_k, vectors, out_full,
        normed_one, p, q, k, v, o, onehot, onehot_t, large_lanes, scale,
        (d_up, d_down) if beside else (), first_sums, dims,
    )
    if not beside:
        unit_sums = scatter(d_up, dims, 6).T, scatter(d_down, dims, 7)
    up_sum, down_sum = unit_sums
    time_send = slot_sums.reshape(2 * HEADS, 8, LANES)
    if time_share != head_dim:
        time_send = time_send[:, :per, :head_dim].transpose(1, 0, 2).reshape(per, devices, time_share)
        time_send = jnp.pad(time_send.transpose(1, 0, 2), ((0, 0), (0, 8 - per), (0, LANES - time_share)))
    pairs = jnp.concatenate([pair[:, :GRID, :GRID], pair[:, GRID : 2 * GRID, GRID : 2 * GRID]])
    tables = jnp.dot(pairs.reshape(2 * HEADS, GRID * GRID), diagonal.astype(F32), precision=HIGHEST)
    tables = tables.reshape(2, HEADS * (2 * GRID - 1))
    vec_in = jnp.concatenate(
        [
            jnp.zeros((2, width), F32),
            vec_two,
            db_up.reshape(units // width, width),
            jnp.pad(tables, ((0, 0), (0, width - tables.shape[1]))),
        ],
        axis=0,
    )
    vec_in = jnp.pad(vec_in, ((0, -vec_in.shape[0] % 8), (0, 0)))
    input_grad, vec_all, time_grad, qkv_sum, out_sum = end(
        tokens, dqkv, qkv_full.reshape(HEADS * 3 * LANES, width), vectors, dh,
        small.reshape(-1, width), time_send, vec_in, d_qkv, d_out, dims, shares, head_dim,
    )

    place = lax.axis_index("dp") * fsdp + lax.axis_index("fsdp")
    vec_sum = lax.dynamic_slice_in_dim(vec_all[:6], place * vector_share, vector_share, 1)
    up_bias = vec_all[6 : 6 + units // width].reshape(units)
    up_bias = lax.dynamic_slice_in_dim(up_bias, place * unit_share, unit_share)
    tables = vec_all[6 + units // width :][:2, : HEADS * (2 * GRID - 1)].reshape(2, fsdp, -1, 2 * GRID - 1)
    tables = lax.dynamic_index_in_dim(tables, lax.axis_index("fsdp"), 1, keepdims=False)

    return (
        layer_out,
        input_grad,
        vec_sum[0],
        vec_sum[1],
        qkv_sum,
        time_grad[:, :time_share],
        out_sum,
        vec_sum[4],
        vec_sum[2],
        vec_sum[3],
        up_sum[:, :unit_share],
        up_bias,
        down_sum[:unit_share],
        vec_sum[5],
        tables[0],
        tables[1],
    )


def solution(mesh):
    rows = P(AXES, None)
    cols = P(None, AXES)
    vector = P(AXES)
    heads = P("fsdp", None)
    in_specs = (
        rows, vector, vector, vector, vector, vector, cols, cols, rows, vector, vector, vector,
        cols, vector, rows, vector, heads, heads, rows,
    )
    out_specs = (
        rows, rows, vector, vector, cols, cols, rows, vector, vector, vector, cols, vector, rows, vector,
        heads, heads,
    )
    return jax.shard_map(local, mesh=mesh, in_specs=in_specs, out_specs=out_specs, check_vma=False)
```

```python
import functools
import math

import jax
import jax.numpy as jnp
from jax import lax
from jax.experimental import pallas as pl
from jax.experimental.pallas import tpu as pltpu
from jax.sharding import PartitionSpec as P

HEADS = 16
GRID = 32
SMALL = 16
AXES = ("dp", "fsdp")
LANES = 128
PIECE = 48
BIG = -1e30
F32 = jnp.float32
BF16 = jnp.bfloat16
HIGHEST = lax.Precision.HIGHEST
MESH_ID = pl.DeviceIdType.MESH
VMEM_LIMIT = 62 * 1024 * 1024


BEGIN_ROWS = (32, 32, 32, 16, 16, 16)
BEGIN_ORDER = ((
    10, 0, 1, 40, 11, 30, 60, 2, 41, 12, 20, 42, 31, 61, 21, 13, 62, 3, 43, 32, 4, 50, 44, 63, 22, 51, 52, 33, 34,
    14, 64, 23, 53, 24, 54,
),)
ATTEND_ORDER = (
    (20,), (), (0,), (21,), (10, 1, 22), (), (11, 30, 2), (), (), (31,), (12,), (3,), (4, 32), (23,), (13,),
    (33,), (34, 24, 14),
)
MLP_ORDER = (
    (0,), (), (), (), (1, 10), (2,), (), (11, 3), (12,), (30, 20), (13, 21), (4, 14, 31), (22,), (23, 32),
    (33,), (), (34, 24),
)
BACK_ORDER = (
    (30, 10), (0,), (11,), (), (20,), (12,), (), (13, 31), (), (1,), (), (14,), (32,), (), (21, 33, 2), (), (),
    (), (22, 3), (), (23, 34), (), (), (4, 24), (),
)
END_ORDER = (
    (20,), (0, 21, 10), (1, 50), (), (22, 11), (30, 2), (23,), (51, 3, 12),
    (52, 31, 40, 13, 60, 41, 53, 24, 4, 32, 61, 42, 33, 54, 43, 62, 63, 14, 34, 44, 64),
)
STAGES = 5
PROJECTS = 4
TURNS = 8


def rounds_order(count, places, extra=False):
    order = [[] for _ in range(places)]
    last = count + STAGES - 2
    for number in range(last + 1):
        for k in range(count):
            if 0 <= number - k < STAGES:
                order[number * (places - 1) // last].append(k * 10 + number - k)
    if extra:
        order[-1] += [count * 10 + number for number in range(STAGES)]
    return order


def dot_nn(a, b):
    return lax.dot_general(a, b, (((1,), (0,)), ((), ())), preferred_element_type=F32)


def dot_nt(a, b):
    return lax.dot_general(a, b, (((1,), (1,)), ((), ())), preferred_element_type=F32)


def dot_tn(a, b):
    return lax.dot_general(a, b, (((0,), (0,)), ((), ())), preferred_element_type=F32)


def params(**more):
    return pltpu.CompilerParams(vmem_limit_bytes=VMEM_LIMIT, **more)


def resident(shape):
    zeros = (0,) * len(shape)
    return pl.BlockSpec(shape, lambda *_: zeros, pipeline_mode=pl.Buffered(1))


def split_dp(dp):
    g2 = 1 if dp <= 16 else 4
    return dp // 4 // g2, g2


class Place:
    def __init__(self, dims):
        self.G1, self.G2 = dims
        dp, self.q = lax.axis_index("dp"), lax.axis_index("fsdp")
        self.c = dp % 2
        rest = dp // 2
        self.g2 = rest % self.G2
        rest = rest // self.G2
        self.p = rest % 2
        self.g1 = rest // 2
        c, p, q = self.c, self.p, self.q
        self.ap, self.aq = (1 - p) * (1 - c) + p * c, q * (1 - c) + (1 - q) * c
        self.bp, self.bq = p * (1 - c) + (1 - p) * c, (1 - q) * (1 - c) + q * c
        self.whole = (pl.ds(0, self.G1), pl.ds(0, self.G2))

    def device(self, g1, p, g2, c, q):
        return (((g1 * 2 + p) * self.G2 + g2) * 2 + c, q)

    def line(self):
        found = []
        for step in range(1, self.G1 * self.G2):
            found.append(((self.g1 + step // self.G2) % self.G1, (self.g2 + step % self.G2) % self.G2))
        return found

    def on_line(self, spot):
        return self.device(spot[0], self.p, spot[1], self.c, self.q)

    def first(self):
        return self.device(self.g1, self.ap, self.g2, self.c, self.aq)

    def second(self):
        return self.device(self.g1, self.bp, self.g2, self.c, self.bq)

    def sibling(self):
        return self.device(self.g1, self.p, self.g2, 1 - self.c, self.q)

    def barrier_all(self):
        semaphore = pltpu.get_barrier_semaphore()
        count = self.count()

        def body(i, carry):
            pl.semaphore_signal(semaphore, inc=1, device_id=self.other(i), device_id_type=MESH_ID)
            return carry

        lax.fori_loop(1, count, body, 0)
        pl.semaphore_wait(semaphore, count - 1)

    def count(self):
        return self.G1 * self.G2 * 8

    def index(self):
        return lax.axis_index("dp") * 2 + self.q

    def other(self, i):
        to = (self.index() + i) % self.count()
        return (to // 2, to % 2)

    def barrier(self):
        partners = [self.on_line(spot) for spot in self.line()] + [self.first(), self.second(), self.sibling()]
        semaphore = pltpu.get_barrier_semaphore()
        for partner in partners:
            pl.semaphore_signal(semaphore, inc=1, device_id=partner, device_id_type=MESH_ID)
        pl.semaphore_wait(semaphore, len(partners))


def wait_for(view, semaphore):
    pltpu.make_async_copy(view, view, semaphore).wait()


class Gather:
    def __init__(self, dims, pieces, sources, results, sems, own_sems):
        self.at = Place(dims)
        self.pieces, self.sources, self.results = pieces, sources, results
        self.sems, self.own_sems = sems, own_sems

    @staticmethod
    def scratch(dims, pieces):
        return [
            pltpu.SemaphoreType.DMA((len(pieces), 7 + dims[0] * dims[1], 2)),
            pltpu.SemaphoreType.DMA((len(pieces),)),
        ]

    def send(self, k, kind, source, target, to):
        pltpu.make_async_remote_copy(
            src_ref=source,
            dst_ref=target,
            send_sem=self.sems.at[k, kind, 0],
            recv_sem=self.sems.at[k, kind, 1],
            device_id=to,
            device_id_type=MESH_ID,
        ).start()

    def finish(self, k, kind, view):
        wait_for(view, self.sems.at[k, kind, 1])
        wait_for(view, self.sems.at[k, kind, 0])

    def stage(self, k, number):
        at = self.at
        array, start, count = self.pieces[k]
        rows = pl.ds(start, count)
        result = self.results[array]
        every, every2 = at.whole
        source = self.sources[array].at[rows]
        own = result.at[at.g1, at.p, at.g2, at.c, at.q, rows]

        def plane(p, q):
            return result.at[every, p, every2, at.c, q, rows]

        if number == 0:
            pltpu.make_async_copy(source, own, self.own_sems.at[k]).start()
            for i, spot in enumerate(at.line()):
                self.send(k, 8 + i, source, own, at.on_line(spot))
        if number == 1:
            pltpu.make_async_copy(source, own, self.own_sems.at[k]).wait()
            for i in range(len(at.line())):
                self.finish(k, 8 + i, own)
            mine = plane(at.p, at.q)
            self.send(k, 1, mine, mine, at.first())
            self.send(k, 3, mine, mine, at.sibling())
        if number == 2:
            mine, came = plane(at.p, at.q), plane(at.ap, at.aq)
            self.finish(k, 1, came)
            self.send(k, 2, mine, mine, at.second())
            self.send(k, 4, came, came, at.second())
            self.send(k, 5, came, came, at.sibling())
        if number == 3:
            for kind, came in ((2, plane(at.bp, at.bq)), (4, plane(1 - at.p, 1 - at.q))):
                self.finish(k, kind, came)
                self.send(k, 6 + kind // 4, came, came, at.sibling())
        if number == 4:
            for kind in (3, 5, 6, 7):
                self.finish(k, kind, plane(at.p, at.q))


class Scatter:
    def __init__(
        self, dims, pieces, sources, put, held, from_core, from_second, from_first, from_line, sems
    ):
        self.at = Place(dims)
        self.pieces, self.sources, self.put = pieces, sources, put
        self.held, self.from_core, self.from_second = held, from_core, from_second
        self.from_first, self.from_line, self.sems = from_first, from_line, sems

    @staticmethod
    def scratch(dims, pieces, width, in_place=False):
        G1, G2 = dims
        n = len(pieces)
        most = max(piece[2] for piece in pieces)
        return [
            pltpu.VMEM((8, LANES) if in_place else (n, G1, 2, G2, 2, most, width), BF16),
            pltpu.VMEM((n, G1, 2, G2, 2, most, width), BF16),
            pltpu.VMEM((n, 2, G1, G2, most, width), BF16),
            pltpu.VMEM((n, G1, G2, most, width), BF16),
            pltpu.VMEM((n, G1 * G2 - 1, most, width), BF16),
            pltpu.SemaphoreType.DMA((n, 5 + G1 * G2, 2)),
        ]

    def send(self, k, kind, source, target, to):
        pltpu.make_async_remote_copy(
            src_ref=source,
            dst_ref=target,
            send_sem=self.sems.at[k, kind, 0],
            recv_sem=self.sems.at[k, kind, 1],
            device_id=to,
            device_id_type=MESH_ID,
        ).start()

    def add(self, target, addend):
        at = self.at

        def body(i, carry):
            g1, g2 = i // at.G2, i % at.G2
            target[g1, g2] = target[g1, g2] + addend[g1, g2]
            return carry

        lax.fori_loop(0, at.G1 * at.G2, body, 0)

    def stage(self, k, number):
        at = self.at
        array, start, count = self.pieces[k]
        rows = pl.ds(start, count)
        source = self.sources[array]
        every, every2 = at.whole
        both = pl.ds(0, 2)
        in_place = len(self.held.shape) == 2
        some = pl.ds(0, count)
        from_core = self.from_core.at[k, every, both, every2, both, some]
        from_second = [self.from_second.at[k, i, every, every2, some] for i in range(2)]
        from_first = self.from_first.at[k, every, every2, some]
        from_line = [self.from_line.at[k, i, some] for i in range(at.G1 * at.G2 - 1)]

        def plane(p, q):
            if in_place:
                return source.at[every, p, every2, at.c, q, rows]
            return self.held.at[k, every, p, every2, q, some]

        local_copy = lambda: pltpu.make_async_copy(
            source.at[every, both, every2, at.c, both, rows],
            self.held.at[k, every, both, every2, both, some],
            self.sems.at[k, 4, 0],
        )
        if number == 0:
            self.send(k, 0, source.at[every, both, every2, 1 - at.c, both, rows], from_core, at.sibling())
            if not in_place:
                local_copy().start()
        if number == 1:
            if not in_place:
                local_copy().wait()
            wait_for(from_core, self.sems.at[k, 0, 1])
            for p, q in ((at.bp, at.bq), (1 - at.p, 1 - at.q)):
                self.add(plane(p, q), from_core.at[every, p, every2, q])
            self.send(k, 1, plane(at.bp, at.bq), from_second[0], at.second())
            self.send(k, 2, plane(1 - at.p, 1 - at.q), from_second[1], at.second())
            for p, q in ((at.p, at.q), (at.ap, at.aq)):
                self.add(plane(p, q), from_core.at[every, p, every2, q])
        if number == 2:
            for kind in (1, 2):
                wait_for(from_second[kind - 1], self.sems.at[k, kind, 1])
            self.add(plane(at.ap, at.aq), from_second[1])
            self.send(k, 3, plane(at.ap, at.aq), from_first, at.first())
            self.add(plane(at.p, at.q), from_second[0])
        if number == 3:
            wait_for(from_first, self.sems.at[k, 3, 1])
            self.add(plane(at.p, at.q), from_first)
            mine = plane(at.p, at.q)
            for i, spot in enumerate(at.line()):
                self.send(k, 5 + i, mine.at[spot[0], spot[1]], from_line[i], at.on_line(spot))
        if number == 4:
            total = plane(at.p, at.q)[at.g1, at.g2].astype(F32)
            for i in range(at.G1 * at.G2 - 1):
                wait_for(from_line[i], self.sems.at[k, 5 + i, 1])
                total = total + from_line[i][...].astype(F32)
            self.put(array, start, count, total)
            wait_for(from_core, self.sems.at[k, 0, 0])
            for kind in (1, 2):
                wait_for(from_second[kind - 1], self.sems.at[k, kind, 0])
            wait_for(from_first, self.sems.at[k, 3, 0])
            for i in range(at.G1 * at.G2 - 1):
                wait_for(from_line[i], self.sems.at[k, 5 + i, 0])


def pieces_of(first, last):
    return [(array, start, PIECE) for start in range(first, last, PIECE) for array in range(2)]


def early_rows(rows):
    return max(PIECE, rows - PIECE)


def summed_rows(rows):
    return PIECE if rows > PIECE else 0


def cut(array, rows, sizes):
    if sum(sizes) != rows:
        sizes = (PIECE,) * (rows // PIECE)
    return [(array, sum(sizes[:i]), size) for i, size in enumerate(sizes)]


def order_for(order, pieces, places, extra=False):
    count = len(pieces) + extra
    if len(order) == places and sum(len(place) for place in order) == count * STAGES:
        return order
    return rounds_order(len(pieces), places, extra)


def pad_rows(shard):
    rows = shard.shape[0]
    return jnp.pad(shard, ((0, -rows % PIECE), (0, 0)))


def spread_of(dims):
    return (dims[0], 2, dims[1], 2, 2)


def exchange(at, source, target, sems):
    me = at.index()

    def body(i, carry):
        to = (me + i) % at.count()
        pltpu.make_async_remote_copy(
            src_ref=source.at[to, pl.ds(0, 8)],
            dst_ref=target.at[me, pl.ds(0, 8)],
            send_sem=sems.at[0],
            recv_sem=sems.at[1],
            device_id=at.other(i),
            device_id_type=MESH_ID,
        ).start()
        return carry

    lax.fori_loop(1, at.count(), body, 0)


def exchanged(at, target, sems):
    view = target.at[pl.ds(0, at.count() - 1), pl.ds(0, 8)]
    wait_for(view, sems.at[1])
    wait_for(view, sems.at[0])


def begin_kernel(dims, pieces, order, shares, head_dim, mixed_shard, small_shard, time_weight, qkv_out, out_out, small_out,
                 time_out, qkv, outs, mixed, small, time_all, time_got, sems, own_sems, time_sems, laid_sems):
    work = Gather(dims, pieces, (small_shard, mixed_shard), (small, mixed), sems, own_sems)
    at = work.at
    devices = at.count()
    width = mixed.shape[-1]
    at.barrier_all()
    for event in order:
        work.stage(*divmod(event, 10))
        if event == STAGES - 1:
            small_out[...] = small[...].reshape(small_out.shape)
            for start in range(0, devices, 32):
                span = pl.ds(start, 32)
                rows = small_out[span].reshape(32 * small_out.shape[1], width)
                time_all[span] = dot_nn(rows, time_weight[...]).reshape(32, small_out.shape[1], LANES)
            exchange(at, time_all, time_got, time_sems)
    exchanged(at, time_got, time_sems)
    time_got[at.index()] = time_all[at.index(), 0:8]
    time_out[...] = time_got[...]

    def rows_of(first, share, base):
        parts, left = [], head_dim
        while left:
            device, offset = divmod(first, share)
            count = min(left, share - offset)
            place = []
            for size in reversed(spread_of(dims)):
                device, digit = divmod(device, size)
                place.insert(0, digit)
            parts.append(mixed[(*place, slice(base + offset, base + offset + count))])
            first, left = first + count, left - count
        parts.append(jnp.zeros((LANES - head_dim, width), BF16))
        return jnp.concatenate(parts, axis=0)

    def laid(number):
        if number == HEADS:
            return pltpu.make_async_copy(outs, out_out, laid_sems.at[number])
        return pltpu.make_async_copy(qkv.at[number], qkv_out.at[number], laid_sems.at[number])

    for head in range(HEADS):
        for kind in range(3):
            qkv[head, kind * LANES : (kind + 1) * LANES] = rows_of((kind * HEADS + head) * head_dim, shares[0], 0)
        laid(head).start()
        outs[head * LANES : (head + 1) * LANES] = rows_of(head * head_dim, shares[1], shares[0])
    laid(HEADS).start()
    for number in range(HEADS + 1):
        laid(number).wait()


def begin(mixed_shard, small_shard, time_weight, dims, shares, head_dim):
    width = mixed_shard.shape[1]
    small_rows = small_shard.shape[0]
    devices = dims[0] * dims[1] * 8
    pieces = [(0, 0, small_rows)] + cut(1, mixed_shard.shape[0], BEGIN_ROWS)
    (order,) = order_for(BEGIN_ORDER, pieces, 1)
    anywhere = pl.BlockSpec(memory_space=pl.ANY)
    vmem = pl.BlockSpec(memory_space=pltpu.VMEM)
    return pl.pallas_call(
        functools.partial(begin_kernel, dims, pieces, order, shares, head_dim),
        in_specs=[anywhere, anywhere, vmem],
        out_specs=[anywhere, anywhere, vmem, vmem],
        out_shape=[
            jax.ShapeDtypeStruct((HEADS, 3 * LANES, width), BF16),
            jax.ShapeDtypeStruct((HEADS * LANES, width), BF16),
            jax.ShapeDtypeStruct((devices, small_rows, width), BF16),
            jax.ShapeDtypeStruct((devices, 8, LANES), F32),
        ],
        scratch_shapes=[
            pltpu.VMEM((HEADS, 3 * LANES, width), BF16),
            pltpu.VMEM((HEADS * LANES, width), BF16),
            pltpu.VMEM(spread_of(dims) + mixed_shard.shape, BF16),
            pltpu.VMEM(spread_of(dims) + small_shard.shape, BF16),
            pltpu.VMEM((devices, small_rows, LANES), F32),
            pltpu.VMEM((devices, 8, LANES), F32),
            *Gather.scratch(dims, pieces),
            pltpu.SemaphoreType.DMA((2,)),
            pltpu.SemaphoreType.DMA((HEADS + 1,)),
        ],
        compiler_params=params(collective_id=1, has_side_effects=True),
        name="begin",
    )(mixed_shard, small_shard, time_weight)


def store_rows(results):
    def put(array, start, count, total):
        results[array][pl.ds(start, count)] = total

    return put


def scatter(part, dims, collective):
    shard = part.shape[5:]
    pieces = cut(0, shard[0], ())
    (order,) = rounds_order(len(pieces), 1)

    def kernel(source, result, *buffers):
        work = Scatter(dims, pieces, (source,), store_rows((result,)), *buffers)
        work.at.barrier()
        for event in order:
            work.stage(*divmod(event, 10))

    return pl.pallas_call(
        kernel,
        out_shape=jax.ShapeDtypeStruct(shard, F32),
        in_specs=[pl.BlockSpec(memory_space=pl.ANY)],
        out_specs=pl.BlockSpec(memory_space=pltpu.VMEM),
        scratch_shapes=Scatter.scratch(dims, pieces, shard[1]),
        compiler_params=params(collective_id=collective, has_side_effects=True),
    )(part)


def normalise(values):
    centre = values - jnp.mean(values, axis=-1, keepdims=True)
    inverse = lax.rsqrt(jnp.mean(centre * centre, axis=-1, keepdims=True) + 1e-06)
    return centre * inverse, inverse


def norm_back(values, gain, grad):
    unit, inverse = normalise(values)
    scaled = grad * gain
    inner = jnp.mean(scaled, axis=-1, keepdims=True) + unit * jnp.mean(scaled * unit, axis=-1, keepdims=True)
    return inverse * (scaled - inner), unit


def events(order, step, work, place):
    if order[place]:

        @pl.when(step == place)
        def _():
            for event in order[place]:
                work.stage(*divmod(event, 10))


def attend_kernel(factor, block, dims, pieces, order, tokens, vectors, weight, time_q, time_v, large, table, onehot,
                  mask_q, mask_k, up_shard, down_shard,
                  normed_out, q_out, k_out, v_out, o_out, p_out, up_out, down_out, keys, sems, own_sems):
    rows = tokens.shape[0]
    gain, shift = vectors.at[0:1], vectors.at[1:2]
    work = Gather(dims, pieces, (up_shard, down_shard), (up_out, down_out), sems, own_sems)
    step = pl.program_id(0)

    @pl.when(step == 0)
    def _():
        work.at.barrier()

    for place in range(HEADS):
        events(order, step, work, place)

    @pl.when(pl.program_id(0) == 0)
    def _():
        for start in range(0, rows, block):
            span = pl.ds(start, block)
            unit, _ = normalise(tokens[span].astype(F32))
            normed_out[span] = (unit * gain[...] + shift[...]).astype(BF16)

    per = rows // (SMALL * SMALL)
    slot = rows // per
    one = large[...] > 0.0
    for i in range(per):
        span = pl.ds(i * slot, slot)
        qkv = dot_nt(normed_out[span], weight[0])
        add_q = jnp.where(one, time_q[0, 0:1], time_q[0, i : i + 1])
        add_v = jnp.where(one, time_v[0, 0:1], time_v[0, i : i + 1])
        q_out[0, span] = (qkv[:, :LANES] + add_q).astype(BF16)
        k_out[0, span] = qkv[:, LANES : 2 * LANES].astype(BF16)
        v_out[0, span] = (qkv[:, 2 * LANES :] + add_v).astype(BF16)
    keys[:, :LANES] = k_out[0] + mask_k[...]
    keys[:, LANES:] = onehot[...]
    for start in range(0, rows, block):
        span = pl.ds(start, block)
        bias = dot_nn(onehot[span], table[0]).astype(BF16)
        query = jnp.concatenate([q_out[0, span] + mask_q[span], bias], axis=1)
        scores = dot_nt(query, keys[...])
        top = jnp.max(scores, axis=1, keepdims=True)
        weights = jnp.exp2((scores - top) * factor)
        total = jnp.sum(weights, axis=1, keepdims=True)
        low = (weights * (1.0 / total)).astype(BF16)
        p_out[0, span] = low
        o_out[span] = dot_nn(low, v_out[0]).astype(BF16)

    @pl.when(step == HEADS - 1)
    def _():
        for event in order[HEADS]:
            work.stage(*divmod(event, 10))


def attend(tokens, vectors, weight, times, large, table, onehot, mask_q, mask_k, factor, shards, dims):
    rows, width = tokens.shape
    block = min(512, rows)
    pieces = pieces_of(0, early_rows(shards[0].shape[0]))
    anywhere = pl.BlockSpec(memory_space=pl.ANY)
    per_head = lambda *shape: pl.BlockSpec((1,) + shape, lambda h: (h, 0, 0))
    head_rows = jax.ShapeDtypeStruct((HEADS, rows, LANES), BF16)
    return pl.pallas_call(
        functools.partial(attend_kernel, factor, block, dims, pieces, order_for(ATTEND_ORDER, pieces, HEADS + 1)),
        grid=(HEADS,),
        in_specs=[
            resident(tokens.shape),
            resident(vectors.shape),
            per_head(3 * LANES, width),
            pl.BlockSpec((1, 8, LANES), lambda h: (h, 0, 0)),
            pl.BlockSpec((1, 8, LANES), lambda h: (HEADS + h, 0, 0)),
            resident(large.shape),
            per_head(LANES, LANES),
            resident(onehot.shape),
            resident(mask_q.shape),
            resident(mask_k.shape),
            anywhere,
            anywhere,
        ],
        out_specs=[
            resident(tokens.shape),
            per_head(rows, LANES),
            per_head(rows, LANES),
            per_head(rows, LANES),
            pl.BlockSpec((rows, LANES), lambda h: (0, h)),
            per_head(rows, rows),
            anywhere,
            anywhere,
        ],
        out_shape=[
            jax.ShapeDtypeStruct(tokens.shape, BF16),
            head_rows,
            head_rows,
            head_rows,
            jax.ShapeDtypeStruct((rows, HEADS * LANES), BF16),
            jax.ShapeDtypeStruct((HEADS, rows, rows), BF16),
            *[jax.ShapeDtypeStruct(spread_of(dims) + s.shape, BF16) for s in shards],
        ],
        scratch_shapes=[pltpu.VMEM((rows, 2 * LANES), BF16), *Gather.scratch(dims, pieces)],
        compiler_params=params(collective_id=2, has_side_effects=True),
        name="attend",
    )(tokens, vectors, weight, times, times, large, table, onehot, mask_q, mask_k, *shards)


def turn_rows(hidden, y, dn, cotangent, mask, vectors, weight, span, out, dh_out, vec_out, da_all, do_all):
    out[...] = (hidden[...] + (y[...] + vectors[5:6])).astype(BF16)
    back, unit = norm_back(hidden[...], vectors[3:4], dn[...])
    dyf = only_valid(cotangent, mask).astype(F32)
    dh = dyf + back
    dh_out[...] = dh
    da = dh.astype(BF16)
    da_all[span] = da
    do = dot_nt(da, weight[...]).astype(BF16)
    for head in range(HEADS):
        do_all[head, span] = do[:, head * LANES : (head + 1) * LANES]
    vec_out[0:1] += jnp.sum(dn[...] * unit, axis=0, keepdims=True)
    vec_out[1:2] += jnp.sum(dn[...], axis=0, keepdims=True)
    vec_out[2:3] += jnp.sum(da.astype(F32), axis=0, keepdims=True)
    vec_out[3:4] += jnp.sum(dyf, axis=0, keepdims=True)


def attend_back_kernel(block, turns, scale, dims, pieces, ready, order, hidden, y, dn, cotangent, mask, vectors, weight,
                       normed, p, q, k, v, o, onehot, onehot_t, large, *refs):
    refs = list(refs)
    take = lambda count: [refs.pop(0) for _ in range(count)]
    parts = take(2 if pieces else 0)
    ready = take(ready)
    out, dh_out, vec_out, dqkv_out, dw_out, dwo_out, sums_out, pair_out = take(8)
    results = take(2 if pieces else 0)
    da_all, do_all, keys, grads, offsets, dq_all, dk_sum, dv_sum = take(8)

    put = store_rows(results)
    work = Scatter(dims, pieces, parts, put, *refs) if pieces else None
    rows = normed.shape[0]
    step = pl.program_id(0)

    @pl.when(step == 0)
    def _():
        if pieces:
            work.at.barrier()
        vec_out[...] = jnp.zeros_like(vec_out)
        for array, part in enumerate(ready):
            put(array, 0, part.shape[0], part[...])

    for place in range(len(order) - 1):
        events(order, step, work, place)

    @pl.when(step < turns)
    def _():
        some = hidden.shape[0]
        span = pl.ds(pl.multiple_of(step * some, some), some)
        turn_rows(hidden, y, dn, cotangent, mask, vectors, weight, span, out, dh_out, vec_out, da_all, do_all)

    @pl.when(step >= turns)
    def _():
        do = do_all.at[step - turns]
        lane = lax.broadcasted_iota(jnp.int32, (rows, LANES), 1)
        head = 72
        delta = jnp.sum(do[...].astype(F32) * o[...].astype(F32), axis=1, keepdims=True)
        high = delta.astype(BF16).astype(F32)
        more = jnp.where(lane == head, -high, jnp.where(lane == head + 1, high - delta, 0.0))
        grads[...] = (do[...].astype(F32) + more).astype(BF16)
        values = v[0] + jnp.where((lane == head) | (lane == head + 1), 1.0, 0.0).astype(BF16)
        keys[:, :LANES] = k[0]
        keys[:, LANES:] = onehot[...]
        for start in range(0, rows, block):
            span = pl.ds(start, block)
            centred = dot_nt(grads[span], values)
            ds = (p[0, span].astype(F32) * centred).astype(BF16)
            both = dot_nn(ds, keys[...])
            dq_all[span] = both[:, :LANES] * scale
            by_place = both[:, LANES:]
            upper = by_place.astype(BF16)
            offsets[span, :LANES] = upper
            offsets[span, LANES:] = (by_place - upper.astype(F32)).astype(BF16)
            dk = dot_tn(q[0, span], ds)
            dv = dot_tn(do[span], p[0, span])
            if start == 0:
                dk_sum[...] = dk
                dv_sum[...] = dv
            else:
                dk_sum[...] += dk
                dv_sum[...] += dv
        dk_sum[...] = dk_sum[...] * scale
        dqkv_out[:, :LANES] = dq_all[...].astype(BF16)
        dqkv_out[:, LANES : 2 * LANES] = dk_sum[...].T.astype(BF16)
        dqkv_out[:, 2 * LANES :] = dv_sum[...].T.astype(BF16)
        turned = jnp.concatenate([dq_all[...].T[:head], dk_sum[:head], dv_sum[:head]], axis=0)
        pair = dot_nn(onehot_t[...], offsets[...])
        pair_out[0] = pair[:, :LANES] + pair[:, LANES:]
        slot = SMALL * SMALL
        one = large[...] > 0.0
        for kind, base in enumerate((0, 2 * LANES)):
            sums = []
            for start in range(0, rows, slot):
                part = dqkv_out[pl.ds(start, slot), base : base + LANES]
                sums.append(jnp.sum(part.astype(F32), axis=0, keepdims=True))
            total = functools.reduce(jnp.add, sums)
            sums = [jnp.where(one, total if i == 0 else jnp.zeros_like(total), part) for i, part in enumerate(sums)]
            sums.append(jnp.zeros((8 - len(sums), LANES), F32))
            sums_out[kind, 0] = jnp.concatenate(sums, axis=0)
        dw_out[0] = dot_nn(turned.astype(BF16), normed[...]).astype(BF16)
        dwo_out[...] = dot_tn(o[...], da_all[...]).astype(BF16)

    if pieces:

        @pl.when(step == pl.num_programs(0) - 1)
        def _():
            for event in order[-1]:
                work.stage(*divmod(event, 10))


def attend_back(
    hidden, y, dn, cotangent, mask, vectors, weight, normed, p, q, k, v, o, onehot, onehot_t, large, scale, parts, ready, dims
):
    rows, width = normed.shape
    head_dim = width // HEADS
    block = min(512, rows)
    turns = TURNS
    some = rows // turns
    pieces, sum_shapes = [], []
    if parts:
        shard_rows = parts[0].shape[5]
        pieces = pieces_of(summed_rows(shard_rows), shard_rows)
        sum_shapes = [(shard_rows, width)] * 2
    anywhere = pl.BlockSpec(memory_space=pl.ANY)
    head_of = lambda s: jnp.maximum(s - turns, 0)
    per_head = lambda *shape: pl.BlockSpec((1,) + shape, lambda s: (head_of(s), 0, 0))
    by_rows = pl.BlockSpec((some, width), lambda s: (jnp.minimum(s, turns - 1), 0))
    return pl.pallas_call(
        functools.partial(
            attend_back_kernel, block, turns, scale, dims, pieces, len(ready),
            order_for(BACK_ORDER, pieces, turns + HEADS + 1),
        ),
        grid=(turns + HEADS,),
        in_specs=[
            by_rows,
            by_rows,
            by_rows,
            by_rows,
            pl.BlockSpec((some, LANES), lambda s: (jnp.minimum(s, turns - 1), 0)),
            resident(vectors.shape),
            resident(weight.shape),
            resident(normed.shape),
            per_head(rows, rows),
            per_head(rows, LANES),
            per_head(rows, LANES),
            per_head(rows, LANES),
            pl.BlockSpec((rows, LANES), lambda s: (0, head_of(s))),
            resident(onehot.shape),
            resident(onehot_t.shape),
            resident(large.shape),
            *[anywhere for _ in parts],
            *[resident(part.shape) for part in ready],
        ],
        out_specs=[
            by_rows,
            by_rows,
            resident((4, width)),
            pl.BlockSpec((rows, 3 * LANES), lambda s: (0, head_of(s))),
            per_head(3 * head_dim, width),
            pl.BlockSpec((LANES, width), lambda s: (head_of(s), 0)),
            pl.BlockSpec((2, 1, 8, LANES), lambda s: (0, head_of(s), 0, 0)),
            per_head(onehot_t.shape[0], LANES),
            *[resident(shape) for shape in sum_shapes],
        ],
        out_shape=[
            jax.ShapeDtypeStruct(hidden.shape, BF16),
            jax.ShapeDtypeStruct(hidden.shape, F32),
            jax.ShapeDtypeStruct((4, width), F32),
            jax.ShapeDtypeStruct((rows, HEADS * 3 * LANES), BF16),
            jax.ShapeDtypeStruct((HEADS, 3 * head_dim, width), BF16),
            jax.ShapeDtypeStruct((HEADS * LANES, width), BF16),
            jax.ShapeDtypeStruct((2, HEADS, 8, LANES), F32),
            jax.ShapeDtypeStruct((HEADS, onehot_t.shape[0], LANES), F32),
            *[jax.ShapeDtypeStruct(shape, F32) for shape in sum_shapes],
        ],
        scratch_shapes=[
            pltpu.VMEM((rows, width), BF16),
            pltpu.VMEM((HEADS, rows, LANES), BF16),
            pltpu.VMEM((rows, 2 * LANES), BF16),
            pltpu.VMEM((rows, LANES), BF16),
            pltpu.VMEM((rows, 2 * LANES), BF16),
            pltpu.VMEM((rows, LANES), F32),
            pltpu.VMEM((LANES, rows), F32),
            pltpu.VMEM((LANES, rows), F32),
            *(Scatter.scratch(dims, pieces, width) if pieces else []),
        ],
        compiler_params=params(collective_id=3, has_side_effects=True) if pieces else params(),
        name="attend_back",
    )(hidden, y, dn, cotangent, mask, vectors, weight, normed, p, q, k, v, o, onehot, onehot_t, large, *parts, *ready)


def normal_parts(u):
    size = jnp.abs(u)
    bell = jnp.exp(-0.5 * u * u)
    t = 1.0 / (1.0 + (0.3275911 * math.sqrt(0.5)) * size)
    poly = t * (
        0.5 * 0.254829592
        + t * (0.5 * -0.284496736 + t * (0.5 * 1.421413741 + t * (0.5 * -1.453152027 + t * (0.5 * 1.061405429))))
    )
    tail = poly * bell
    return jnp.where(u >= 0.0, 1.0 - tail, tail), bell * (1.0 / math.sqrt(2.0 * math.pi))


BLOCK = (2, 2, 1, 2, 2)
BLOCK_DEVICES = 16


def block_of(ref, i, rows):
    whole = [pl.ds(0, size) for size in BLOCK]
    if len(ref.shape) == 7:
        return ref.at[(pl.ds(2 * i, 2), *whole[1:], rows)]
    return ref.at[(i, *whole, rows)]


def only_valid(cotangent, mask):
    lane = 72 + GRID * GRID // (SMALL * SMALL)
    return jnp.where(mask[:, lane : lane + 1].astype(F32) > 0.5, 0.0, cotangent[...].astype(F32)).astype(BF16)


def mlp_kernel(dims, block, projects, blocks, gathers, sums, order, *refs):
    refs = list(refs)
    take = lambda count: [refs.pop(0) for _ in range(count)]
    tokens, o, out_weight, vectors, cotangent, mask, bias, *early = take(9)
    out_bias, gain, offset = (vectors.at[i : i + 1] for i in (2, 3, 4))
    shards = take(2) if gathers else None
    hidden_out, y_out, dn_out, dbias_out, *grads_out = take(6)
    late = take(2) if gathers else None
    totals = take(2) if sums else None
    normed, dy, weights, grads, act_all, du_all, weight_sems, grad_sems = take(8)
    if gathers:
        first_late = early[0].shape[-2] - PIECE
        shards = [shard.at[pl.ds(first_late, PIECE)] for shard in shards]
        gather = Gather(dims, gathers, shards, late, *take(2))
    if sums:
        scatter = Scatter(dims, sums, grads_out, store_rows(totals), *refs)
    rows = normed.shape[0]
    units = act_all.shape[1]
    step = pl.program_id(0) - projects
    steps = pl.num_programs(0) - projects
    late_step = steps - blocks if gathers else steps

    def copies(target_step, source):
        slot = target_step % 2
        i = target_step % blocks
        rows_of = pl.ds(pl.multiple_of(target_step // blocks * PIECE, PIECE), PIECE)
        return [
            pltpu.make_async_copy(block_of(source[array], i, rows_of), weights.at[slot, array], weight_sems.at[slot, array])
            for array in range(2)
        ]

    def late_copies(target_step):
        slot = target_step % 2
        i = target_step % blocks
        return [
            pltpu.make_async_copy(
                block_of(late[array], i, pl.ds(0, PIECE)), weights.at[slot, array], weight_sems.at[slot, array]
            )
            for array in range(2)
        ]

    def write_copies(target_step):
        slot = target_step % 2
        i = target_step % blocks
        rows_of = pl.ds(pl.multiple_of(target_step // blocks * PIECE, PIECE), PIECE)
        return [
            pltpu.make_async_copy(grads.at[slot, array], block_of(grads_out[array], i, rows_of), grad_sems.at[slot, array])
            for array in range(2)
        ]

    def happen(place, at_step):
        if gathers and order[place]:

            @pl.when(step == at_step)
            def _():
                for event in order[place]:
                    k, number = divmod(event, 10)
                    if k < len(gathers):
                        gather.stage(k, number)
                    else:
                        scatter.stage(k - len(gathers), number)

    def mlp_step():
        for place in range(projects, len(order) - 1, 2):
            happen(place, (place - projects) // 2)
        for copy in copies(step, early):
            copy.wait()

        @pl.when(step + 1 < late_step)
        def _():
            for copy in copies(step + 1, early):
                copy.start()

        if gathers:

            @pl.when((step + 1 > late_step) & (step + 1 < steps))
            def _():
                for copy in late_copies(step + 1):
                    copy.start()

        slot = step % 2
        up = weights[slot, 0].reshape(units, -1)
        down = weights[slot, 1].reshape(units, -1)
        total = jnp.zeros((1, units), F32)
        for start in range(0, rows, block):
            span = pl.ds(start, block)
            if start == rows // 2:

                @pl.when(step >= 1)
                def _():
                    for copy in write_copies(step - 1):
                        copy.wait()

                for place in range(projects + 1, len(order) - 1, 2):
                    happen(place, (place - projects) // 2)
                if gathers:

                    @pl.when(step + 1 == late_step)
                    def _():
                        for copy in late_copies(step + 1):
                            copy.start()

            u = dot_nt(normed[span], up) + bias[0]
            phi, density = normal_parts(u)
            act = (u * phi).astype(BF16)
            slope = phi + u * density
            du = (slope * dot_nt(dy[span], down)).astype(BF16)
            total = total + jnp.sum(du.astype(F32), axis=0, keepdims=True)
            act_all[span] = act
            du_all[span] = du
            y_out[span] += dot_nn(act, down)
            dn_out[span] += dot_nn(du, up)
        dbias_out[0] = total
        grads[slot, 0] = dot_tn(du_all[...], normed[...]).astype(BF16).reshape(grads.shape[2:])
        grads[slot, 1] = dot_tn(act_all[...], dy[...]).astype(BF16).reshape(grads.shape[2:])
        for copy in write_copies(step):
            copy.start()

        @pl.when(step == steps - 1)
        def _():
            for copy in write_copies(step):
                copy.wait()

    @pl.when(step == -projects)
    def _():
        if gathers:
            gather.at.barrier()
        for copy in copies(0, early):
            copy.start()
        y_out[...] = jnp.zeros_like(y_out)
        dn_out[...] = jnp.zeros_like(dn_out)

    for place in range(projects):
        happen(place, place - projects)

    @pl.when(step < 0)
    def _():
        some = tokens.shape[0]
        span = pl.ds(pl.multiple_of(pl.program_id(0) * some, some), some)
        hidden = tokens[...].astype(F32) + (dot_nn(o[...], out_weight[...]) + out_bias[...])
        hidden_out[...] = hidden
        unit, _ = normalise(hidden)
        normed[span] = (unit * gain[...] + offset[...]).astype(BF16)
        dy[span] = only_valid(cotangent, mask)

    @pl.when(step >= 0)
    def _():
        mlp_step()

    happen(len(order) - 1, steps - 1)


def mlp(tokens, o, out_weight, vectors, cotangent, mask, bias, weights, shards, dims):
    rows, width = tokens.shape
    shard_rows = shards[0].shape[0]
    devices = dims[0] * dims[1] * 8
    blocks = devices // BLOCK_DEVICES
    steps = blocks * shard_rows // PIECE
    units = BLOCK_DEVICES * PIECE
    overlap = shard_rows > PIECE
    gathers = pieces_of(0, PIECE) if overlap else []
    sums = pieces_of(0, PIECE) if overlap else []
    anywhere = pl.BlockSpec(memory_space=pl.ANY)
    projects = PROJECTS
    some = rows // projects
    by_step = pl.BlockSpec((1, 1, units), lambda i: (jnp.maximum(i - projects, 0), 0, 0))
    by_rows = lambda cols: pl.BlockSpec((some, cols), lambda i: (jnp.minimum(i, projects - 1), 0))
    spread = spread_of(dims)
    if dims[1] > 1:
        weights = [weight.reshape((blocks,) + BLOCK + (shard_rows, width)) for weight in weights]
    landing = jax.ShapeDtypeStruct(spread + (PIECE, width), BF16)
    total = jax.ShapeDtypeStruct((PIECE, width), F32)
    full = jax.ShapeDtypeStruct(tokens.shape, F32)
    order = order_for(MLP_ORDER, gathers + sums, projects + 2 * steps + 1)
    hidden, y, dn, dbias, d_up, d_down, *rest = pl.pallas_call(
        functools.partial(mlp_kernel, dims, min(256, rows), projects, blocks, gathers, sums, order),
        grid=(projects + steps,),
        in_specs=[by_rows(width), by_rows(o.shape[1]), resident(out_weight.shape)]
        + [resident(vectors.shape), by_rows(width), by_rows(LANES), by_step, anywhere, anywhere]
        + [anywhere, anywhere] * overlap,
        out_specs=[by_rows(width), resident(tokens.shape), resident(tokens.shape), by_step, anywhere, anywhere]
        + ([anywhere] * 2 + [resident((PIECE, width))] * 2) * overlap,
        out_shape=[
            full,
            full,
            full,
            jax.ShapeDtypeStruct(bias.shape, F32),
            *[jax.ShapeDtypeStruct(weight.shape, BF16) for weight in weights],
            *([landing] * 2 + [total] * 2) * overlap,
        ],
        scratch_shapes=[
            pltpu.VMEM((rows, width), BF16),
            pltpu.VMEM((rows, width), BF16),
            pltpu.VMEM((2, 2) + BLOCK + (PIECE, width), BF16),
            pltpu.VMEM((2, 2) + BLOCK + (PIECE, width), BF16),
            pltpu.VMEM((rows, units), BF16),
            pltpu.VMEM((rows, units), BF16),
            pltpu.SemaphoreType.DMA((2, 2)),
            pltpu.SemaphoreType.DMA((2, 2)),
            *(Gather.scratch(dims, gathers) + Scatter.scratch(dims, sums, width) if overlap else []),
        ],
        compiler_params=params(collective_id=5, has_side_effects=True) if overlap else params(),
        name="mlp",
    )(tokens, o, out_weight, vectors, cotangent, mask, bias, *weights, *(shards if overlap else []))
    whole = spread + (shard_rows, width)
    return hidden, y, dn, dbias, d_up.reshape(whole), d_down.reshape(whole), rest[2:]


class SumAll:
    def __init__(self, at, total, send, got, sems):
        self.at, self.total, self.send, self.got, self.sems = at, total, send, got, sems

    @staticmethod
    def scratch(dims, shape):
        copies = 2 + dims[0] * dims[1]
        return [
            pltpu.VMEM(shape, F32),
            pltpu.VMEM((4,) + shape, F32),
            pltpu.VMEM((copies,) + shape, F32),
            pltpu.SemaphoreType.DMA((copies, 2)),
        ]

    def start(self, stage, kind, to):
        pltpu.make_async_remote_copy(
            src_ref=self.send.at[stage],
            dst_ref=self.got.at[kind],
            send_sem=self.sems.at[kind, 0],
            recv_sem=self.sems.at[kind, 1],
            device_id=to,
            device_id_type=MESH_ID,
        ).start()

    def take(self, kind):
        wait_for(self.got.at[kind], self.sems.at[kind, 1])
        wait_for(self.got.at[kind], self.sems.at[kind, 0])

    def stage(self, number):
        at = self.at
        p_next = at.device(at.g1, 1 - at.p, at.g2, at.c, at.q)
        q_next = at.device(at.g1, at.p, at.g2, at.c, 1 - at.q)
        if 0 < number < 4:
            self.take(number - 1)
            self.total[...] += self.got[number - 1]
        if number < 4:
            self.send[number] = self.total[...]
        if number < 3:
            self.start(number, number, (at.sibling(), p_next, q_next)[number])
        if number == 3:
            line = at.G1 * at.G2
            mine = at.g1 * at.G2 + at.g2
            for i, spot in enumerate(at.line()):
                self.start(3, 3 + i, at.on_line(spot))
        if number == 4:
            line = at.G1 * at.G2
            mine = at.g1 * at.G2 + at.g2
            for i in range(line - 1):
                self.take(3 + i)
            spots = [spot[0] * at.G2 + spot[1] for spot in at.line()]
            parts = [self.got[3 + i] for i in range(line - 1)] + [self.send[3]]
            spots.append(mine)
            total = jnp.zeros_like(parts[0])
            for place in range(line):
                chosen = jnp.zeros_like(parts[0])
                for spot, part in zip(spots, parts):
                    chosen = jnp.where(spot == place, part, chosen)
                total = total + chosen
            self.total[...] = total


def end_kernel(dims, pieces, order, shares, head_dim, tokens, dqkv, weight_all, vectors, dh, small, time_send, vec_in, dw, dw_out,
               out, vec_out, time_out, qkv_out, out_out, weight, weight_sem, mixed, dw_buffer, dw_sems, time_got, time_sems,
               vec_total, vec_send, vec_got, vec_sems, *buffers):
    step = pl.program_id(0)
    steps = pl.num_programs(0)

    def put_sum(array, start, count, total):
        stop, cut_at = start + count, shares[0]
        if start < cut_at:
            qkv_out[start : min(stop, cut_at)] = total[: min(stop, cut_at) - start]
        first, last = max(start, cut_at), min(stop, sum(shares))
        if first < last:
            out_out[first - cut_at : last - cut_at] = total[first - start : last - start]

    work = Scatter(dims, pieces, (mixed,), put_sum, *buffers)
    at = work.at
    sums = SumAll(at, vec_total, vec_send, vec_got, vec_sems)
    width = tokens.shape[1]
    fetches = HEADS + HEADS // 2
    pair = 2 * LANES

    def fetch(number):
        slot = number % 2
        if number < HEADS:
            return pltpu.make_async_copy(dw.at[number], dw_buffer.at[slot, pl.ds(0, dw.shape[1])], dw_sems.at[slot])
        source = dw_out.at[pl.ds((number - HEADS) * pair, pair)]
        return pltpu.make_async_copy(source, dw_buffer.at[slot, pl.ds(0, pair)], dw_sems.at[slot])

    def place_of(device):
        place = []
        for size in reversed(spread_of(dims)):
            device, digit = divmod(device, size)
            place.insert(0, digit)
        return tuple(place)

    def put(first, share, base, value):
        done = 0
        while done < head_dim:
            device, offset = divmod(first + done, share)
            count = min(head_dim - done, share - offset)
            mixed[(*place_of(device), slice(base + offset, base + offset + count))] = value[done : done + count]
            done += count

    @pl.when(step == 0)
    def _():
        fetch(0).start()
        pltpu.make_async_copy(weight_all, weight, weight_sem).start()
        time_got[...] = jnp.zeros_like(time_got)
        at.barrier_all()
        exchange(at, time_send, time_got, time_sems)
        vec_total[...] = vec_in[...]
        for number in range(fetches):
            if number + 1 < fetches:
                fetch(number + 1).start()
            fetch(number).wait()
            if number < HEADS:
                for kind in range(3):
                    value = dw_buffer[number % 2, kind * head_dim : (kind + 1) * head_dim]
                    put((kind * HEADS + number) * head_dim, shares[0], 0, value)
            else:
                for i in range(2):
                    head = (number - HEADS) * 2 + i
                    value = dw_buffer[number % 2, i * LANES : i * LANES + head_dim]
                    put(head * head_dim, shares[1], shares[0], value)

    for place in range(len(order) - 1):
        events(order, step, work, place)

    @pl.when(step == 0)
    def _():
        pltpu.make_async_copy(weight_all, weight, weight_sem).wait()

    dn = dot_nn(dqkv[...], weight[...])
    back, unit = norm_back(tokens[...].astype(F32), vectors[0:1], dn)
    out[...] = (dh[...] + back).astype(BF16)
    vec_total[0:1, :width] += jnp.sum(dn * unit, axis=0, keepdims=True)
    vec_total[1:2, :width] += jnp.sum(dn, axis=0, keepdims=True)

    @pl.when(step == steps - 1)
    def _():
        for event in order[-1]:
            k, number = divmod(event, 10)
            if k == len(pieces):
                sums.stage(number)
            else:
                work.stage(k, number)
        exchanged(at, time_got, time_sems)
        time_got[at.index(), 0:8] = time_send[at.index()]
        vec_out[...] = vec_total[...]
        times = time_got[...].reshape(small.shape[0], LANES)
        high = times.astype(BF16)
        low = (times - high.astype(F32)).astype(BF16)
        time_out[...] = (dot_tn(high, small[...]) + dot_tn(low, small[...]))[: time_out.shape[0]]


def end(tokens, dqkv, weight, vectors, dh, small, time_send, vec_in, dw, dw_out, dims, shares, time_share, head_dim):
    rows, width = tokens.shape
    block = rows // 8
    by_rows = lambda cols: pl.BlockSpec((block, cols), lambda i: (i, 0))
    shard_rows = -(-sum(shares) // PIECE) * PIECE
    pieces = cut(0, shard_rows, BEGIN_ROWS)
    order = order_for(END_ORDER, pieces, rows // block + 1, True)
    anywhere = pl.BlockSpec(memory_space=pl.ANY)
    devices = time_send.shape[0]
    return pl.pallas_call(
        functools.partial(end_kernel, dims, pieces, order, shares, head_dim),
        grid=(rows // block,),
        in_specs=[
            by_rows(width),
            by_rows(dqkv.shape[1]),
            anywhere,
            resident(vectors.shape),
            by_rows(width),
            resident(small.shape),
            resident(time_send.shape),
            resident(vec_in.shape),
            anywhere,
            anywhere,
        ],
        out_specs=[
            by_rows(width),
            resident(vec_in.shape),
            resident((time_share, width)),
            resident((shares[0], width)),
            resident((shares[1], width)),
        ],
        out_shape=[
            jax.ShapeDtypeStruct(tokens.shape, BF16),
            jax.ShapeDtypeStruct(vec_in.shape, F32),
            jax.ShapeDtypeStruct((time_share, width), F32),
            jax.ShapeDtypeStruct((shares[0], width), F32),
            jax.ShapeDtypeStruct((shares[1], width), F32),
        ],
        scratch_shapes=[
            pltpu.VMEM(weight.shape, BF16),
            pltpu.SemaphoreType.DMA,
            pltpu.VMEM(spread_of(dims) + (shard_rows, width), BF16),
            pltpu.VMEM((2, 2 * LANES, width), BF16),
            pltpu.SemaphoreType.DMA((2,)),
            pltpu.VMEM((devices, small.shape[0] // devices, LANES), F32),
            pltpu.SemaphoreType.DMA((2,)),
            *SumAll.scratch(dims, vec_in.shape),
            *Scatter.scratch(dims, pieces, width, in_place=True),
        ],
        compiler_params=params(collective_id=4, has_side_effects=True),
        name="end",
    )(tokens, dqkv, weight, vectors, dh, small, time_send, vec_in, dw, dw_out)


def split_kernel(width, share, unit_share, heads, total, *refs):
    count = (len(refs) - 10) // 3
    sources, outs, targets = refs[:count], refs[count : count + 9], refs[count + 9 : 2 * count + 9]
    middles, sems = refs[2 * count + 9 : -1], refs[-1]
    for i in range(count):
        pltpu.make_async_copy(sources[i], middles[i], sems.at[i]).start()
    for i in range(count):
        pltpu.make_async_copy(sources[i], middles[i], sems.at[i]).wait()
        pltpu.make_async_copy(middles[i], targets[i], sems.at[i]).start()
    place = lax.axis_index("dp") * lax.axis_size("fsdp") + lax.axis_index("fsdp")
    turned = pltpu.roll(total[0:8, :width], (width - place * share) % width, 1)
    for i in range(6):
        outs[i][...] = turned[i, :share]
    per_row = width // unit_share
    row = jnp.zeros((8, width), F32)
    for i in range(4):
        row = jnp.where(place // per_row == i, total[6 + i : 7 + i, :width], row)
    row = pltpu.roll(row, (width - place % per_row * unit_share) % width, 1)
    outs[6][...] = row[0, :unit_share]
    mine = pl.ds(pl.multiple_of(lax.axis_index("fsdp") * heads, heads), heads)
    for i in range(2):
        outs[7 + i][...] = total[mine, width + i * LANES : width + i * LANES + 2 * GRID - 1]
    for i in range(count):
        pltpu.make_async_copy(middles[i], targets[i], sems.at[i]).wait()


def split(total, width, share, unit_share, heads, results):
    vmem, anywhere = pl.BlockSpec(memory_space=pltpu.VMEM), pl.BlockSpec(memory_space=pl.ANY)
    shapes = [(share,)] * 6 + [(unit_share,)] + [(heads, 2 * GRID - 1)] * 2
    return pl.pallas_call(
        functools.partial(split_kernel, width, share, unit_share, heads),
        in_specs=[vmem] + [anywhere] * len(results),
        out_specs=[vmem] * len(shapes) + [anywhere] * len(results),
        out_shape=[jax.ShapeDtypeStruct(shape, F32) for shape in shapes]
        + [jax.ShapeDtypeStruct(result.shape, result.dtype) for result in results],
        scratch_shapes=[pltpu.VMEM(result.shape, result.dtype) for result in results]
        + [pltpu.SemaphoreType.DMA((len(results),))],
        compiler_params=params(),
        name="split",
    )(total, *results)


def time_embed(stamps, feat_width):
    half_width = feat_width // 2
    frequency = jnp.exp(-math.log(10000.0) * jnp.arange(half_width, dtype=F32) / half_width)
    angles = stamps.astype(F32)[:, None] * frequency[None, :]
    return jnp.concatenate([jnp.cos(angles), jnp.sin(angles)], axis=1)


def local(
    tokens,
    image_lengths,
    timesteps,
    patch_cells,
    norm1_gain,
    norm1_bias,
    qkv_weight,
    time_weight,
    out_weight,
    out_bias,
    norm2_gain,
    norm2_bias,
    fc1_weight,
    fc1_bias,
    fc2_weight,
    fc2_bias,
    row_table,
    col_table,
    cotangent,
):
    rows, width = tokens.shape
    head_dim = width // HEADS
    slot_rows = SMALL * SMALL
    per = image_lengths.shape[0]
    assert rows == GRID * GRID and per * slot_rows == rows
    fsdp = lax.axis_size("fsdp")
    devices = lax.axis_size("dp") * fsdp
    dims = split_dp(lax.axis_size("dp"))

    qkv_share, out_share = qkv_weight.shape[1], out_weight.shape[0]
    unit_share, time_share = fc1_weight.shape[1], time_weight.shape[1]
    units = devices * unit_share
    mixed_shard = pad_rows(jnp.concatenate([qkv_weight.T, out_weight], axis=0))
    embedded = time_embed(timesteps, width).astype(BF16)
    vectors = (norm1_gain, norm1_bias, out_bias, norm2_gain, norm2_bias, fc2_bias, fc1_bias)
    table_rows, table_width = row_table.shape
    small_rows, table_at = 16, 8
    put_at = lambda part, row, lane: jnp.pad(
        part, ((row, small_rows - row - part.shape[0]), (lane, width - lane - part.shape[1]))
    )
    spots_of = [put_at(embedded, 0, 0), put_at(row_table, table_at, 2 * LANES), put_at(col_table, table_at, 3 * LANES)]
    spots_of += [put_at(vector[None], per + i, 0) for i, vector in enumerate(vectors)]
    small_shard = functools.reduce(jnp.add, spots_of)
    time_padded = jnp.pad(time_weight, ((0, 0), (0, LANES - time_share)))
    shares = (qkv_share, out_share)
    qkv_full, out_full, small, times = begin(mixed_shard, small_shard, time_padded, dims, shares, head_dim)
    vector_share = norm1_gain.shape[0]
    vectors = small[:, per : per + 6, :vector_share].transpose(1, 0, 2).reshape(6, width).astype(F32)
    b_up = small[:, per + 6, :unit_share].astype(F32)
    b_up = jnp.pad(b_up, ((0, 0), (0, -unit_share % PIECE)))
    b_up = b_up.reshape(devices // BLOCK_DEVICES, BLOCK_DEVICES, b_up.shape[1] // PIECE, PIECE)
    b_up = b_up.transpose(2, 0, 1, 3).reshape(-1, 1, BLOCK_DEVICES * PIECE)
    unit_shards = (pad_rows(fc1_weight.T), pad_rows(fc2_weight))
    tables = small[:fsdp, table_at : table_at + table_rows, 2 * LANES : 4 * LANES].reshape(HEADS, 2, LANES)
    tables = tables.transpose(1, 0, 2).reshape(2 * HEADS, LANES)[:, :table_width]

    lengths = image_lengths
    large = lengths[0] > slot_rows
    local_rows = jnp.arange(rows, dtype=jnp.int32)
    slot = jnp.where(large, 0, local_rows // slot_rows)
    spots = jnp.arange(per, dtype=jnp.int32)
    slot_pick = slot[:, None] == spots[None, :]
    slot_length = jnp.sum(jnp.where(slot_pick, lengths[None, :], 0), axis=1)
    valid = local_rows - slot * slot_rows < slot_length
    grid_index = jnp.arange(GRID, dtype=jnp.int32)
    row_hot = ((patch_cells // GRID)[:, None] == grid_index[None, :]).astype(BF16)
    col_hot = ((patch_cells % GRID)[:, None] == grid_index[None, :]).astype(BF16)
    onehot = jnp.concatenate([row_hot, col_hot, row_hot, col_hot], axis=1)
    both_index = jnp.concatenate([grid_index, grid_index])[:, None]
    both_cells = jnp.where(jnp.arange(2 * GRID)[:, None] < GRID, patch_cells // GRID, patch_cells % GRID)
    onehot_t = (both_cells == both_index).astype(BF16)
    lanes_left = ((0, 0), (head_dim, LANES - head_dim - per - 1))
    mask_q = jnp.concatenate(
        [jnp.where(slot_pick, 0.0, BIG), jnp.full((rows, 1), BIG, F32)], axis=1
    ).astype(BF16)
    mask_k = jnp.concatenate([slot_pick, jnp.logical_not(valid)[:, None]], axis=1).astype(BF16)
    mask_q, mask_k = jnp.pad(mask_q, lanes_left), jnp.pad(mask_k, lanes_left)

    offsets = grid_index[:, None] - grid_index[None, :] + GRID - 1
    diagonal = offsets[:, :, None] == jnp.arange(2 * GRID - 1, dtype=jnp.int32)[None, None, :]
    diagonal = diagonal.reshape(GRID * GRID, 2 * GRID - 1)
    toeplitz = dot_nt(tables, diagonal.astype(BF16)).reshape(2, HEADS, GRID, GRID) * math.sqrt(head_dim)
    high = lax.reduce_precision(toeplitz, 8, 7)
    low = toeplitz - high
    zero = jnp.zeros((HEADS, GRID, GRID), F32)
    table = jnp.concatenate(
        [
            jnp.concatenate([high[0], zero, low[0], zero], axis=2),
            jnp.concatenate([zero, high[1], zero, low[1]], axis=2),
            jnp.zeros((HEADS, 2 * GRID, LANES), F32),
        ],
        axis=1,
    ).astype(BF16)

    if time_share != head_dim:
        times = times[:, :per, :time_share].transpose(1, 0, 2).reshape(per, 2 * HEADS, head_dim)
        times = jnp.pad(times.transpose(1, 0, 2), ((0, 0), (0, 8 - per), (0, LANES - head_dim)))

    scale = 1.0 / math.sqrt(head_dim)
    large_lanes = jnp.broadcast_to(large.astype(F32), (1, LANES))
    normed_one, q, k, v, o, p, up, down = attend(
        tokens, vectors, qkv_full, times, large_lanes, table, onehot, mask_q, mask_k,
        scale * math.log2(math.e), unit_shards, dims,
    )
    hidden, y, dn_two, db_up, d_up, d_down, first_sums = mlp(
        tokens, o, out_full, vectors, cotangent, mask_k, b_up, (up, down), unit_shards, dims
    )
    db_up = db_up.reshape(-1, devices // BLOCK_DEVICES, BLOCK_DEVICES, PIECE).transpose(1, 2, 0, 3)
    db_up = db_up.reshape(devices, -1)[:, :unit_share]

    beside = dims[1] == 1
    layer_out, dh, vec_two, dqkv, d_qkv, d_out, slot_sums, pair, *unit_sums = attend_back(
        hidden, y, dn_two, cotangent, mask_k, vectors, out_full,
        normed_one, p, q, k, v, o, onehot, onehot_t, large_lanes, scale,
        (d_up, d_down) if beside else (), first_sums, dims,
    )
    if not beside:
        unit_sums = scatter(d_up, dims, 6), scatter(d_down, dims, 7)
    up_sum, down_sum = unit_sums
    time_send = slot_sums.reshape(2 * HEADS, 8, LANES)
    if time_share != head_dim:
        time_send = time_send[:, :per, :head_dim].transpose(1, 0, 2).reshape(per, devices, time_share)
        time_send = jnp.pad(time_send.transpose(1, 0, 2), ((0, 0), (0, 8 - per), (0, LANES - time_share)))
    pairs = jnp.concatenate([pair[:, :GRID, :GRID], pair[:, GRID : 2 * GRID, GRID : 2 * GRID]])
    tables = jnp.dot(pairs.reshape(2 * HEADS, GRID * GRID), diagonal.astype(F32), precision=HIGHEST)
    vec_rows, vec_width = HEADS, width + 2 * LANES
    put_in = lambda part, row, lane: jnp.pad(
        part, ((row, vec_rows - row - part.shape[0]), (lane, vec_width - lane - part.shape[1]))
    )
    vec_in = put_in(vec_two, 2, 0) + put_in(db_up.reshape(units // width, width), 6, 0)
    vec_in = vec_in + put_in(tables[:HEADS], 0, width) + put_in(tables[HEADS:], 0, width + LANES)
    input_grad, vec_all, time_grad, qkv_sum, out_sum = end(
        tokens, dqkv, qkv_full.reshape(HEADS * 3 * LANES, width), vectors, dh,
        small.reshape(-1, width), time_send, vec_in, d_qkv, d_out, dims, shares, time_share, head_dim,
    )

    results = (layer_out, input_grad, qkv_sum, time_grad, out_sum, up_sum[:unit_share], down_sum[:unit_share])
    found = split(vec_all, width, vector_share, unit_share, HEADS // fsdp, results)
    vec_sum, (up_bias, row_sum, col_sum) = found[:6], found[6:9]
    layer_out, input_grad, qkv_sum, time_grad, out_sum, up_sum, down_sum = found[9:]

    return (
        layer_out,
        input_grad,
        vec_sum[0],
        vec_sum[1],
        qkv_sum.T,
        time_grad.T,
        out_sum,
        vec_sum[4],
        vec_sum[2],
        vec_sum[3],
        up_sum.T,
        up_bias,
        down_sum,
        vec_sum[5],
        row_sum,
        col_sum,
    )


def solution(mesh):
    rows = P(AXES, None)
    cols = P(None, AXES)
    vector = P(AXES)
    heads = P("fsdp", None)
    in_specs = (
        rows, vector, vector, vector, vector, vector, cols, cols, rows, vector, vector, vector,
        cols, vector, rows, vector, heads, heads, rows,
    )
    out_specs = (
        rows, rows, vector, vector, cols, cols, rows, vector, vector, vector, cols, vector, rows, vector,
        heads, heads,
    )
    return jax.shard_map(local, mesh=mesh, in_specs=in_specs, out_specs=out_specs, check_vma=False)
```

```python
import functools
import math

import jax
import jax.numpy as jnp
from jax import lax
from jax.experimental import pallas as pl
from jax.experimental.pallas import tpu as pltpu
from jax.sharding import PartitionSpec as P

HEADS = 16
GRID = 32
SMALL = 16
AXES = ("dp", "fsdp")
LANES = 128
PIECE = 48
BIG = -1e30
F32 = jnp.float32
BF16 = jnp.bfloat16
HIGHEST = lax.Precision.HIGHEST
MESH_ID = pl.DeviceIdType.MESH
VMEM_LIMIT = 62 * 1024 * 1024


BEGIN_ROWS = (32, 32, 32, 16, 16, 16)
BEGIN_ORDER = ((
    10, 0, 1, 40, 11, 30, 60, 2, 41, 12, 20, 42, 31, 61, 21, 13, 62, 3, 43, 32, 4, 50, 44, 63, 22, 51, 52, 33, 34,
    14, 64, 23, 53, 24, 54,
),)
ATTEND_ORDER = (
    (20,), (), (0,), (21,), (10, 1, 22), (), (11, 30, 2), (), (), (31,), (12,), (3,), (4, 32), (23,), (13,),
    (33,), (34, 24, 14),
)
MLP_ORDER = (
    (0,), (), (), (), (1, 10), (2,), (), (11, 3), (12,), (30, 20), (13, 21), (4, 14, 31), (22,), (23, 32),
    (33,), (), (34, 24),
)
BACK_ORDER = (
    (30, 10), (0,), (11,), (), (20,), (12,), (), (13, 31), (), (1,), (), (14,), (32,), (), (21, 33, 2), (), (),
    (), (22, 3), (), (23, 34), (), (), (4, 24), (),
)
END_ORDER = (
    (20,), (0, 21, 10), (1, 50), (), (22, 11), (30, 2), (23,), (51, 3, 12),
    (52, 31, 40, 13, 60, 41, 53, 24, 4, 32, 61, 42, 33, 54, 43, 62, 63, 14, 34, 44, 64),
)
STAGES = 5
PROJECTS = 4
TURNS = 8


def rounds_order(count, places, extra=False):
    order = [[] for _ in range(places)]
    last = count + STAGES - 2
    for number in range(last + 1):
        for k in range(count):
            if 0 <= number - k < STAGES:
                order[number * (places - 1) // last].append(k * 10 + number - k)
    if extra:
        order[-1] += [count * 10 + number for number in range(STAGES)]
    return order


def dot_nn(a, b):
    return lax.dot_general(a, b, (((1,), (0,)), ((), ())), preferred_element_type=F32)


def dot_nt(a, b):
    return lax.dot_general(a, b, (((1,), (1,)), ((), ())), preferred_element_type=F32)


def dot_tn(a, b):
    return lax.dot_general(a, b, (((0,), (0,)), ((), ())), preferred_element_type=F32)


def params(**more):
    return pltpu.CompilerParams(vmem_limit_bytes=VMEM_LIMIT, **more)


def resident(shape):
    zeros = (0,) * len(shape)
    return pl.BlockSpec(shape, lambda *_: zeros, pipeline_mode=pl.Buffered(1))


def split_dp(dp):
    g2 = 1 if dp <= 16 else 4
    return dp // 4 // g2, g2


class Place:
    def __init__(self, dims):
        self.G1, self.G2 = dims
        dp, self.q = lax.axis_index("dp"), lax.axis_index("fsdp")
        self.c = dp % 2
        rest = dp // 2
        self.g2 = rest % self.G2
        rest = rest // self.G2
        self.p = rest % 2
        self.g1 = rest // 2
        c, p, q = self.c, self.p, self.q
        self.ap, self.aq = (1 - p) * (1 - c) + p * c, q * (1 - c) + (1 - q) * c
        self.bp, self.bq = p * (1 - c) + (1 - p) * c, (1 - q) * (1 - c) + q * c
        self.whole = (pl.ds(0, self.G1), pl.ds(0, self.G2))

    def device(self, g1, p, g2, c, q):
        return (((g1 * 2 + p) * self.G2 + g2) * 2 + c, q)

    def line(self):
        found = []
        for step in range(1, self.G1 * self.G2):
            found.append(((self.g1 + step // self.G2) % self.G1, (self.g2 + step % self.G2) % self.G2))
        return found

    def on_line(self, spot):
        return self.device(spot[0], self.p, spot[1], self.c, self.q)

    def first(self):
        return self.device(self.g1, self.ap, self.g2, self.c, self.aq)

    def second(self):
        return self.device(self.g1, self.bp, self.g2, self.c, self.bq)

    def sibling(self):
        return self.device(self.g1, self.p, self.g2, 1 - self.c, self.q)

    def barrier_all(self):
        semaphore = pltpu.get_barrier_semaphore()
        count = self.count()

        def body(i, carry):
            pl.semaphore_signal(semaphore, inc=1, device_id=self.other(i), device_id_type=MESH_ID)
            return carry

        lax.fori_loop(1, count, body, 0)
        pl.semaphore_wait(semaphore, count - 1)

    def count(self):
        return self.G1 * self.G2 * 8

    def index(self):
        return lax.axis_index("dp") * 2 + self.q

    def other(self, i):
        to = (self.index() + i) % self.count()
        return (to // 2, to % 2)

    def barrier(self):
        partners = [self.on_line(spot) for spot in self.line()] + [self.first(), self.second(), self.sibling()]
        semaphore = pltpu.get_barrier_semaphore()
        for partner in partners:
            pl.semaphore_signal(semaphore, inc=1, device_id=partner, device_id_type=MESH_ID)
        pl.semaphore_wait(semaphore, len(partners))


def wait_for(view, semaphore):
    pltpu.make_async_copy(view, view, semaphore).wait()


class Gather:
    def __init__(self, dims, pieces, sources, results, sems, own_sems):
        self.at = Place(dims)
        self.pieces, self.sources, self.results = pieces, sources, results
        self.sems, self.own_sems = sems, own_sems

    @staticmethod
    def scratch(dims, pieces):
        return [
            pltpu.SemaphoreType.DMA((len(pieces), 7 + dims[0] * dims[1], 2)),
            pltpu.SemaphoreType.DMA((len(pieces),)),
        ]

    def send(self, k, kind, source, target, to):
        pltpu.make_async_remote_copy(
            src_ref=source,
            dst_ref=target,
            send_sem=self.sems.at[k, kind, 0],
            recv_sem=self.sems.at[k, kind, 1],
            device_id=to,
            device_id_type=MESH_ID,
        ).start()

    def finish(self, k, kind, view):
        wait_for(view, self.sems.at[k, kind, 1])
        wait_for(view, self.sems.at[k, kind, 0])

    def stage(self, k, number):
        at = self.at
        array, start, count = self.pieces[k]
        rows = pl.ds(start, count)
        result = self.results[array]
        every, every2 = at.whole
        source = self.sources[array].at[rows]
        own = result.at[at.g1, at.p, at.g2, at.c, at.q, rows]

        def plane(p, q):
            return result.at[every, p, every2, at.c, q, rows]

        if number == 0:
            pltpu.make_async_copy(source, own, self.own_sems.at[k]).start()
            for i, spot in enumerate(at.line()):
                self.send(k, 8 + i, source, own, at.on_line(spot))
        if number == 1:
            pltpu.make_async_copy(source, own, self.own_sems.at[k]).wait()
            for i in range(len(at.line())):
                self.finish(k, 8 + i, own)
            mine = plane(at.p, at.q)
            self.send(k, 1, mine, mine, at.first())
            self.send(k, 3, mine, mine, at.sibling())
        if number == 2:
            mine, came = plane(at.p, at.q), plane(at.ap, at.aq)
            self.finish(k, 1, came)
            self.send(k, 2, mine, mine, at.second())
            self.send(k, 4, came, came, at.second())
            self.send(k, 5, came, came, at.sibling())
        if number == 3:
            for kind, came in ((2, plane(at.bp, at.bq)), (4, plane(1 - at.p, 1 - at.q))):
                self.finish(k, kind, came)
                self.send(k, 6 + kind // 4, came, came, at.sibling())
        if number == 4:
            for kind in (3, 5, 6, 7):
                self.finish(k, kind, plane(at.p, at.q))


class Scatter:
    def __init__(
        self, dims, pieces, sources, put, held, from_core, from_second, from_first, from_line, sems
    ):
        self.at = Place(dims)
        self.pieces, self.sources, self.put = pieces, sources, put
        self.held, self.from_core, self.from_second = held, from_core, from_second
        self.from_first, self.from_line, self.sems = from_first, from_line, sems

    @staticmethod
    def scratch(dims, pieces, width, in_place=False):
        G1, G2 = dims
        n = len(pieces)
        most = max(piece[2] for piece in pieces)
        return [
            pltpu.VMEM((8, LANES) if in_place else (n, G1, 2, G2, 2, most, width), BF16),
            pltpu.VMEM((n, G1, 2, G2, 2, most, width), BF16),
            pltpu.VMEM((n, 2, G1, G2, most, width), BF16),
            pltpu.VMEM((n, G1, G2, most, width), BF16),
            pltpu.VMEM((n, G1 * G2 - 1, most, width), BF16),
            pltpu.SemaphoreType.DMA((n, 5 + G1 * G2, 2)),
        ]

    def send(self, k, kind, source, target, to):
        pltpu.make_async_remote_copy(
            src_ref=source,
            dst_ref=target,
            send_sem=self.sems.at[k, kind, 0],
            recv_sem=self.sems.at[k, kind, 1],
            device_id=to,
            device_id_type=MESH_ID,
        ).start()

    def add(self, target, addend):
        at = self.at

        def body(i, carry):
            g1, g2 = i // at.G2, i % at.G2
            target[g1, g2] = target[g1, g2] + addend[g1, g2]
            return carry

        lax.fori_loop(0, at.G1 * at.G2, body, 0)

    def stage(self, k, number):
        at = self.at
        array, start, count = self.pieces[k]
        rows = pl.ds(start, count)
        source = self.sources[array]
        every, every2 = at.whole
        both = pl.ds(0, 2)
        in_place = len(self.held.shape) == 2
        some = pl.ds(0, count)
        from_core = self.from_core.at[k, every, both, every2, both, some]
        from_second = [self.from_second.at[k, i, every, every2, some] for i in range(2)]
        from_first = self.from_first.at[k, every, every2, some]
        from_line = [self.from_line.at[k, i, some] for i in range(at.G1 * at.G2 - 1)]

        def plane(p, q):
            if in_place:
                return source.at[every, p, every2, at.c, q, rows]
            return self.held.at[k, every, p, every2, q, some]

        local_copy = lambda: pltpu.make_async_copy(
            source.at[every, both, every2, at.c, both, rows],
            self.held.at[k, every, both, every2, both, some],
            self.sems.at[k, 4, 0],
        )
        if number == 0:
            self.send(k, 0, source.at[every, both, every2, 1 - at.c, both, rows], from_core, at.sibling())
            if not in_place:
                local_copy().start()
        if number == 1:
            if not in_place:
                local_copy().wait()
            wait_for(from_core, self.sems.at[k, 0, 1])
            for p, q in ((at.bp, at.bq), (1 - at.p, 1 - at.q)):
                self.add(plane(p, q), from_core.at[every, p, every2, q])
            self.send(k, 1, plane(at.bp, at.bq), from_second[0], at.second())
            self.send(k, 2, plane(1 - at.p, 1 - at.q), from_second[1], at.second())
            for p, q in ((at.p, at.q), (at.ap, at.aq)):
                self.add(plane(p, q), from_core.at[every, p, every2, q])
        if number == 2:
            for kind in (1, 2):
                wait_for(from_second[kind - 1], self.sems.at[k, kind, 1])
            self.add(plane(at.ap, at.aq), from_second[1])
            self.send(k, 3, plane(at.ap, at.aq), from_first, at.first())
            self.add(plane(at.p, at.q), from_second[0])
        if number == 3:
            wait_for(from_first, self.sems.at[k, 3, 1])
            self.add(plane(at.p, at.q), from_first)
            mine = plane(at.p, at.q)
            for i, spot in enumerate(at.line()):
                self.send(k, 5 + i, mine.at[spot[0], spot[1]], from_line[i], at.on_line(spot))
        if number == 4:
            total = plane(at.p, at.q)[at.g1, at.g2].astype(F32)
            for i in range(at.G1 * at.G2 - 1):
                wait_for(from_line[i], self.sems.at[k, 5 + i, 1])
                total = total + from_line[i][...].astype(F32)
            self.put(array, start, count, total)
            wait_for(from_core, self.sems.at[k, 0, 0])
            for kind in (1, 2):
                wait_for(from_second[kind - 1], self.sems.at[k, kind, 0])
            wait_for(from_first, self.sems.at[k, 3, 0])
            for i in range(at.G1 * at.G2 - 1):
                wait_for(from_line[i], self.sems.at[k, 5 + i, 0])


def pieces_of(first, last):
    return [(array, start, PIECE) for start in range(first, last, PIECE) for array in range(2)]


def early_rows(rows):
    return max(PIECE, rows - PIECE)


def summed_rows(rows):
    return PIECE if rows > PIECE else 0


def cut(array, rows, sizes):
    if sum(sizes) != rows:
        sizes = (PIECE,) * (rows // PIECE)
    return [(array, sum(sizes[:i]), size) for i, size in enumerate(sizes)]


def order_for(order, pieces, places, extra=False):
    count = len(pieces) + extra
    if len(order) == places and sum(len(place) for place in order) == count * STAGES:
        return order
    return rounds_order(len(pieces), places, extra)


def pad_rows(shard):
    rows = shard.shape[0]
    return jnp.pad(shard, ((0, -rows % PIECE), (0, 0)))


def spread_of(dims):
    return (dims[0], 2, dims[1], 2, 2)


def exchange(at, source, target, sems):
    me = at.index()

    def body(i, carry):
        to = (me + i) % at.count()
        pltpu.make_async_remote_copy(
            src_ref=source.at[to, pl.ds(0, 8)],
            dst_ref=target.at[me, pl.ds(0, 8)],
            send_sem=sems.at[0],
            recv_sem=sems.at[1],
            device_id=at.other(i),
            device_id_type=MESH_ID,
        ).start()
        return carry

    lax.fori_loop(1, at.count(), body, 0)


def exchanged(at, target, sems):
    view = target.at[pl.ds(0, at.count() - 1), pl.ds(0, 8)]
    wait_for(view, sems.at[1])
    wait_for(view, sems.at[0])


def frame_arrays(head_dim, cells, cells_row, lengths, onehot, onehot_t, mask_q, mask_k, large):
    rows = onehot.shape[0]
    slot_rows = SMALL * SMALL
    per = rows // slot_rows
    lane = lax.broadcasted_iota(jnp.int32, (rows, LANES), 1)
    row = lax.broadcasted_iota(jnp.int32, (rows, LANES), 0)
    cell = jnp.broadcast_to(cells[...], (rows, LANES))
    place = jnp.where(lane % (2 * GRID) < GRID, cell // GRID, cell % GRID)
    onehot[...] = jnp.where(place == lane % GRID, 1.0, 0.0).astype(BF16)
    index = lax.broadcasted_iota(jnp.int32, (2 * GRID, rows), 0)
    cell = jnp.broadcast_to(cells_row[...], (2 * GRID, rows))
    place = jnp.where(index < GRID, cell // GRID, cell % GRID)
    onehot_t[...] = jnp.where(place == index % GRID, 1.0, 0.0).astype(BF16)
    one = jnp.broadcast_to(lengths[0], (rows, LANES)) > slot_rows
    slot = jnp.where(one, 0, row // slot_rows)
    length = jnp.zeros((rows, LANES), jnp.int32)
    for i in range(per):
        length = jnp.where(slot == i, lengths[i], length)
    valid = row - slot * slot_rows < length
    own = slot == lane - head_dim
    in_slots = (lane >= head_dim) & (lane < head_dim + per)
    last = lane == head_dim + per
    mask_q[...] = jnp.where(last | (in_slots & jnp.logical_not(own)), BIG, 0.0).astype(BF16)
    mask_k[...] = jnp.where((in_slots & own) | (last & jnp.logical_not(valid)), 1.0, 0.0).astype(BF16)
    large[...] = jnp.where(one[0:1], 1.0, 0.0)


def begin_kernel(dims, pieces, order, shares, head_dim, mixed_shard, small_shard, time_weight, cells, cells_row, lengths, qkv_out, out_out, small_out,
                 time_out, onehot_out, onehot_t_out, mask_q_out, mask_k_out, large_out, qkv, outs, mixed, small, time_all, time_got, sems, own_sems, time_sems, laid_sems):
    work = Gather(dims, pieces, (small_shard, mixed_shard), (small, mixed), sems, own_sems)
    at = work.at
    devices = at.count()
    width = mixed.shape[-1]
    at.barrier_all()
    for count, event in enumerate(order):
        work.stage(*divmod(event, 10))
        if count == 5:
            frame_arrays(head_dim, cells, cells_row, lengths, onehot_out, onehot_t_out, mask_q_out, mask_k_out, large_out)
        if event == STAGES - 1:
            small_out[...] = small[...].reshape(small_out.shape)
            for start in range(0, devices, 32):
                span = pl.ds(start, 32)
                rows = small_out[span].reshape(32 * small_out.shape[1], width)
                time_all[span] = dot_nn(rows, time_weight[...]).reshape(32, small_out.shape[1], LANES)
            exchange(at, time_all, time_got, time_sems)
    exchanged(at, time_got, time_sems)
    time_got[at.index()] = time_all[at.index(), 0:8]
    time_out[...] = time_got[...]

    def rows_of(first, share, base):
        parts, left = [], head_dim
        while left:
            device, offset = divmod(first, share)
            count = min(left, share - offset)
            place = []
            for size in reversed(spread_of(dims)):
                device, digit = divmod(device, size)
                place.insert(0, digit)
            parts.append(mixed[(*place, slice(base + offset, base + offset + count))])
            first, left = first + count, left - count
        parts.append(jnp.zeros((LANES - head_dim, width), BF16))
        return jnp.concatenate(parts, axis=0)

    def laid(number):
        if number == HEADS:
            return pltpu.make_async_copy(outs, out_out, laid_sems.at[number])
        return pltpu.make_async_copy(qkv.at[number], qkv_out.at[number], laid_sems.at[number])

    for head in range(HEADS):
        for kind in range(3):
            qkv[head, kind * LANES : (kind + 1) * LANES] = rows_of((kind * HEADS + head) * head_dim, shares[0], 0)
        laid(head).start()
        outs[head * LANES : (head + 1) * LANES] = rows_of(head * head_dim, shares[1], shares[0])
    laid(HEADS).start()
    for number in range(HEADS + 1):
        laid(number).wait()


def begin(mixed_shard, small_shard, time_weight, patch_cells, image_lengths, dims, shares, head_dim):
    width = mixed_shard.shape[1]
    small_rows = small_shard.shape[0]
    rows = patch_cells.shape[0]
    devices = dims[0] * dims[1] * 8
    pieces = [(0, 0, small_rows)] + cut(1, mixed_shard.shape[0], BEGIN_ROWS)
    (order,) = order_for(BEGIN_ORDER, pieces, 1)
    anywhere = pl.BlockSpec(memory_space=pl.ANY)
    vmem = pl.BlockSpec(memory_space=pltpu.VMEM)
    return pl.pallas_call(
        functools.partial(begin_kernel, dims, pieces, order, shares, head_dim),
        in_specs=[anywhere, anywhere, vmem, vmem, vmem, pl.BlockSpec(memory_space=pltpu.SMEM)],
        out_specs=[anywhere, anywhere] + [vmem] * 7,
        out_shape=[
            jax.ShapeDtypeStruct((HEADS, 3 * LANES, width), BF16),
            jax.ShapeDtypeStruct((HEADS * LANES, width), BF16),
            jax.ShapeDtypeStruct((devices, small_rows, width), BF16),
            jax.ShapeDtypeStruct((devices, 8, LANES), F32),
            jax.ShapeDtypeStruct((rows, LANES), BF16),
            jax.ShapeDtypeStruct((2 * GRID, rows), BF16),
            jax.ShapeDtypeStruct((rows, LANES), BF16),
            jax.ShapeDtypeStruct((rows, LANES), BF16),
            jax.ShapeDtypeStruct((1, LANES), F32),
        ],
        scratch_shapes=[
            pltpu.VMEM((HEADS, 3 * LANES, width), BF16),
            pltpu.VMEM((HEADS * LANES, width), BF16),
            pltpu.VMEM(spread_of(dims) + mixed_shard.shape, BF16),
            pltpu.VMEM(spread_of(dims) + small_shard.shape, BF16),
            pltpu.VMEM((devices, small_rows, LANES), F32),
            pltpu.VMEM((devices, 8, LANES), F32),
            *Gather.scratch(dims, pieces),
            pltpu.SemaphoreType.DMA((2,)),
            pltpu.SemaphoreType.DMA((HEADS + 1,)),
        ],
        compiler_params=params(collective_id=1, has_side_effects=True),
        name="begin",
    )(mixed_shard, small_shard, time_weight, patch_cells[:, None], patch_cells[None], image_lengths)


def store_rows(results):
    def put(array, start, count, total):
        results[array][pl.ds(start, count)] = total

    return put


def scatter(part, dims, collective):
    shard = part.shape[5:]
    pieces = cut(0, shard[0], ())
    (order,) = rounds_order(len(pieces), 1)

    def kernel(source, result, *buffers):
        work = Scatter(dims, pieces, (source,), store_rows((result,)), *buffers)
        work.at.barrier()
        for event in order:
            work.stage(*divmod(event, 10))

    return pl.pallas_call(
        kernel,
        out_shape=jax.ShapeDtypeStruct(shard, F32),
        in_specs=[pl.BlockSpec(memory_space=pl.ANY)],
        out_specs=pl.BlockSpec(memory_space=pltpu.VMEM),
        scratch_shapes=Scatter.scratch(dims, pieces, shard[1]),
        compiler_params=params(collective_id=collective, has_side_effects=True),
    )(part)


def normalise(values):
    centre = values - jnp.mean(values, axis=-1, keepdims=True)
    inverse = lax.rsqrt(jnp.mean(centre * centre, axis=-1, keepdims=True) + 1e-06)
    return centre * inverse, inverse


def norm_back(values, gain, grad):
    unit, inverse = normalise(values)
    scaled = grad * gain
    inner = jnp.mean(scaled, axis=-1, keepdims=True) + unit * jnp.mean(scaled * unit, axis=-1, keepdims=True)
    return inverse * (scaled - inner), unit


def events(order, step, work, place):
    if order[place]:

        @pl.when(step == place)
        def _():
            for event in order[place]:
                work.stage(*divmod(event, 10))


def attend_kernel(factor, block, dims, pieces, order, tokens, vectors, weight, time_q, time_v, large, table, onehot,
                  mask_q, mask_k, up_shard, down_shard,
                  normed_out, q_out, k_out, v_out, o_out, p_out, up_out, down_out, keys, sems, own_sems):
    rows = tokens.shape[0]
    gain, shift = vectors.at[0:1], vectors.at[1:2]
    work = Gather(dims, pieces, (up_shard, down_shard), (up_out, down_out), sems, own_sems)
    step = pl.program_id(0)

    @pl.when(step == 0)
    def _():
        work.at.barrier()

    for place in range(HEADS):
        events(order, step, work, place)

    @pl.when(pl.program_id(0) == 0)
    def _():
        for start in range(0, rows, block):
            span = pl.ds(start, block)
            unit, _ = normalise(tokens[span].astype(F32))
            normed_out[span] = (unit * gain[...] + shift[...]).astype(BF16)

    per = rows // (SMALL * SMALL)
    slot = rows // per
    one = large[...] > 0.0
    for i in range(per):
        span = pl.ds(i * slot, slot)
        qkv = dot_nt(normed_out[span], weight[0])
        add_q = jnp.where(one, time_q[0, 0:1], time_q[0, i : i + 1])
        add_v = jnp.where(one, time_v[0, 0:1], time_v[0, i : i + 1])
        q_out[0, span] = (qkv[:, :LANES] + add_q).astype(BF16)
        k_out[0, span] = qkv[:, LANES : 2 * LANES].astype(BF16)
        v_out[0, span] = (qkv[:, 2 * LANES :] + add_v).astype(BF16)
    keys[:, :LANES] = k_out[0] + mask_k[...]
    keys[:, LANES:] = onehot[...]
    for start in range(0, rows, block):
        span = pl.ds(start, block)
        bias = dot_nn(onehot[span], table[0]).astype(BF16)
        query = jnp.concatenate([q_out[0, span] + mask_q[span], bias], axis=1)
        scores = dot_nt(query, keys[...])
        top = jnp.max(scores, axis=1, keepdims=True)
        weights = jnp.exp2((scores - top) * factor)
        total = jnp.sum(weights, axis=1, keepdims=True)
        low = (weights * (1.0 / total)).astype(BF16)
        p_out[0, span] = low
        o_out[span] = dot_nn(low, v_out[0]).astype(BF16)

    @pl.when(step == HEADS - 1)
    def _():
        for event in order[HEADS]:
            work.stage(*divmod(event, 10))


def attend(tokens, vectors, weight, times, large, table, onehot, mask_q, mask_k, factor, shards, dims):
    rows, width = tokens.shape
    block = min(512, rows)
    pieces = pieces_of(0, early_rows(shards[0].shape[0]))
    anywhere = pl.BlockSpec(memory_space=pl.ANY)
    per_head = lambda *shape: pl.BlockSpec((1,) + shape, lambda h: (h, 0, 0))
    head_rows = jax.ShapeDtypeStruct((HEADS, rows, LANES), BF16)
    return pl.pallas_call(
        functools.partial(attend_kernel, factor, block, dims, pieces, order_for(ATTEND_ORDER, pieces, HEADS + 1)),
        grid=(HEADS,),
        in_specs=[
            resident(tokens.shape),
            resident(vectors.shape),
            per_head(3 * LANES, width),
            pl.BlockSpec((1, 8, LANES), lambda h: (h, 0, 0)),
            pl.BlockSpec((1, 8, LANES), lambda h: (HEADS + h, 0, 0)),
            resident(large.shape),
            per_head(LANES, LANES),
            resident(onehot.shape),
            resident(mask_q.shape),
            resident(mask_k.shape),
            anywhere,
            anywhere,
        ],
        out_specs=[
            resident(tokens.shape),
            per_head(rows, LANES),
            per_head(rows, LANES),
            per_head(rows, LANES),
            pl.BlockSpec((rows, LANES), lambda h: (0, h)),
            per_head(rows, rows),
            anywhere,
            anywhere,
        ],
        out_shape=[
            jax.ShapeDtypeStruct(tokens.shape, BF16),
            head_rows,
            head_rows,
            head_rows,
            jax.ShapeDtypeStruct((rows, HEADS * LANES), BF16),
            jax.ShapeDtypeStruct((HEADS, rows, rows), BF16),
            *[jax.ShapeDtypeStruct(spread_of(dims) + s.shape, BF16) for s in shards],
        ],
        scratch_shapes=[pltpu.VMEM((rows, 2 * LANES), BF16), *Gather.scratch(dims, pieces)],
        compiler_params=params(collective_id=2, has_side_effects=True),
        name="attend",
    )(tokens, vectors, weight, times, times, large, table, onehot, mask_q, mask_k, *shards)


def turn_rows(hidden, y, dn, cotangent, mask, vectors, weight, span, out, dh_out, vec_out, da_all, do_all):
    out[...] = (hidden[...] + (y[...] + vectors[5:6])).astype(BF16)
    back, unit = norm_back(hidden[...], vectors[3:4], dn[...])
    dyf = only_valid(cotangent, mask).astype(F32)
    dh = dyf + back
    dh_out[...] = dh
    da = dh.astype(BF16)
    da_all[span] = da
    do = dot_nt(da, weight[...]).astype(BF16)
    for head in range(HEADS):
        do_all[head, span] = do[:, head * LANES : (head + 1) * LANES]
    vec_out[0:1] += jnp.sum(dn[...] * unit, axis=0, keepdims=True)
    vec_out[1:2] += jnp.sum(dn[...], axis=0, keepdims=True)
    vec_out[2:3] += jnp.sum(da.astype(F32), axis=0, keepdims=True)
    vec_out[3:4] += jnp.sum(dyf, axis=0, keepdims=True)


def attend_back_kernel(block, turns, scale, dims, pieces, ready, order, hidden, y, dn, cotangent, mask, vectors, weight,
                       normed, p, q, k, v, o, onehot, onehot_t, large, *refs):
    refs = list(refs)
    take = lambda count: [refs.pop(0) for _ in range(count)]
    parts = take(2 if pieces else 0)
    ready = take(ready)
    out, dh_out, vec_out, dqkv_out, dw_out, dwo_out, sums_out, pair_out = take(8)
    results = take(2 if pieces else 0)
    da_all, do_all, keys, grads, offsets, dq_all, dk_sum, dv_sum = take(8)

    put = store_rows(results)
    work = Scatter(dims, pieces, parts, put, *refs) if pieces else None
    rows = normed.shape[0]
    step = pl.program_id(0)

    @pl.when(step == 0)
    def _():
        if pieces:
            work.at.barrier()
        vec_out[...] = jnp.zeros_like(vec_out)
        for array, part in enumerate(ready):
            put(array, 0, part.shape[0], part[...])

    for place in range(len(order) - 1):
        events(order, step, work, place)

    @pl.when(step < turns)
    def _():
        some = hidden.shape[0]
        span = pl.ds(pl.multiple_of(step * some, some), some)
        turn_rows(hidden, y, dn, cotangent, mask, vectors, weight, span, out, dh_out, vec_out, da_all, do_all)

    @pl.when(step >= turns)
    def _():
        do = do_all.at[step - turns]
        lane = lax.broadcasted_iota(jnp.int32, (rows, LANES), 1)
        head = 72
        delta = jnp.sum(do[...].astype(F32) * o[...].astype(F32), axis=1, keepdims=True)
        high = delta.astype(BF16).astype(F32)
        more = jnp.where(lane == head, -high, jnp.where(lane == head + 1, high - delta, 0.0))
        grads[...] = (do[...].astype(F32) + more).astype(BF16)
        values = v[0] + jnp.where((lane == head) | (lane == head + 1), 1.0, 0.0).astype(BF16)
        keys[:, :LANES] = k[0]
        keys[:, LANES:] = onehot[...]
        for start in range(0, rows, block):
            span = pl.ds(start, block)
            centred = dot_nt(grads[span], values)
            ds = (p[0, span].astype(F32) * centred).astype(BF16)
            both = dot_nn(ds, keys[...])
            dq_all[span] = both[:, :LANES] * scale
            by_place = both[:, LANES:]
            upper = by_place.astype(BF16)
            offsets[span, :LANES] = upper
            offsets[span, LANES:] = (by_place - upper.astype(F32)).astype(BF16)
            dk = dot_tn(q[0, span], ds)
            dv = dot_tn(do[span], p[0, span])
            if start == 0:
                dk_sum[...] = dk
                dv_sum[...] = dv
            else:
                dk_sum[...] += dk
                dv_sum[...] += dv
        dk_sum[...] = dk_sum[...] * scale
        dqkv_out[:, :LANES] = dq_all[...].astype(BF16)
        dqkv_out[:, LANES : 2 * LANES] = dk_sum[...].T.astype(BF16)
        dqkv_out[:, 2 * LANES :] = dv_sum[...].T.astype(BF16)
        turned = jnp.concatenate([dq_all[...].T[:head], dk_sum[:head], dv_sum[:head]], axis=0)
        pair = dot_nn(onehot_t[...], offsets[...])
        pair_out[0] = pair[:, :LANES] + pair[:, LANES:]
        slot = SMALL * SMALL
        one = large[...] > 0.0
        for kind, base in enumerate((0, 2 * LANES)):
            sums = []
            for start in range(0, rows, slot):
                part = dqkv_out[pl.ds(start, slot), base : base + LANES]
                sums.append(jnp.sum(part.astype(F32), axis=0, keepdims=True))
            total = functools.reduce(jnp.add, sums)
            sums = [jnp.where(one, total if i == 0 else jnp.zeros_like(total), part) for i, part in enumerate(sums)]
            sums.append(jnp.zeros((8 - len(sums), LANES), F32))
            sums_out[kind, 0] = jnp.concatenate(sums, axis=0)
        dw_out[0] = dot_nn(turned.astype(BF16), normed[...]).astype(BF16)
        dwo_out[...] = dot_tn(o[...], da_all[...]).astype(BF16)

    if pieces:

        @pl.when(step == pl.num_programs(0) - 1)
        def _():
            for event in order[-1]:
                work.stage(*divmod(event, 10))


def attend_back(
    hidden, y, dn, cotangent, mask, vectors, weight, normed, p, q, k, v, o, onehot, onehot_t, large, scale, parts, ready, dims
):
    rows, width = normed.shape
    head_dim = width // HEADS
    block = min(512, rows)
    turns = TURNS
    some = rows // turns
    pieces, sum_shapes = [], []
    if parts:
        shard_rows = parts[0].shape[5]
        pieces = pieces_of(summed_rows(shard_rows), shard_rows)
        sum_shapes = [(shard_rows, width)] * 2
    anywhere = pl.BlockSpec(memory_space=pl.ANY)
    head_of = lambda s: jnp.maximum(s - turns, 0)
    per_head = lambda *shape: pl.BlockSpec((1,) + shape, lambda s: (head_of(s), 0, 0))
    by_rows = pl.BlockSpec((some, width), lambda s: (jnp.minimum(s, turns - 1), 0))
    return pl.pallas_call(
        functools.partial(
            attend_back_kernel, block, turns, scale, dims, pieces, len(ready),
            order_for(BACK_ORDER, pieces, turns + HEADS + 1),
        ),
        grid=(turns + HEADS,),
        in_specs=[
            by_rows,
            by_rows,
            by_rows,
            by_rows,
            pl.BlockSpec((some, LANES), lambda s: (jnp.minimum(s, turns - 1), 0)),
            resident(vectors.shape),
            resident(weight.shape),
            resident(normed.shape),
            per_head(rows, rows),
            per_head(rows, LANES),
            per_head(rows, LANES),
            per_head(rows, LANES),
            pl.BlockSpec((rows, LANES), lambda s: (0, head_of(s))),
            resident(onehot.shape),
            resident(onehot_t.shape),
            resident(large.shape),
            *[anywhere for _ in parts],
            *[resident(part.shape) for part in ready],
        ],
        out_specs=[
            by_rows,
            by_rows,
            resident((4, width)),
            pl.BlockSpec((rows, 3 * LANES), lambda s: (0, head_of(s))),
            per_head(3 * head_dim, width),
            pl.BlockSpec((LANES, width), lambda s: (head_of(s), 0)),
            pl.BlockSpec((2, 1, 8, LANES), lambda s: (0, head_of(s), 0, 0)),
            per_head(onehot_t.shape[0], LANES),
            *[resident(shape) for shape in sum_shapes],
        ],
        out_shape=[
            jax.ShapeDtypeStruct(hidden.shape, BF16),
            jax.ShapeDtypeStruct(hidden.shape, F32),
            jax.ShapeDtypeStruct((4, width), F32),
            jax.ShapeDtypeStruct((rows, HEADS * 3 * LANES), BF16),
            jax.ShapeDtypeStruct((HEADS, 3 * head_dim, width), BF16),
            jax.ShapeDtypeStruct((HEADS * LANES, width), BF16),
            jax.ShapeDtypeStruct((2, HEADS, 8, LANES), F32),
            jax.ShapeDtypeStruct((HEADS, onehot_t.shape[0], LANES), F32),
            *[jax.ShapeDtypeStruct(shape, F32) for shape in sum_shapes],
        ],
        scratch_shapes=[
            pltpu.VMEM((rows, width), BF16),
            pltpu.VMEM((HEADS, rows, LANES), BF16),
            pltpu.VMEM((rows, 2 * LANES), BF16),
            pltpu.VMEM((rows, LANES), BF16),
            pltpu.VMEM((rows, 2 * LANES), BF16),
            pltpu.VMEM((rows, LANES), F32),
            pltpu.VMEM((LANES, rows), F32),
            pltpu.VMEM((LANES, rows), F32),
            *(Scatter.scratch(dims, pieces, width) if pieces else []),
        ],
        compiler_params=params(collective_id=3, has_side_effects=True) if pieces else params(),
        name="attend_back",
    )(hidden, y, dn, cotangent, mask, vectors, weight, normed, p, q, k, v, o, onehot, onehot_t, large, *parts, *ready)


def normal_parts(u):
    size = jnp.abs(u)
    bell = jnp.exp(-0.5 * u * u)
    t = 1.0 / (1.0 + (0.3275911 * math.sqrt(0.5)) * size)
    poly = t * (
        0.5 * 0.254829592
        + t * (0.5 * -0.284496736 + t * (0.5 * 1.421413741 + t * (0.5 * -1.453152027 + t * (0.5 * 1.061405429))))
    )
    tail = poly * bell
    return jnp.where(u >= 0.0, 1.0 - tail, tail), bell * (1.0 / math.sqrt(2.0 * math.pi))


BLOCK = (2, 2, 1, 2, 2)
BLOCK_DEVICES = 16


def block_of(ref, i, rows):
    whole = [pl.ds(0, size) for size in BLOCK]
    if len(ref.shape) == 7:
        return ref.at[(pl.ds(2 * i, 2), *whole[1:], rows)]
    return ref.at[(i, *whole, rows)]


def only_valid(cotangent, mask):
    lane = 72 + GRID * GRID // (SMALL * SMALL)
    return jnp.where(mask[:, lane : lane + 1].astype(F32) > 0.5, 0.0, cotangent[...].astype(F32)).astype(BF16)


def mlp_kernel(dims, block, projects, blocks, gathers, sums, order, *refs):
    refs = list(refs)
    take = lambda count: [refs.pop(0) for _ in range(count)]
    tokens, o, out_weight, vectors, cotangent, mask, bias, *early = take(9)
    out_bias, gain, offset = (vectors.at[i : i + 1] for i in (2, 3, 4))
    shards = take(2) if gathers else None
    hidden_out, y_out, dn_out, dbias_out, *grads_out = take(6)
    late = take(2) if gathers else None
    totals = take(2) if sums else None
    normed, dy, weights, grads, act_all, du_all, weight_sems, grad_sems = take(8)
    if gathers:
        first_late = early[0].shape[-2] - PIECE
        shards = [shard.at[pl.ds(first_late, PIECE)] for shard in shards]
        gather = Gather(dims, gathers, shards, late, *take(2))
    if sums:
        scatter = Scatter(dims, sums, grads_out, store_rows(totals), *refs)
    rows = normed.shape[0]
    units = act_all.shape[1]
    step = pl.program_id(0) - projects
    steps = pl.num_programs(0) - projects
    late_step = steps - blocks if gathers else steps

    def copies(target_step, source):
        slot = target_step % 2
        i = target_step % blocks
        rows_of = pl.ds(pl.multiple_of(target_step // blocks * PIECE, PIECE), PIECE)
        return [
            pltpu.make_async_copy(block_of(source[array], i, rows_of), weights.at[slot, array], weight_sems.at[slot, array])
            for array in range(2)
        ]

    def late_copies(target_step):
        slot = target_step % 2
        i = target_step % blocks
        return [
            pltpu.make_async_copy(
                block_of(late[array], i, pl.ds(0, PIECE)), weights.at[slot, array], weight_sems.at[slot, array]
            )
            for array in range(2)
        ]

    def write_copies(target_step):
        slot = target_step % 2
        i = target_step % blocks
        rows_of = pl.ds(pl.multiple_of(target_step // blocks * PIECE, PIECE), PIECE)
        return [
            pltpu.make_async_copy(grads.at[slot, array], block_of(grads_out[array], i, rows_of), grad_sems.at[slot, array])
            for array in range(2)
        ]

    def happen(place, at_step):
        if gathers and order[place]:

            @pl.when(step == at_step)
            def _():
                for event in order[place]:
                    k, number = divmod(event, 10)
                    if k < len(gathers):
                        gather.stage(k, number)
                    else:
                        scatter.stage(k - len(gathers), number)

    def mlp_step():
        for place in range(projects, len(order) - 1, 2):
            happen(place, (place - projects) // 2)
        for copy in copies(step, early):
            copy.wait()

        @pl.when(step + 1 < late_step)
        def _():
            for copy in copies(step + 1, early):
                copy.start()

        if gathers:

            @pl.when((step + 1 > late_step) & (step + 1 < steps))
            def _():
                for copy in late_copies(step + 1):
                    copy.start()

        slot = step % 2
        up = weights[slot, 0].reshape(units, -1)
        down = weights[slot, 1].reshape(units, -1)
        total = jnp.zeros((1, units), F32)
        for start in range(0, rows, block):
            span = pl.ds(start, block)
            if start == rows // 2:

                @pl.when(step >= 1)
                def _():
                    for copy in write_copies(step - 1):
                        copy.wait()

                for place in range(projects + 1, len(order) - 1, 2):
                    happen(place, (place - projects) // 2)
                if gathers:

                    @pl.when(step + 1 == late_step)
                    def _():
                        for copy in late_copies(step + 1):
                            copy.start()

            u = dot_nt(normed[span], up) + bias[0]
            phi, density = normal_parts(u)
            act = (u * phi).astype(BF16)
            slope = phi + u * density
            du = (slope * dot_nt(dy[span], down)).astype(BF16)
            total = total + jnp.sum(du.astype(F32), axis=0, keepdims=True)
            act_all[span] = act
            du_all[span] = du
            y_out[span] += dot_nn(act, down)
            dn_out[span] += dot_nn(du, up)
        dbias_out[0] = total
        grads[slot, 0] = dot_tn(du_all[...], normed[...]).astype(BF16).reshape(grads.shape[2:])
        grads[slot, 1] = dot_tn(act_all[...], dy[...]).astype(BF16).reshape(grads.shape[2:])
        for copy in write_copies(step):
            copy.start()

        @pl.when(step == steps - 1)
        def _():
            for copy in write_copies(step):
                copy.wait()

    @pl.when(step == -projects)
    def _():
        if gathers:
            gather.at.barrier()
        for copy in copies(0, early):
            copy.start()
        y_out[...] = jnp.zeros_like(y_out)
        dn_out[...] = jnp.zeros_like(dn_out)

    for place in range(projects):
        happen(place, place - projects)

    @pl.when(step < 0)
    def _():
        some = tokens.shape[0]
        span = pl.ds(pl.multiple_of(pl.program_id(0) * some, some), some)
        hidden = tokens[...].astype(F32) + (dot_nn(o[...], out_weight[...]) + out_bias[...])
        hidden_out[...] = hidden
        unit, _ = normalise(hidden)
        normed[span] = (unit * gain[...] + offset[...]).astype(BF16)
        dy[span] = only_valid(cotangent, mask)

    @pl.when(step >= 0)
    def _():
        mlp_step()

    happen(len(order) - 1, steps - 1)


def mlp(tokens, o, out_weight, vectors, cotangent, mask, bias, weights, shards, dims):
    rows, width = tokens.shape
    shard_rows = shards[0].shape[0]
    devices = dims[0] * dims[1] * 8
    blocks = devices // BLOCK_DEVICES
    steps = blocks * shard_rows // PIECE
    units = BLOCK_DEVICES * PIECE
    overlap = shard_rows > PIECE
    gathers = pieces_of(0, PIECE) if overlap else []
    sums = pieces_of(0, PIECE) if overlap else []
    anywhere = pl.BlockSpec(memory_space=pl.ANY)
    projects = PROJECTS
    some = rows // projects
    by_step = pl.BlockSpec((1, 1, units), lambda i: (jnp.maximum(i - projects, 0), 0, 0))
    by_rows = lambda cols: pl.BlockSpec((some, cols), lambda i: (jnp.minimum(i, projects - 1), 0))
    spread = spread_of(dims)
    if dims[1] > 1:
        weights = [weight.reshape((blocks,) + BLOCK + (shard_rows, width)) for weight in weights]
    landing = jax.ShapeDtypeStruct(spread + (PIECE, width), BF16)
    total = jax.ShapeDtypeStruct((PIECE, width), F32)
    full = jax.ShapeDtypeStruct(tokens.shape, F32)
    order = order_for(MLP_ORDER, gathers + sums, projects + 2 * steps + 1)
    hidden, y, dn, dbias, d_up, d_down, *rest = pl.pallas_call(
        functools.partial(mlp_kernel, dims, min(256, rows), projects, blocks, gathers, sums, order),
        grid=(projects + steps,),
        in_specs=[by_rows(width), by_rows(o.shape[1]), resident(out_weight.shape)]
        + [resident(vectors.shape), by_rows(width), by_rows(LANES), by_step, anywhere, anywhere]
        + [anywhere, anywhere] * overlap,
        out_specs=[by_rows(width), resident(tokens.shape), resident(tokens.shape), by_step, anywhere, anywhere]
        + ([anywhere] * 2 + [resident((PIECE, width))] * 2) * overlap,
        out_shape=[
            full,
            full,
            full,
            jax.ShapeDtypeStruct(bias.shape, F32),
            *[jax.ShapeDtypeStruct(weight.shape, BF16) for weight in weights],
            *([landing] * 2 + [total] * 2) * overlap,
        ],
        scratch_shapes=[
            pltpu.VMEM((rows, width), BF16),
            pltpu.VMEM((rows, width), BF16),
            pltpu.VMEM((2, 2) + BLOCK + (PIECE, width), BF16),
            pltpu.VMEM((2, 2) + BLOCK + (PIECE, width), BF16),
            pltpu.VMEM((rows, units), BF16),
            pltpu.VMEM((rows, units), BF16),
            pltpu.SemaphoreType.DMA((2, 2)),
            pltpu.SemaphoreType.DMA((2, 2)),
            *(Gather.scratch(dims, gathers) + Scatter.scratch(dims, sums, width) if overlap else []),
        ],
        compiler_params=params(collective_id=5, has_side_effects=True) if overlap else params(),
        name="mlp",
    )(tokens, o, out_weight, vectors, cotangent, mask, bias, *weights, *(shards if overlap else []))
    whole = spread + (shard_rows, width)
    return hidden, y, dn, dbias, d_up.reshape(whole), d_down.reshape(whole), rest[2:]


class SumAll:
    def __init__(self, at, total, send, got, sems):
        self.at, self.total, self.send, self.got, self.sems = at, total, send, got, sems

    @staticmethod
    def scratch(dims, shape):
        copies = 2 + dims[0] * dims[1]
        return [
            pltpu.VMEM(shape, F32),
            pltpu.VMEM((4,) + shape, F32),
            pltpu.VMEM((copies,) + shape, F32),
            pltpu.SemaphoreType.DMA((copies, 2)),
        ]

    def start(self, stage, kind, to):
        pltpu.make_async_remote_copy(
            src_ref=self.send.at[stage],
            dst_ref=self.got.at[kind],
            send_sem=self.sems.at[kind, 0],
            recv_sem=self.sems.at[kind, 1],
            device_id=to,
            device_id_type=MESH_ID,
        ).start()

    def take(self, kind):
        wait_for(self.got.at[kind], self.sems.at[kind, 1])
        wait_for(self.got.at[kind], self.sems.at[kind, 0])

    def stage(self, number):
        at = self.at
        p_next = at.device(at.g1, 1 - at.p, at.g2, at.c, at.q)
        q_next = at.device(at.g1, at.p, at.g2, at.c, 1 - at.q)
        if 0 < number < 4:
            self.take(number - 1)
            self.total[...] += self.got[number - 1]
        if number < 4:
            self.send[number] = self.total[...]
        if number < 3:
            self.start(number, number, (at.sibling(), p_next, q_next)[number])
        if number == 3:
            line = at.G1 * at.G2
            mine = at.g1 * at.G2 + at.g2
            for i, spot in enumerate(at.line()):
                self.start(3, 3 + i, at.on_line(spot))
        if number == 4:
            line = at.G1 * at.G2
            mine = at.g1 * at.G2 + at.g2
            for i in range(line - 1):
                self.take(3 + i)
            spots = [spot[0] * at.G2 + spot[1] for spot in at.line()]
            parts = [self.got[3 + i] for i in range(line - 1)] + [self.send[3]]
            spots.append(mine)
            total = jnp.zeros_like(parts[0])
            for place in range(line):
                chosen = jnp.zeros_like(parts[0])
                for spot, part in zip(spots, parts):
                    chosen = jnp.where(spot == place, part, chosen)
                total = total + chosen
            self.total[...] = total


def end_kernel(dims, pieces, order, shares, head_dim, tokens, dqkv, weight_all, vectors, dh, small, time_send, vec_in, dw, dw_out,
               out, vec_out, time_out, qkv_out, out_out, weight, weight_sem, mixed, dw_buffer, dw_sems, time_got, time_sems,
               vec_total, vec_send, vec_got, vec_sems, *buffers):
    step = pl.program_id(0)
    steps = pl.num_programs(0)

    def put_sum(array, start, count, total):
        stop, cut_at = start + count, shares[0]
        if start < cut_at:
            qkv_out[start : min(stop, cut_at)] = total[: min(stop, cut_at) - start]
        first, last = max(start, cut_at), min(stop, sum(shares))
        if first < last:
            out_out[first - cut_at : last - cut_at] = total[first - start : last - start]

    work = Scatter(dims, pieces, (mixed,), put_sum, *buffers)
    at = work.at
    sums = SumAll(at, vec_total, vec_send, vec_got, vec_sems)
    width = tokens.shape[1]
    fetches = HEADS + HEADS // 2
    pair = 2 * LANES

    def fetch(number):
        slot = number % 2
        if number < HEADS:
            return pltpu.make_async_copy(dw.at[number], dw_buffer.at[slot, pl.ds(0, dw.shape[1])], dw_sems.at[slot])
        source = dw_out.at[pl.ds((number - HEADS) * pair, pair)]
        return pltpu.make_async_copy(source, dw_buffer.at[slot, pl.ds(0, pair)], dw_sems.at[slot])

    def place_of(device):
        place = []
        for size in reversed(spread_of(dims)):
            device, digit = divmod(device, size)
            place.insert(0, digit)
        return tuple(place)

    def put(first, share, base, value):
        done = 0
        while done < head_dim:
            device, offset = divmod(first + done, share)
            count = min(head_dim - done, share - offset)
            mixed[(*place_of(device), slice(base + offset, base + offset + count))] = value[done : done + count]
            done += count

    @pl.when(step == 0)
    def _():
        fetch(0).start()
        pltpu.make_async_copy(weight_all, weight, weight_sem).start()
        time_got[...] = jnp.zeros_like(time_got)
        at.barrier_all()
        exchange(at, time_send, time_got, time_sems)
        vec_total[...] = vec_in[...]
        for number in range(fetches):
            if number + 1 < fetches:
                fetch(number + 1).start()
            fetch(number).wait()
            if number < HEADS:
                for kind in range(3):
                    value = dw_buffer[number % 2, kind * head_dim : (kind + 1) * head_dim]
                    put((kind * HEADS + number) * head_dim, shares[0], 0, value)
            else:
                for i in range(2):
                    head = (number - HEADS) * 2 + i
                    value = dw_buffer[number % 2, i * LANES : i * LANES + head_dim]
                    put(head * head_dim, shares[1], shares[0], value)

    for place in range(len(order) - 1):
        events(order, step, work, place)

    @pl.when(step == 0)
    def _():
        pltpu.make_async_copy(weight_all, weight, weight_sem).wait()

    dn = dot_nn(dqkv[...], weight[...])
    back, unit = norm_back(tokens[...].astype(F32), vectors[0:1], dn)
    out[...] = (dh[...] + back).astype(BF16)
    vec_total[0:1, :width] += jnp.sum(dn * unit, axis=0, keepdims=True)
    vec_total[1:2, :width] += jnp.sum(dn, axis=0, keepdims=True)

    @pl.when(step == steps - 1)
    def _():
        for event in order[-1]:
            k, number = divmod(event, 10)
            if k == len(pieces):
                sums.stage(number)
            else:
                work.stage(k, number)
        exchanged(at, time_got, time_sems)
        time_got[at.index(), 0:8] = time_send[at.index()]
        vec_out[...] = vec_total[...]
        times = time_got[...].reshape(small.shape[0], LANES)
        high = times.astype(BF16)
        low = (times - high.astype(F32)).astype(BF16)
        time_out[...] = (dot_tn(high, small[...]) + dot_tn(low, small[...]))[: time_out.shape[0]]


def end(tokens, dqkv, weight, vectors, dh, small, time_send, vec_in, dw, dw_out, dims, shares, time_share, head_dim):
    rows, width = tokens.shape
    block = rows // 8
    by_rows = lambda cols: pl.BlockSpec((block, cols), lambda i: (i, 0))
    shard_rows = -(-sum(shares) // PIECE) * PIECE
    pieces = cut(0, shard_rows, BEGIN_ROWS)
    order = order_for(END_ORDER, pieces, rows // block + 1, True)
    anywhere = pl.BlockSpec(memory_space=pl.ANY)
    devices = time_send.shape[0]
    return pl.pallas_call(
        functools.partial(end_kernel, dims, pieces, order, shares, head_dim),
        grid=(rows // block,),
        in_specs=[
            by_rows(width),
            by_rows(dqkv.shape[1]),
            anywhere,
            resident(vectors.shape),
            by_rows(width),
            resident(small.shape),
            resident(time_send.shape),
            resident(vec_in.shape),
            anywhere,
            anywhere,
        ],
        out_specs=[
            by_rows(width),
            resident(vec_in.shape),
            resident((time_share, width)),
            resident((shares[0], width)),
            resident((shares[1], width)),
        ],
        out_shape=[
            jax.ShapeDtypeStruct(tokens.shape, BF16),
            jax.ShapeDtypeStruct(vec_in.shape, F32),
            jax.ShapeDtypeStruct((time_share, width), F32),
            jax.ShapeDtypeStruct((shares[0], width), F32),
            jax.ShapeDtypeStruct((shares[1], width), F32),
        ],
        scratch_shapes=[
            pltpu.VMEM(weight.shape, BF16),
            pltpu.SemaphoreType.DMA,
            pltpu.VMEM(spread_of(dims) + (shard_rows, width), BF16),
            pltpu.VMEM((2, 2 * LANES, width), BF16),
            pltpu.SemaphoreType.DMA((2,)),
            pltpu.VMEM((devices, small.shape[0] // devices, LANES), F32),
            pltpu.SemaphoreType.DMA((2,)),
            *SumAll.scratch(dims, vec_in.shape),
            *Scatter.scratch(dims, pieces, width, in_place=True),
        ],
        compiler_params=params(collective_id=4, has_side_effects=True),
        name="end",
    )(tokens, dqkv, weight, vectors, dh, small, time_send, vec_in, dw, dw_out)


def split_kernel(width, share, unit_share, heads, total, *refs):
    count = (len(refs) - 10) // 3
    sources, outs, targets = refs[:count], refs[count : count + 9], refs[count + 9 : 2 * count + 9]
    middles, sems = refs[2 * count + 9 : -1], refs[-1]
    for i in range(count):
        pltpu.make_async_copy(sources[i], middles[i], sems.at[i]).start()
    for i in range(count):
        pltpu.make_async_copy(sources[i], middles[i], sems.at[i]).wait()
        pltpu.make_async_copy(middles[i], targets[i], sems.at[i]).start()
    place = lax.axis_index("dp") * lax.axis_size("fsdp") + lax.axis_index("fsdp")
    turned = pltpu.roll(total[0:8, :width], (width - place * share) % width, 1)
    for i in range(6):
        outs[i][...] = turned[i, :share]
    per_row = width // unit_share
    row = jnp.zeros((8, width), F32)
    for i in range(4):
        row = jnp.where(place // per_row == i, total[6 + i : 7 + i, :width], row)
    row = pltpu.roll(row, (width - place % per_row * unit_share) % width, 1)
    outs[6][...] = row[0, :unit_share]
    mine = pl.ds(pl.multiple_of(lax.axis_index("fsdp") * heads, heads), heads)
    for i in range(2):
        outs[7 + i][...] = total[mine, width + i * LANES : width + i * LANES + 2 * GRID - 1]
    for i in range(count):
        pltpu.make_async_copy(middles[i], targets[i], sems.at[i]).wait()


def split(total, width, share, unit_share, heads, results):
    vmem, anywhere = pl.BlockSpec(memory_space=pltpu.VMEM), pl.BlockSpec(memory_space=pl.ANY)
    shapes = [(share,)] * 6 + [(unit_share,)] + [(heads, 2 * GRID - 1)] * 2
    return pl.pallas_call(
        functools.partial(split_kernel, width, share, unit_share, heads),
        in_specs=[vmem] + [anywhere] * len(results),
        out_specs=[vmem] * len(shapes) + [anywhere] * len(results),
        out_shape=[jax.ShapeDtypeStruct(shape, F32) for shape in shapes]
        + [jax.ShapeDtypeStruct(result.shape, result.dtype) for result in results],
        scratch_shapes=[pltpu.VMEM(result.shape, result.dtype) for result in results]
        + [pltpu.SemaphoreType.DMA((len(results),))],
        compiler_params=params(),
        name="split",
    )(total, *results)


def time_embed(stamps, feat_width):
    half_width = feat_width // 2
    frequency = jnp.exp(-math.log(10000.0) * jnp.arange(half_width, dtype=F32) / half_width)
    angles = stamps.astype(F32)[:, None] * frequency[None, :]
    return jnp.concatenate([jnp.cos(angles), jnp.sin(angles)], axis=1)


def local(
    tokens,
    image_lengths,
    timesteps,
    patch_cells,
    norm1_gain,
    norm1_bias,
    qkv_weight,
    time_weight,
    out_weight,
    out_bias,
    norm2_gain,
    norm2_bias,
    fc1_weight,
    fc1_bias,
    fc2_weight,
    fc2_bias,
    row_table,
    col_table,
    cotangent,
):
    rows, width = tokens.shape
    head_dim = width // HEADS
    slot_rows = SMALL * SMALL
    per = image_lengths.shape[0]
    assert rows == GRID * GRID and per * slot_rows == rows
    fsdp = lax.axis_size("fsdp")
    devices = lax.axis_size("dp") * fsdp
    dims = split_dp(lax.axis_size("dp"))

    qkv_share, out_share = qkv_weight.shape[1], out_weight.shape[0]
    unit_share, time_share = fc1_weight.shape[1], time_weight.shape[1]
    units = devices * unit_share
    mixed_shard = pad_rows(jnp.concatenate([qkv_weight.T, out_weight], axis=0))
    embedded = time_embed(timesteps, width).astype(BF16)
    vectors = (norm1_gain, norm1_bias, out_bias, norm2_gain, norm2_bias, fc2_bias, fc1_bias)
    table_rows, table_width = row_table.shape
    small_rows, table_at = 16, 8
    put_at = lambda part, row, lane: jnp.pad(
        part, ((row, small_rows - row - part.shape[0]), (lane, width - lane - part.shape[1]))
    )
    spots_of = [put_at(embedded, 0, 0), put_at(row_table, table_at, 2 * LANES), put_at(col_table, table_at, 3 * LANES)]
    spots_of += [put_at(vector[None], per + i, 0) for i, vector in enumerate(vectors)]
    small_shard = functools.reduce(jnp.add, spots_of)
    time_padded = jnp.pad(time_weight, ((0, 0), (0, LANES - time_share)))
    shares = (qkv_share, out_share)
    qkv_full, out_full, small, times, onehot, onehot_t, mask_q, mask_k, large_lanes = begin(
        mixed_shard, small_shard, time_padded, patch_cells, image_lengths, dims, shares, head_dim
    )
    vector_share = norm1_gain.shape[0]
    vectors = small[:, per : per + 6, :vector_share].transpose(1, 0, 2).reshape(6, width).astype(F32)
    b_up = small[:, per + 6, :unit_share].astype(F32)
    b_up = jnp.pad(b_up, ((0, 0), (0, -unit_share % PIECE)))
    b_up = b_up.reshape(devices // BLOCK_DEVICES, BLOCK_DEVICES, b_up.shape[1] // PIECE, PIECE)
    b_up = b_up.transpose(2, 0, 1, 3).reshape(-1, 1, BLOCK_DEVICES * PIECE)
    unit_shards = (pad_rows(fc1_weight.T), pad_rows(fc2_weight))
    tables = small[:fsdp, table_at : table_at + table_rows, 2 * LANES : 4 * LANES].reshape(HEADS, 2, LANES)
    tables = tables.transpose(1, 0, 2).reshape(2 * HEADS, LANES)[:, :table_width]

    grid_index = jnp.arange(GRID, dtype=jnp.int32)

    offsets = grid_index[:, None] - grid_index[None, :] + GRID - 1
    diagonal = offsets[:, :, None] == jnp.arange(2 * GRID - 1, dtype=jnp.int32)[None, None, :]
    diagonal = diagonal.reshape(GRID * GRID, 2 * GRID - 1)
    toeplitz = dot_nt(tables, diagonal.astype(BF16)).reshape(2, HEADS, GRID, GRID) * math.sqrt(head_dim)
    high = lax.reduce_precision(toeplitz, 8, 7)
    low = toeplitz - high
    zero = jnp.zeros((HEADS, GRID, GRID), F32)
    table = jnp.concatenate(
        [
            jnp.concatenate([high[0], zero, low[0], zero], axis=2),
            jnp.concatenate([zero, high[1], zero, low[1]], axis=2),
            jnp.zeros((HEADS, 2 * GRID, LANES), F32),
        ],
        axis=1,
    ).astype(BF16)

    if time_share != head_dim:
        times = times[:, :per, :time_share].transpose(1, 0, 2).reshape(per, 2 * HEADS, head_dim)
        times = jnp.pad(times.transpose(1, 0, 2), ((0, 0), (0, 8 - per), (0, LANES - head_dim)))

    scale = 1.0 / math.sqrt(head_dim)
    normed_one, q, k, v, o, p, up, down = attend(
        tokens, vectors, qkv_full, times, large_lanes, table, onehot, mask_q, mask_k,
        scale * math.log2(math.e), unit_shards, dims,
    )
    hidden, y, dn_two, db_up, d_up, d_down, first_sums = mlp(
        tokens, o, out_full, vectors, cotangent, mask_k, b_up, (up, down), unit_shards, dims
    )
    db_up = db_up.reshape(-1, devices // BLOCK_DEVICES, BLOCK_DEVICES, PIECE).transpose(1, 2, 0, 3)
    db_up = db_up.reshape(devices, -1)[:, :unit_share]

    beside = dims[1] == 1
    layer_out, dh, vec_two, dqkv, d_qkv, d_out, slot_sums, pair, *unit_sums = attend_back(
        hidden, y, dn_two, cotangent, mask_k, vectors, out_full,
        normed_one, p, q, k, v, o, onehot, onehot_t, large_lanes, scale,
        (d_up, d_down) if beside else (), first_sums, dims,
    )
    if not beside:
        unit_sums = scatter(d_up, dims, 6), scatter(d_down, dims, 7)
    up_sum, down_sum = unit_sums
    time_send = slot_sums.reshape(2 * HEADS, 8, LANES)
    if time_share != head_dim:
        time_send = time_send[:, :per, :head_dim].transpose(1, 0, 2).reshape(per, devices, time_share)
        time_send = jnp.pad(time_send.transpose(1, 0, 2), ((0, 0), (0, 8 - per), (0, LANES - time_share)))
    pairs = jnp.concatenate([pair[:, :GRID, :GRID], pair[:, GRID : 2 * GRID, GRID : 2 * GRID]])
    tables = jnp.dot(pairs.reshape(2 * HEADS, GRID * GRID), diagonal.astype(F32), precision=HIGHEST)
    vec_rows, vec_width = HEADS, width + 2 * LANES
    put_in = lambda part, row, lane: jnp.pad(
        part, ((row, vec_rows - row - part.shape[0]), (lane, vec_width - lane - part.shape[1]))
    )
    vec_in = put_in(vec_two, 2, 0) + put_in(db_up.reshape(units // width, width), 6, 0)
    vec_in = vec_in + put_in(tables[:HEADS], 0, width) + put_in(tables[HEADS:], 0, width + LANES)
    input_grad, vec_all, time_grad, qkv_sum, out_sum = end(
        tokens, dqkv, qkv_full.reshape(HEADS * 3 * LANES, width), vectors, dh,
        small.reshape(-1, width), time_send, vec_in, d_qkv, d_out, dims, shares, time_share, head_dim,
    )

    results = (layer_out, input_grad, qkv_sum, time_grad, out_sum, up_sum[:unit_share], down_sum[:unit_share])
    found = split(vec_all, width, vector_share, unit_share, HEADS // fsdp, results)
    vec_sum, (up_bias, row_sum, col_sum) = found[:6], found[6:9]
    layer_out, input_grad, qkv_sum, time_grad, out_sum, up_sum, down_sum = found[9:]

    return (
        layer_out,
        input_grad,
        vec_sum[0],
        vec_sum[1],
        qkv_sum.T,
        time_grad.T,
        out_sum,
        vec_sum[4],
        vec_sum[2],
        vec_sum[3],
        up_sum.T,
        up_bias,
        down_sum,
        vec_sum[5],
        row_sum,
        col_sum,
    )


def solution(mesh):
    rows = P(AXES, None)
    cols = P(None, AXES)
    vector = P(AXES)
    heads = P("fsdp", None)
    in_specs = (
        rows, vector, vector, vector, vector, vector, cols, cols, rows, vector, vector, vector,
        cols, vector, rows, vector, heads, heads, rows,
    )
    out_specs = (
        rows, rows, vector, vector, cols, cols, rows, vector, vector, vector, cols, vector, rows, vector,
        heads, heads,
    )
    return jax.shard_map(local, mesh=mesh, in_specs=in_specs, out_specs=out_specs, check_vma=False)
```
